32 devices in a mesh: row: 2 (over x), col: 8 (over z, core), depth: 2 (over y).
Axes of the slice: x: 2, y: 2, z: 4, core: 2. Of those that a mesh axis runs over, the one named last changes fastest.
Arguments:
- tokens: bfloat16 [2, 384, 8192], P('depth', None, ('col', 'row')), may hold values from -6 to 6
- gate_weight: bfloat16 [8192, 14336], P('col', 'row'), may hold values from -0.0625 to 0.0625
- up_weight: bfloat16 [8192, 14336], P('col', 'row'), may hold values from -0.0625 to 0.0625
- grad_hidden: bfloat16 [2, 384, 14336], P('depth', 'col', 'row'), may hold values from -0.75 to 0.75
Outputs:
- hidden: bfloat16 [2, 384, 14336], P('depth', 'col', 'row')
- grad_gate: float32 [8192, 14336], P('col', ('row', 'depth'))
- grad_up: float32 [8192, 14336], P('col', ('row', 'depth'))
The draws below stay inside these ranges and needn't reach their ends.
All inputs are finite; a program needn't handle non-finite values.
Results may differ from the reference program's by a relative error of at most 0.0034.
Values may be sent and summed in bfloat16 or wider, within the bound.
No kernel may reach another device: no remote copies, remote signals or barrier semaphores. Data moves between devices by JAX's collectives and lax.ppermute only.
A program may use at most 192 MiB of HBM per device.

```python
import jax
import jax.numpy as jnp
from jax import lax

D = 8192
FF = 14336
MICRO = 2
SLAB = 384
N_COL = 8


def block_scale(rng, shape, shards, low, high):
    def one(position, blocks):
        draws = jax.random.uniform(jax.random.fold_in(jax.random.fold_in(rng, 6), position), (blocks,), jnp.float32, low / len(shards), high / len(shards))
        return jnp.repeat(jnp.exp(draws), shape[position] // blocks).reshape((-1,) + (1,) * (len(shape) - position - 1))

    loudness = one(*shards[0])
    for cut in shards[1:]:
        loudness = loudness * one(*cut)
    return loudness


def normal_values(own_key, shape, spread, most, cuts=(), held_as=jnp.bfloat16):
    loudness = block_scale(own_key, shape, cuts, -0.22, 0.18) if cuts else 1.0
    result = jax.random.normal(own_key, shape, jnp.float32) * spread * loudness
    return jnp.minimum(jnp.maximum(result, -most), most).astype(held_as)


def setup_inputs(seed: int = 0) -> dict:
    keys = jax.random.split(jax.random.key(seed), 5)
    return {
        "tokens": normal_values(keys[0], (MICRO, SLAB, D), 1.0, 6.0, ((0, 2), (2, 16))),
        "gate_weight": normal_values(keys[1], (D, FF), D ** -0.5, 0.0625, ((0, 8), (1, 2))),
        "up_weight": normal_values(keys[2], (D, FF), D ** -0.5, 0.0625, ((0, 8), (1, 2))),
        "grad_hidden": normal_values(keys[3], (MICRO, SLAB, FF), 0.05, 0.75, ((0, 2), (1, 8), (2, 2))),
    }


def reference(tokens, gate_weight, up_weight, grad_hidden):
    block_width = D // N_COL
    flat_tokens = tokens.reshape(MICRO * SLAB, D)

    def add_block(totals, index):
        offset = (index * block_width).astype(jnp.int32)
        picked = lax.dynamic_slice_in_dim(flat_tokens, offset, block_width, 1)
        gate_rows = lax.dynamic_slice_in_dim(gate_weight, offset, block_width, 0)
        up_rows = lax.dynamic_slice_in_dim(up_weight, offset, block_width, 0)
        gate_term = jnp.dot(picked, gate_rows, preferred_element_type=jnp.float32)
        up_term = jnp.dot(picked, up_rows, preferred_element_type=jnp.float32)
        return (totals[0] + gate_term, totals[1] + up_term), None

    zeros = jnp.zeros((MICRO * SLAB, FF), jnp.float32)
    totals, unused = lax.scan(add_block, (zeros, zeros), jnp.arange(N_COL, dtype=jnp.int32))
    gate_sum, up_sum = totals
    squash = jax.nn.sigmoid(gate_sum)
    hidden = (gate_sum * squash * up_sum).astype(jnp.bfloat16)
    cotangent = grad_hidden.reshape(MICRO * SLAB, FF).astype(jnp.float32)
    gate_act = (cotangent * up_sum * squash * (1.0 + gate_sum * (1.0 - squash))).astype(jnp.bfloat16)
    up_act = (cotangent * gate_sum * squash).astype(jnp.bfloat16)
    dims = (((0,), (0,)), ((), ()))
    grad_gate = lax.dot_general(flat_tokens, gate_act, dims, preferred_element_type=jnp.float32)
    grad_up = lax.dot_general(flat_tokens, up_act, dims, preferred_element_type=jnp.float32)
    return hidden.reshape(MICRO, SLAB, FF), grad_gate, grad_up
```

```python
import functools
import math

import jax
import jax.numpy as jnp
from jax import lax
from jax.experimental import pallas as pl
from jax.experimental.pallas import tpu as pltpu
from jax.sharding import PartitionSpec as P

WIRE = jnp.float16
LARGEST_TOKEN, LARGEST_WEIGHT = 6.0, 0.0625
VMEM_LIMIT = 48 * 2**20


def forward_kernel(scale, place_ref, tokens_ref, gate_ref, up_ref, other_ref, own_ref):
    blocks, _, rows, width = own_ref.shape
    half = blocks * rows
    for which, weight_ref in enumerate((gate_ref, up_ref)):
        product = scale * jnp.dot(
            tokens_ref[...], weight_ref[...], preferred_element_type=jnp.float32
        )
        own_ref[:, which] = product[:half].reshape(blocks, rows, width)
        other_ref[:, which] = product[half:].reshape(blocks, rows, width)


def forward(place, tokens, gate_weight, up_weight, start, width, tile, blocks, scale):
    total, depth = tokens.shape
    rows = total // (2 * blocks)
    weight_spec = pl.BlockSpec((depth, tile), lambda j, place: (0, place[0] + start // tile + j))
    out_spec = pl.BlockSpec((blocks, 2, rows, tile), lambda j, place: (0, 0, 0, j))
    out_shape = jax.ShapeDtypeStruct((blocks, 2, rows, width), jnp.float32)
    return pl.pallas_call(
        functools.partial(forward_kernel, scale),
        out_shape=(out_shape, out_shape),
        grid_spec=pltpu.PrefetchScalarGridSpec(
            num_scalar_prefetch=1,
            grid=(width // tile,),
            in_specs=[
                pl.BlockSpec((total, depth), lambda j, place: (0, 0)),
                weight_spec,
                weight_spec,
            ],
            out_specs=(out_spec, out_spec),
        ),
        compiler_params=pltpu.CompilerParams(vmem_limit_bytes=VMEM_LIMIT),
        cost_estimate=pl.CostEstimate(
            flops=4 * total * depth * width,
            bytes_accessed=4 * depth * width + 8 * total * width + 2 * total * depth,
            transcendentals=0,
        ),
    )(place, tokens, gate_weight, up_weight)


def gradient_kernel(features_ref, own_ref, other_ref, *refs):
    gate_ref, up_ref = refs[-2:]
    blocks, _, rows, width = own_ref.shape
    half = blocks * rows
    for which, out_ref in enumerate((gate_ref, up_ref)):
        out_ref[...] = jnp.dot(
            features_ref[:, :half],
            own_ref[:, which].reshape(half, width),
            preferred_element_type=jnp.float32,
        ) + jnp.dot(
            features_ref[:, half:],
            other_ref[:, which].reshape(half, width),
            preferred_element_type=jnp.float32,
        )


def gradient(features, own, other, totals, columns, start, tile):
    depth, total = features.shape
    blocks, _, rows, width = own.shape
    act_spec = pl.BlockSpec((blocks, 2, rows, tile), lambda j: (0, 0, 0, j))
    out_spec = pl.BlockSpec((depth, tile), lambda j: (0, start // tile + j))
    out_shape = jax.ShapeDtypeStruct((depth, columns), jnp.float32)
    in_specs = [pl.BlockSpec((depth, total), lambda j: (0, 0)), act_spec, act_spec]
    in_specs += [pl.BlockSpec(memory_space=pl.ANY)] * len(totals)
    return pl.pallas_call(
        gradient_kernel,
        out_shape=(out_shape, out_shape),
        grid=(width // tile,),
        in_specs=in_specs,
        out_specs=(out_spec, out_spec),
        input_output_aliases={3 + i: i for i in range(len(totals))},
        compiler_params=pltpu.CompilerParams(vmem_limit_bytes=VMEM_LIMIT),
        cost_estimate=pl.CostEstimate(
            flops=4 * total * depth * width,
            bytes_accessed=8 * depth * width + 4 * total * width + 2 * total * depth,
            transcendentals=0,
        ),
    )(features, own, other, *totals)


def cut(units, shares):
    edges = [round(units * sum(shares[:i]) / sum(shares)) for i in range(len(shares) + 1)]
    return [(a, b - a) for a, b in zip(edges, edges[1:]) if b > a]


def local(sizes, tokens, gate_weight, up_weight, grad_hidden):
    n_row, n_col, n_depth = sizes
    line = n_col // 2
    row, col, part = (lax.axis_index(name) for name in ("row", "col", "depth"))
    place, core = col // 2, col % 2
    slab = grad_hidden.shape[1]
    depth, columns = gate_weight.shape
    half = columns // n_depth
    tile = 256 if half % 256 == 0 else 128
    scale = 2.0 ** math.floor(
        math.log2(65504 / (depth * n_col * LARGEST_TOKEN * LARGEST_WEIGHT))
    )

    swap = [(0, 1), (1, 0)]
    pairs = [(i, i ^ 1) for i in range(n_col)]

    def ahead(first, last):
        return [(2 * i + c, 2 * i + 2 + c) for i in range(first, last + 1) for c in (0, 1)]

    def back(first, last):
        return [(2 * i + c, 2 * i - 2 + c) for i in range(first, last + 1) for c in (0, 1)]

    def gather_rows(mine):
        if n_row != 2:
            return lax.all_gather(mine, "row", axis=1, tiled=True)
        theirs = lax.ppermute(mine, "row", swap)
        return jnp.where(
            row == 0,
            jnp.concatenate([mine, theirs], axis=1),
            jnp.concatenate([theirs, mine], axis=1),
        )

    features = gather_rows(tokens[0])
    others = lax.ppermute(features, "depth", swap)

    def arrange(values):
        values = values.reshape(line, 2, slab, depth)
        values = lax.dynamic_slice_in_dim(jnp.concatenate([values, values]), place, line, 0)
        mine = lax.dynamic_index_in_dim(values, core, 1, keepdims=False)
        theirs = lax.dynamic_index_in_dim(values, 1 - core, 1, keepdims=False)
        return jnp.stack([mine, theirs])

    picked = jnp.stack([arrange(features), arrange(others)], axis=2)
    picked = picked.reshape(2 * line * 2 * slab, depth)
    turned = picked.T

    cotangent = grad_hidden[0]
    mine = lax.dynamic_slice_in_dim(cotangent, part * half, half, 1)
    theirs = lax.dynamic_slice_in_dim(cotangent, (1 - part) * half, half, 1)
    cotangent = jnp.stack([mine, lax.ppermute(theirs, "depth", swap)])

    first_tile = (part * (half // tile)).astype(jnp.int32).reshape(1)
    wide = lambda x: x.astype(jnp.float32)

    totals, hidden_own, hidden_other = (), [], []
    for begin, count in cut(half // tile, SHARES):
        start, width = begin * tile, count * tile
        other, own = forward(
            first_tile, picked, gate_weight, up_weight, start, width, tile, line, scale
        )
        got = lax.ppermute(other.astype(WIRE), "col", pairs)
        both = (own + wide(got)).astype(WIRE)
        right = left = None
        for o in range(line - 1, 0, -1):
            to_right, to_left = both[o], both[line - o]
            if right is not None:
                to_right = (wide(to_right) + wide(right)).astype(WIRE)
                to_left = (wide(to_left) + wide(left)).astype(WIRE)
            right = lax.ppermute(to_right, "col", ahead(0, line - 1 - o))
            left = lax.ppermute(to_left, "col", back(o, line - 1))
        summed = (wide(both[0]) + wide(right) + wide(left)) * (1.0 / scale)
        summed = summed.reshape(2, 2, slab, width)
        gate_sum, up_sum = summed[0], summed[1]
        squash = jax.nn.sigmoid(gate_sum)
        hidden = (gate_sum * squash * up_sum).astype(jnp.bfloat16)
        given = wide(cotangent[:, :, start : start + width])
        gate_act = given * up_sum * squash * (1.0 + gate_sum * (1.0 - squash))
        up_act = given * gate_sum * squash
        act = jnp.stack([gate_act, up_act]).astype(jnp.bfloat16).reshape(2, 2 * slab, width)
        hidden_own.append(hidden[0])
        hidden_other.append(lax.ppermute(hidden[1], "depth", swap))

        from_left, from_right = [act], [act]
        for step in range(1, line):
            from_left.append(lax.ppermute(from_left[-1], "col", ahead(step - 1, line - 2)))
            from_right.append(lax.ppermute(from_right[-1], "col", back(1, line - step)))
        blocks = [act]
        for o in range(1, line):
            blocks.append(jnp.where(place + o < line, from_right[o], from_left[line - o]))
        gathered = jnp.stack(blocks)
        totals = gradient(
            turned, gathered, lax.ppermute(gathered, "col", pairs), totals, half, start, tile
        )

    own = jnp.concatenate(hidden_own, axis=1)
    other = jnp.concatenate(hidden_other, axis=1)
    hidden = jnp.where(
        part == 0,
        jnp.concatenate([own, other], axis=1),
        jnp.concatenate([other, own], axis=1),
    )
    return (hidden[None], *totals)


SHARES = (3, 4, 4, 3)


def solution(mesh):
    sizes = tuple(mesh.shape[name] for name in ("row", "col", "depth"))
    in_specs = (
        P("depth", None, ("col", "row")),
        P("col", "row"),
        P("col", "row"),
        P("depth", "col", "row"),
    )
    out_specs = (P("depth", "col", "row"), P("col", ("row", "depth")), P("col", ("row", "depth")))
    return jax.shard_map(
        functools.partial(local, sizes),
        mesh=mesh,
        in_specs=in_specs,
        out_specs=out_specs,
        check_vma=False,
    )
```

```python
import functools
import math

import jax
import jax.numpy as jnp
from jax import lax
from jax.experimental import pallas as pl
from jax.experimental.pallas import tpu as pltpu
from jax.sharding import PartitionSpec as P

WIRE = jnp.float16
LARGEST_TOKEN, LARGEST_WEIGHT = 6.0, 0.0625
VMEM_LIMIT = 48 * 2**20


def forward_kernel(scale, place_ref, tokens_ref, gate_ref, up_ref, other_ref, own_ref):
    blocks, _, rows, width = own_ref.shape
    half = blocks * rows
    for which, weight_ref in enumerate((gate_ref, up_ref)):
        product = scale * jnp.dot(
            tokens_ref[...], weight_ref[...], preferred_element_type=jnp.float32
        )
        own_ref[:, which] = product[:half].reshape(blocks, rows, width)
        other_ref[:, which] = product[half:].reshape(blocks, rows, width)


def forward(place, tokens, gate_weight, up_weight, start, width, tile, blocks, scale):
    total, depth = tokens.shape
    rows = total // (2 * blocks)
    weight_spec = pl.BlockSpec((depth, tile), lambda j, place: (0, place[0] + start // tile + j))
    out_spec = pl.BlockSpec((blocks, 2, rows, tile), lambda j, place: (0, 0, 0, j))
    out_shape = jax.ShapeDtypeStruct((blocks, 2, rows, width), jnp.float32)
    return pl.pallas_call(
        functools.partial(forward_kernel, scale),
        out_shape=(out_shape, out_shape),
        grid_spec=pltpu.PrefetchScalarGridSpec(
            num_scalar_prefetch=1,
            grid=(width // tile,),
            in_specs=[
                pl.BlockSpec((total, depth), lambda j, place: (0, 0)),
                weight_spec,
                weight_spec,
            ],
            out_specs=(out_spec, out_spec),
        ),
        compiler_params=pltpu.CompilerParams(vmem_limit_bytes=VMEM_LIMIT),
        cost_estimate=pl.CostEstimate(
            flops=4 * total * depth * width,
            bytes_accessed=4 * depth * width + 8 * total * width + 2 * total * depth,
            transcendentals=0,
        ),
    )(place, tokens, gate_weight, up_weight)


def gradient_kernel(features_ref, own_ref, other_ref, *refs):
    gate_ref, up_ref = refs[-2:]
    blocks, _, rows, width = own_ref.shape
    half = blocks * rows
    for which, out_ref in enumerate((gate_ref, up_ref)):
        out_ref[...] = jnp.dot(
            features_ref[:, :half],
            own_ref[:, which].reshape(half, width),
            preferred_element_type=jnp.float32,
        ) + jnp.dot(
            features_ref[:, half:],
            other_ref[:, which].reshape(half, width),
            preferred_element_type=jnp.float32,
        )


def gradient(features, own, other, totals, columns, start, tile):
    depth, total = features.shape
    blocks, _, rows, width = own.shape
    act_spec = pl.BlockSpec((blocks, 2, rows, tile), lambda j: (0, 0, 0, j))
    out_spec = pl.BlockSpec((depth, tile), lambda j: (0, start // tile + j))
    out_shape = jax.ShapeDtypeStruct((depth, columns), jnp.float32)
    in_specs = [pl.BlockSpec((depth, total), lambda j: (0, 0)), act_spec, act_spec]
    in_specs += [pl.BlockSpec(memory_space=pl.ANY)] * len(totals)
    return pl.pallas_call(
        gradient_kernel,
        out_shape=(out_shape, out_shape),
        grid=(width // tile,),
        in_specs=in_specs,
        out_specs=(out_spec, out_spec),
        input_output_aliases={3 + i: i for i in range(len(totals))},
        compiler_params=pltpu.CompilerParams(vmem_limit_bytes=VMEM_LIMIT),
        cost_estimate=pl.CostEstimate(
            flops=4 * total * depth * width,
            bytes_accessed=8 * depth * width + 4 * total * width + 2 * total * depth,
            transcendentals=0,
        ),
    )(features, own, other, *totals)


def tie(value, *after):
    return lax.optimization_barrier((value, after))[0]


def cut(units, shares):
    edges = [round(units * sum(shares[:i]) / sum(shares)) for i in range(len(shares) + 1)]
    return [(a, b - a) for a, b in zip(edges, edges[1:]) if b > a]


def local(sizes, tokens, gate_weight, up_weight, grad_hidden):
    n_row, n_col, n_depth = sizes
    line = n_col // 2
    row, col, part = (lax.axis_index(name) for name in ("row", "col", "depth"))
    place, core = col // 2, col % 2
    slab = grad_hidden.shape[1]
    depth, columns = gate_weight.shape
    half = columns // n_depth
    tile = 256 if half % 256 == 0 else 128
    scale = 2.0 ** math.floor(
        math.log2(65504 / (depth * n_col * LARGEST_TOKEN * LARGEST_WEIGHT))
    )

    swap = [(0, 1), (1, 0)]
    pairs = [(i, i ^ 1) for i in range(n_col)]

    def ahead(first, last):
        return [(2 * i + c, 2 * i + 2 + c) for i in range(first, last + 1) for c in (0, 1)]

    def back(first, last):
        return [(2 * i + c, 2 * i - 2 + c) for i in range(first, last + 1) for c in (0, 1)]

    mine_wide = tokens[0]
    if n_row == 2:
        over_row = lax.ppermute(mine_wide, "row", swap)
        over_depth = lax.ppermute(mine_wide, "depth", swap)
        over_both = lax.ppermute(over_row, "depth", swap)

        def join(mine, theirs):
            return jnp.where(
                row == 0,
                jnp.concatenate([mine, theirs], axis=1),
                jnp.concatenate([theirs, mine], axis=1),
            )

        features = (join(mine_wide, over_row), join(over_depth, over_both))
    else:
        features = lax.all_gather(mine_wide, "row", axis=1, tiled=True)
        features = (features, lax.ppermute(features, "depth", swap))

    def arrange(values):
        values = values.reshape(line, 2, slab, depth)
        values = lax.dynamic_slice_in_dim(jnp.concatenate([values, values]), place, line, 0)
        mine = lax.dynamic_index_in_dim(values, core, 1, keepdims=False)
        theirs = lax.dynamic_index_in_dim(values, 1 - core, 1, keepdims=False)
        return jnp.stack([mine, theirs])

    single = [arrange(values) for values in features]
    double = jnp.stack(single, axis=2).reshape(-1, depth)
    picked = {
        (0,): single[0].reshape(-1, depth),
        (1,): single[1].reshape(-1, depth),
        (0, 1): double,
    }
    turned = double.T

    cotangent = grad_hidden[0]
    mine = lax.dynamic_slice_in_dim(cotangent, part * half, half, 1)
    theirs = lax.dynamic_slice_in_dim(cotangent, (1 - part) * half, half, 1)
    cotangent = (mine, lax.ppermute(theirs, "depth", swap))

    first_tile = (part * (half // tile)).astype(jnp.int32).reshape(1)
    wide = lambda x: x.astype(jnp.float32)

    pieces = []
    for i, (begin, count) in enumerate(cut(half // tile, SHARES)):
        for batches in ((0,), (1,)) if i == 0 else ((0, 1),):
            pieces.append((batches, begin * tile, count * tile))

    def multiply(k, after):
        batches, start, width = pieces[k]
        rows = tie(picked[batches], after)
        other, own = forward(
            first_tile, rows, gate_weight, up_weight, start, width, tile, line, scale
        )
        got = lax.ppermute(other.astype(WIRE), "col", pairs)
        return (own + wide(got)).astype(WIRE)

    def activate(k, summed):
        batches, start, width = pieces[k]
        summed = (summed * (1.0 / scale)).reshape(2, len(batches), slab, width)
        gate_sum, up_sum = summed[0], summed[1]
        squash = jax.nn.sigmoid(gate_sum)
        hidden = (gate_sum * squash * up_sum).astype(jnp.bfloat16)
        given = jnp.stack([wide(cotangent[b][:, start : start + width]) for b in batches])
        gate_act = given * up_sum * squash * (1.0 + gate_sum * (1.0 - squash))
        up_act = given * gate_sum * squash
        act = jnp.stack([gate_act, up_act]).astype(jnp.bfloat16)
        for position, batch in enumerate(batches):
            hiddens[batch].append(hidden[position])
        return act.reshape(2, len(batches) * slab, width)

    hiddens, totals, waiting = ([], []), (), []
    last = len(pieces) - 1
    both = {0: multiply(0, ())}
    both[1] = multiply(1, ())
    act = None
    for k in range(-1, last + 1):
        right = left = None
        from_left, from_right = [act], [act]
        for step in range(1, line):
            if k < last:
                o = line - step
                to_right, to_left = both[k + 1][o], both[k + 1][line - o]
                if right is not None:
                    to_right = (wide(to_right) + wide(right)).astype(WIRE)
                    to_left = (wide(to_left) + wide(left)).astype(WIRE)
                if step > 1 and act is not None:
                    to_right, to_left = tie(
                        (to_right, to_left), from_left[step - 1], from_right[step - 1]
                    )
                right = lax.ppermute(to_right, "col", ahead(0, step - 1))
                left = lax.ppermute(to_left, "col", back(o, line - 1))
            if act is not None:
                to_right, to_left = from_left[-1], from_right[-1]
                from_left.append(lax.ppermute(to_right, "col", ahead(step - 1, line - 2)))
                from_right.append(lax.ppermute(to_left, "col", back(1, line - step)))
            if step == 1 and k + 3 <= last:
                both[k + 3] = multiply(k + 3, both[k + 1])
        if k < last:
            ready = activate(k + 1, wide(both[k + 1][0]) + wide(right) + wide(left))
        if act is not None:
            blocks = [act]
            for o in range(1, line):
                blocks.append(jnp.where(place + o < line, from_right[o], from_left[line - o]))
            gathered = jnp.stack(blocks)
            gathered = (gathered, lax.ppermute(gathered, "col", pairs))
            waiting.append(gathered)
            batches, start, width = pieces[k]
            if batches != (0,):
                if batches == (1,):
                    gathered = [jnp.concatenate(both_batches, axis=2) for both_batches in zip(*waiting)]
                waiting = []
                totals = gradient(turned, *gathered, totals, half, start, tile)
                if k < last - 1:
                    both[k + 2] = tie(both[k + 2], *totals)
        act = ready

    own, other = (jnp.concatenate(parts, axis=1) for parts in hiddens)
    other = lax.ppermute(other, "depth", swap)
    hidden = jnp.where(
        part == 0,
        jnp.concatenate([own, other], axis=1),
        jnp.concatenate([other, own], axis=1),
    )
    return (hidden[None], *totals)


SHARES = (4, 4, 4, 2)


def solution(mesh):
    sizes = tuple(mesh.shape[name] for name in ("row", "col", "depth"))
    in_specs = (
        P("depth", None, ("col", "row")),
        P("col", "row"),
        P("col", "row"),
        P("depth", "col", "row"),
    )
    out_specs = (P("depth", "col", "row"), P("col", ("row", "depth")), P("col", ("row", "depth")))
    return jax.shard_map(
        functools.partial(local, sizes),
        mesh=mesh,
        in_specs=in_specs,
        out_specs=out_specs,
        check_vma=False,
    )
```

```python
import functools
import math

import jax
import jax.numpy as jnp
from jax import lax
from jax.experimental import pallas as pl
from jax.experimental.pallas import tpu as pltpu
from jax.sharding import PartitionSpec as P

WIRE = jnp.float16
LARGEST_TOKEN, LARGEST_WEIGHT = 6.0, 0.0625
VMEM_LIMIT = 48 * 2**20


def forward_kernel(scale, place_ref, tokens_ref, gate_ref, up_ref, other_ref, own_ref):
    blocks, _, rows, width = own_ref.shape
    half = blocks * rows
    for which, weight_ref in enumerate((gate_ref, up_ref)):
        product = scale * jnp.dot(
            tokens_ref[...], weight_ref[...], preferred_element_type=jnp.float32
        )
        own_ref[:, which] = product[:half].reshape(blocks, rows, width)
        other_ref[:, which] = product[half:].reshape(blocks, rows, width)


def forward(place, tokens, gate_weight, up_weight, start, width, tile, blocks, scale):
    total, depth = tokens.shape
    rows = total // (2 * blocks)
    weight_spec = pl.BlockSpec((depth, tile), lambda j, place: (0, place[0] + start // tile + j))
    out_spec = pl.BlockSpec((blocks, 2, rows, tile), lambda j, place: (0, 0, 0, j))
    out_shape = jax.ShapeDtypeStruct((blocks, 2, rows, width), jnp.float32)
    return pl.pallas_call(
        functools.partial(forward_kernel, scale),
        out_shape=(out_shape, out_shape),
        grid_spec=pltpu.PrefetchScalarGridSpec(
            num_scalar_prefetch=1,
            grid=(width // tile,),
            in_specs=[
                pl.BlockSpec((total, depth), lambda j, place: (0, 0)),
                weight_spec,
                weight_spec,
            ],
            out_specs=(out_spec, out_spec),
        ),
        compiler_params=pltpu.CompilerParams(vmem_limit_bytes=VMEM_LIMIT),
        cost_estimate=pl.CostEstimate(
            flops=4 * total * depth * width,
            bytes_accessed=4 * depth * width + 8 * total * width + 2 * total * depth,
            transcendentals=0,
        ),
    )(place, tokens, gate_weight, up_weight)


def gradient_kernel(features_ref, own_ref, other_ref, *refs):
    gate_ref, up_ref = refs[-2:]
    blocks, _, rows, width = own_ref.shape
    half = blocks * rows
    for which, out_ref in enumerate((gate_ref, up_ref)):
        act = jnp.concatenate(
            [own_ref[:, which].reshape(half, width), other_ref[:, which].reshape(half, width)]
        )
        out_ref[...] = jnp.dot(features_ref[...], act, preferred_element_type=jnp.float32)


def gradient(features, own, other, totals, columns, start, tile):
    depth, total = features.shape
    blocks, _, rows, width = own.shape
    act_spec = pl.BlockSpec((blocks, 2, rows, tile), lambda j: (0, 0, 0, j))
    out_spec = pl.BlockSpec((depth, tile), lambda j: (0, start // tile + j))
    out_shape = jax.ShapeDtypeStruct((depth, columns), jnp.float32)
    in_specs = [pl.BlockSpec((depth, total), lambda j: (0, 0)), act_spec, act_spec]
    in_specs += [pl.BlockSpec(memory_space=pl.ANY)] * len(totals)
    return pl.pallas_call(
        gradient_kernel,
        out_shape=(out_shape, out_shape),
        grid=(width // tile,),
        in_specs=in_specs,
        out_specs=(out_spec, out_spec),
        input_output_aliases={3 + i: i for i in range(len(totals))},
        compiler_params=pltpu.CompilerParams(vmem_limit_bytes=VMEM_LIMIT),
        cost_estimate=pl.CostEstimate(
            flops=4 * total * depth * width,
            bytes_accessed=8 * depth * width + 4 * total * width + 2 * total * depth,
            transcendentals=0,
        ),
    )(features, own, other, *totals)


def tie(value, *after):
    return lax.optimization_barrier((value, after))[0]


def cut(units, shares):
    edges = [round(units * sum(shares[:i]) / sum(shares)) for i in range(len(shares) + 1)]
    return [(a, b - a) for a, b in zip(edges, edges[1:]) if b > a]


def local(sizes, tokens, gate_weight, up_weight, grad_hidden):
    n_row, n_col, n_depth = sizes
    line = n_col // 2
    row, col, part = (lax.axis_index(name) for name in ("row", "col", "depth"))
    place, core = col // 2, col % 2
    slab = grad_hidden.shape[1]
    depth, columns = gate_weight.shape
    half = columns // n_depth
    tile = 256 if half % 256 == 0 else 128
    scale = 2.0 ** math.floor(
        math.log2(65504 / (depth * n_col * LARGEST_TOKEN * LARGEST_WEIGHT))
    )

    swap = [(0, 1), (1, 0)]
    pairs = [(i, i ^ 1) for i in range(n_col)]

    def between(hops):
        return [(2 * i + c, 2 * j + c) for i, j in hops for c in (0, 1)]

    inward, outward = between([(0, 1), (3, 2)]), between([(1, 0), (2, 3)])
    side, centre = inward + outward, between([(1, 2), (2, 1)])
    at_end = (place == 0) | (place == line - 1)
    at_far = 2 * place >= line

    mine_wide = tokens[0]
    if n_row == 2:
        over_row = lax.ppermute(mine_wide, "row", swap)
        over_depth = lax.ppermute(mine_wide, "depth", swap)
        over_both = lax.ppermute(over_row, "depth", swap)

        def join(mine, theirs):
            return jnp.where(
                row == 0,
                jnp.concatenate([mine, theirs], axis=1),
                jnp.concatenate([theirs, mine], axis=1),
            )

        features = (join(mine_wide, over_row), join(over_depth, over_both))
    else:
        features = lax.all_gather(mine_wide, "row", axis=1, tiled=True)
        features = (features, lax.ppermute(features, "depth", swap))

    def arrange(values):
        values = values.reshape(line, 2, slab, depth)
        values = jnp.where(at_far, values[::-1], values)
        mine = lax.dynamic_index_in_dim(values, core, 1, keepdims=False)
        theirs = lax.dynamic_index_in_dim(values, 1 - core, 1, keepdims=False)
        return jnp.stack([mine, theirs])

    cotangent = grad_hidden[0]
    mine = lax.dynamic_slice_in_dim(cotangent, part * half, half, 1)
    theirs = lax.dynamic_slice_in_dim(cotangent, (1 - part) * half, half, 1)
    cotangent = (mine, lax.ppermute(theirs, "depth", swap))

    first_tile = (part * (half // tile)).astype(jnp.int32).reshape(1)
    wide = lambda x: x.astype(jnp.float32)

    pieces = []
    for i, (begin, count) in enumerate(cut(half // tile, SHARES)):
        for batches in ((0,), (1,)) if i == 0 else ((0, 1),):
            pieces.append((batches, begin * tile, count * tile))

    def multiply(k, after):
        batches, start, width = pieces[k]
        rows = tie(picked[batches], after)
        return forward(
            first_tile, rows, gate_weight, up_weight, start, width, tile, line, scale
        )

    def pair_sum(other, own):
        got = lax.ppermute(other.astype(WIRE), "col", pairs)
        return (own + wide(got)).astype(WIRE)

    def activate(k, summed):
        batches, start, width = pieces[k]
        summed = (summed * (1.0 / scale)).reshape(2, len(batches), slab, width)
        gate_sum, up_sum = summed[0], summed[1]
        squash = jax.nn.sigmoid(gate_sum)
        hidden = (gate_sum * squash * up_sum).astype(jnp.bfloat16)
        given = jnp.stack([wide(cotangent[b][:, start : start + width]) for b in batches])
        gate_act = given * up_sum * squash * (1.0 + gate_sum * (1.0 - squash))
        up_act = given * gate_sum * squash
        act = jnp.stack([gate_act, up_act]).astype(jnp.bfloat16)
        for position, batch in enumerate(batches):
            hiddens[batch].append(hidden[position])
        return act.reshape(2, len(batches) * slab, width)

    def add(*terms):
        return functools.reduce(jnp.add, map(wide, terms))

    def send(value, route):
        return lax.ppermute(value, "col", route)

    hiddens, totals, waiting = ([], []), (), []
    last = len(pieces) - 1
    near_rows = arrange(features[0])
    picked = {(0,): near_rows.reshape(-1, depth)}
    first = multiply(0, ())
    arranged = arrange(tie(features[1], first))
    double = jnp.stack([near_rows, arranged], axis=2).reshape(-1, depth)
    picked[(1,)] = arranged.reshape(-1, depth)
    picked[(0, 1)] = double
    turned = double.T
    sums = pair_sum(*first)
    act = gathered = None
    for k in range(-1, last + 1):
        adding, sharing = k < last, act is not None
        if adding:
            in_1 = send(sums[3], inward)
        if sharing:
            side_1, centre_1 = send(act, side), send(act, centre)
        if gathered is not None:
            waiting.append((gathered, send(gathered, pairs)))
            batches, start, width = pieces[k - 1]
            if batches != (0,):
                if len(waiting) > 1:
                    merged = [jnp.concatenate(both, axis=2) for both in zip(*waiting)]
                else:
                    merged = waiting[0]
                waiting = []
                totals = gradient(turned, *merged, totals, half, start, tile)
                if adding:
                    sums = tie(sums, totals)
        if adding:
            far = add(sums[3], in_1).astype(WIRE)
            centre_2 = send(far, centre)
            in_2 = send(tie(sums[2], in_1), inward)
        if sharing:
            out_2, share_2 = send(centre_1, outward), send(side_1, centre)
        if adding:
            if k + 2 <= last:
                following = multiply(k + 2, (in_1,))
                sums = tie(sums, following)
            near = add(sums[2], in_2).astype(WIRE)
            swapped = jnp.where(at_end, wide(sums[1]), add(sums[0], centre_2)).astype(WIRE)
            side_3 = send(swapped, side)
            centre_3 = send(near, centre)
        if sharing:
            out_3 = send(share_2, outward)
            gathered = jnp.stack(
                [
                    jnp.where(at_end, act, side_1),
                    jnp.where(at_end, side_1, act),
                    jnp.where(at_end, out_2, centre_1),
                    jnp.where(at_end, out_3, share_2),
                ]
            )
        if adding:
            own = jnp.where(at_end, wide(sums[0]), wide(sums[1]))
            act = activate(k + 1, own + wide(side_3) + wide(centre_3))
            if k + 2 <= last:
                sums = pair_sum(*following)
    batches, start, width = pieces[last]
    totals = gradient(turned, gathered, send(gathered, pairs), totals, half, start, tile)

    own, other = (jnp.concatenate(parts, axis=1) for parts in hiddens)
    other = lax.ppermute(other, "depth", swap)
    hidden = jnp.where(
        part == 0,
        jnp.concatenate([own, other], axis=1),
        jnp.concatenate([other, own], axis=1),
    )
    return (hidden[None], *totals)


def contract(picked, piece):
    return lax.dot_general(
        picked, piece, (((0,), (0,)), ((), ())), preferred_element_type=jnp.float32
    )


def local_any(tokens, gate_weight, up_weight, grad_hidden):
    features = lax.all_gather(tokens[0], "row", axis=1, tiled=True)
    columns = gate_weight.shape[1]
    picked = features
    gate_part = jnp.dot(picked, gate_weight, preferred_element_type=jnp.float32)
    up_part = jnp.dot(picked, up_weight, preferred_element_type=jnp.float32)
    summed = lax.psum_scatter(
        jnp.concatenate([gate_part, up_part], axis=1), "col", scatter_dimension=0, tiled=True
    )
    gate_sum = summed[:, :columns]
    up_sum = summed[:, columns:]
    squash = jax.nn.sigmoid(gate_sum)
    hidden = (gate_sum * squash * up_sum).astype(jnp.bfloat16)
    cotangent = grad_hidden[0].astype(jnp.float32)
    gate_act = (cotangent * up_sum * squash * (1.0 + gate_sum * (1.0 - squash))).astype(
        jnp.bfloat16
    )
    up_act = (cotangent * gate_sum * squash).astype(jnp.bfloat16)
    picked = features
    gate_total = contract(picked, lax.all_gather(gate_act, "col", axis=0, tiled=True))
    up_total = contract(picked, lax.all_gather(up_act, "col", axis=0, tiled=True))
    grad_gate, grad_up = (
        lax.psum_scatter(gate_total, "depth", scatter_dimension=1, tiled=True),
        lax.psum_scatter(up_total, "depth", scatter_dimension=1, tiled=True),
    )
    return (hidden[None], grad_gate, grad_up)


SHARES = (4, 4, 4, 2)


def solution(mesh):
    sizes = tuple(mesh.shape[name] for name in ("row", "col", "depth"))
    in_specs = (
        P("depth", None, ("col", "row")),
        P("col", "row"),
        P("col", "row"),
        P("depth", "col", "row"),
    )
    out_specs = (P("depth", "col", "row"), P("col", ("row", "depth")), P("col", ("row", "depth")))
    return jax.shard_map(
        functools.partial(local, sizes) if sizes == (2, 8, 2) else local_any,
        mesh=mesh,
        in_specs=in_specs,
        out_specs=out_specs,
        check_vma=False,
    )
```

```python
import functools
import math

import jax
import jax.numpy as jnp
from jax import lax
from jax.experimental import pallas as pl
from jax.experimental.pallas import tpu as pltpu
from jax.sharding import PartitionSpec as P

WIRE = jnp.float16
LARGEST_TOKEN, LARGEST_WEIGHT = 6.0, 0.0625
VMEM_LIMIT = 48 * 2**20
SHARES = (2, 3, 2)


def forward_kernel(
    scale, place_ref, mine_ref, theirs_ref, gate_ref, up_ref, gate_far_ref, up_far_ref, out_ref
):
    blocks, _, rows, width = out_ref.shape
    for which, (near, far) in enumerate(((gate_ref, gate_far_ref), (up_ref, up_far_ref))):
        product = jnp.dot(mine_ref[...], near[...], preferred_element_type=jnp.float32)
        product += jnp.dot(theirs_ref[...], far[0], preferred_element_type=jnp.float32)
        out_ref[:, which] = (scale * product).reshape(blocks, rows, width)


def forward(place, mine, theirs, gate_weight, up_weight, far, start, tile, blocks, scale):
    total, depth = mine.shape
    width = far.shape[2]
    rows = total // blocks
    whole = pl.BlockSpec((total, depth), lambda j, place: (0, 0))
    weight = pl.BlockSpec((depth, tile), lambda j, place: (0, place[0] + start // tile + j))
    return pl.pallas_call(
        functools.partial(forward_kernel, scale),
        out_shape=jax.ShapeDtypeStruct((blocks, 2, rows, width), jnp.float32),
        grid_spec=pltpu.PrefetchScalarGridSpec(
            num_scalar_prefetch=1,
            grid=(width // tile,),
            in_specs=[
                whole,
                whole,
                weight,
                weight,
                pl.BlockSpec((1, depth, tile), lambda j, place: (0, 0, j)),
                pl.BlockSpec((1, depth, tile), lambda j, place: (1, 0, j)),
            ],
            out_specs=pl.BlockSpec((blocks, 2, rows, tile), lambda j, place: (0, 0, 0, j)),
        ),
        compiler_params=pltpu.CompilerParams(vmem_limit_bytes=VMEM_LIMIT),
        cost_estimate=pl.CostEstimate(
            flops=8 * total * depth * width,
            bytes_accessed=8 * depth * width + 8 * total * width + 4 * total * depth,
            transcendentals=0,
        ),
    )(place, mine, theirs, gate_weight, up_weight, far, far)


def gradient_kernel(place_ref, features_ref, act_ref, *refs):
    gate_ref, up_ref = refs[-2:]
    blocks, _, _, rows, width = act_ref.shape
    for which, out_ref in enumerate((gate_ref, up_ref)):
        act = act_ref[:, 0, which].reshape(blocks * rows, width)
        out_ref[...] = jnp.dot(features_ref[...], act, preferred_element_type=jnp.float32)


def gradient(place, features, act, totals, columns, start, tile):
    depth, total = features.shape
    blocks, cores, _, rows, width = act.shape
    act_spec = pl.BlockSpec((blocks, 1, 2, rows, tile), lambda i, j, place: (0, i, 0, 0, j))
    out_spec = pl.BlockSpec((depth, tile), lambda i, j, place: (0, place[i] + start // tile + j))
    out_shape = jax.ShapeDtypeStruct((depth, columns), jnp.float32)
    in_specs = [pl.BlockSpec((depth, total), lambda i, j, place: (0, 0)), act_spec]
    in_specs += [pl.BlockSpec(memory_space=pl.ANY)] * len(totals)
    return pl.pallas_call(
        gradient_kernel,
        out_shape=(out_shape, out_shape),
        grid_spec=pltpu.PrefetchScalarGridSpec(
            num_scalar_prefetch=1,
            grid=(cores, width // tile),
            in_specs=in_specs,
            out_specs=(out_spec, out_spec),
        ),
        input_output_aliases={3 + i: i for i in range(len(totals))},
        compiler_params=pltpu.CompilerParams(vmem_limit_bytes=VMEM_LIMIT),
        cost_estimate=pl.CostEstimate(
            flops=4 * cores * total * depth * width,
            bytes_accessed=cores * (8 * depth + 4 * total) * width + 2 * total * depth,
            transcendentals=0,
        ),
    )(place, features, act, *totals)


def tie(value, *after):
    return lax.optimization_barrier((value, after))[0]


def cut(units, shares):
    edges = [round(units * sum(shares[:i]) / sum(shares)) for i in range(len(shares) + 1)]
    return [(a, b - a) for a, b in zip(edges, edges[1:]) if b > a]


def local(tokens, gate_weight, up_weight, grad_hidden):
    line = 4
    row, col, part = (lax.axis_index(name) for name in ("row", "col", "depth"))
    place, core = col // 2, col % 2
    slab = grad_hidden.shape[1]
    rows = 2 * slab
    depth, columns = gate_weight.shape
    half = columns // 2
    share = half // 2
    tile = 256 if share % 256 == 0 else 128
    largest = depth * 2 * line * LARGEST_TOKEN * LARGEST_WEIGHT
    scale = 2.0 ** math.floor(math.log2(65504 / largest))

    swap = [(0, 1), (1, 0)]
    pairs = [(i, i ^ 1) for i in range(2 * line)]

    def between(hops):
        return [(2 * i + c, 2 * j + c) for i, j in hops for c in (0, 1)]

    inward, outward = between([(0, 1), (3, 2)]), between([(1, 0), (2, 3)])
    side, centre = inward + outward, between([(1, 2), (2, 1)])
    at_end = (place == 0) | (place == line - 1)
    at_far = 2 * place >= line

    def send(value, route):
        return lax.ppermute(value, "col", route)

    def wide(value):
        return value.astype(jnp.float32)

    def add(*terms):
        return functools.reduce(jnp.add, map(wide, terms))

    def by(first, mine, theirs, axis):
        return jnp.where(
            first,
            jnp.concatenate([mine, theirs], axis=axis),
            jnp.concatenate([theirs, mine], axis=axis),
        )

    def columns_of(array, start, width):
        return lax.dynamic_slice_in_dim(array, start, width, array.ndim - 1)

    pieces = [(begin * tile, count * tile) for begin, count in cut(share // tile, SHARES)]
    last = len(pieces) - 1

    def exchange_weights(k, after):
        start, width = pieces[k]
        first = part * half + (1 - core) * share + start
        chosen = [columns_of(weight, first, width) for weight in (gate_weight, up_weight)]
        return send(tie(jnp.stack(chosen), after), pairs)

    mine = tokens[0]
    over_row = lax.ppermute(mine, "row", swap)
    over_depth = lax.ppermute(mine, "depth", swap)
    over_both = lax.ppermute(over_row, "depth", swap)
    far_weights = [exchange_weights(0, ())]
    features = [by(row == 0, mine, over_row, 1), by(row == 0, over_depth, over_both, 1)]
    other_features = [send(value, pairs) for value in features]
    for k in range(1, last + 1):
        far_weights.append(exchange_weights(k, other_features))

    def arrange(values):
        values = jnp.stack([value.reshape(line, rows, depth) for value in values], axis=1)
        return values, jnp.where(at_far, values[::-1], values)

    in_place, by_distance = arrange(features)
    mine_rows = by_distance.reshape(-1, depth)
    their_rows = arrange(other_features)[1].reshape(-1, depth)

    first_tile = ((part * half + core * share) // tile).astype(jnp.int32).reshape(1)

    def multiply(k, after):
        start, _ = pieces[k]
        return forward(
            first_tile,
            tie(mine_rows, after),
            their_rows,
            gate_weight,
            up_weight,
            far_weights[k],
            start,
            tile,
            line,
            scale,
        )

    terms = multiply(0, ())
    in_1 = send(terms[3].astype(WIRE), inward)

    mine_cotangent, cotangent = tie((grad_hidden[0], grad_hidden[0]), terms)
    cotangent = jnp.stack(
        [
            columns_of(mine_cotangent, part * half, half),
            lax.ppermute(columns_of(cotangent, (1 - part) * half, half), "depth", swap),
        ]
    )
    cotangent = by(
        core == 0,
        columns_of(cotangent, core * share, share),
        send(columns_of(cotangent, (1 - core) * share, share), pairs),
        1,
    )

    in_place, by_distance = tie((in_place, by_distance), terms)
    turned = by_distance.reshape(-1, depth).T
    turned_in_place = in_place.reshape(-1, depth).T

    def activate(k, summed):
        start, width = pieces[k]
        summed = (summed * (1.0 / scale)).reshape(2, 2, rows, width)
        gate_sum, up_sum = summed[0], summed[1]
        squash = jax.nn.sigmoid(gate_sum)
        hidden.append((gate_sum * squash * up_sum).astype(jnp.bfloat16))
        given = wide(cotangent[:, :, start : start + width])
        gate_act = given * up_sum * squash * (1.0 + gate_sum * (1.0 - squash))
        up_act = given * gate_sum * squash
        act = jnp.stack([gate_act, up_act]).astype(jnp.bfloat16)
        return act.reshape(2, 2 * rows, width)

    def finish(k, gathered, totals):
        start, _ = pieces[k]
        for value, owner in ((gathered, core), (send(gathered, pairs), 1 - core)):
            where = (owner * (share // tile)).astype(jnp.int32).reshape(1)
            totals = gradient(where, turned, value[:, None], totals, half, start, tile)
        return totals

    hidden, totals = [], ()
    act = gathered = None
    for k in range(-1, last):
        if act is not None:
            side_1, centre_1 = send(act, side), send(act, centre)
        if gathered is not None:
            totals = finish(k - 1, gathered, totals)
            terms = tie(terms, totals)
        far = add(terms[3], in_1).astype(WIRE)
        centre_2 = send(far, centre)
        in_2 = send(tie(terms[2], in_1).astype(WIRE), inward)
        if act is not None:
            out_2, share_2 = send(centre_1, outward), send(side_1, centre)
        following = None
        if k + 2 <= last:
            following = multiply(k + 2, (in_1,))
            terms = tie(terms, following)
        near = add(terms[2], in_2).astype(WIRE)
        swapped = jnp.where(at_end, terms[1], add(terms[0], centre_2)).astype(WIRE)
        centre_3, side_3 = send(near, centre), send(swapped, side)
        if following is not None:
            in_1 = send(tie(following[3], near, swapped).astype(WIRE), inward)
        if act is not None:
            out_3 = send(share_2, outward)
            gathered = jnp.stack(
                [
                    jnp.where(at_end, act, side_1),
                    jnp.where(at_end, side_1, act),
                    jnp.where(at_end, out_2, centre_1),
                    jnp.where(at_end, out_3, share_2),
                ]
            )
        own = jnp.where(at_end, terms[0], terms[1])
        act = activate(k + 1, add(own, side_3, centre_3))
        terms = following

    everything = lax.all_gather(act, "col", axis=0).reshape(line, 2, *act.shape)
    if gathered is not None:
        totals = finish(last - 1, gathered, totals)
    start, _ = pieces[last]
    both_cores = jnp.array([0, share // tile], jnp.int32)
    totals = gradient(both_cores, turned_in_place, everything, totals, half, start, tile)

    hidden = jnp.concatenate(hidden, axis=2).reshape(2, 2, slab, share)
    mine = lax.dynamic_index_in_dim(hidden, core, 1, keepdims=False)
    theirs = lax.dynamic_index_in_dim(hidden, 1 - core, 1, keepdims=False)
    hidden = by(core == 0, mine, send(theirs, pairs), 2)
    hidden = by(part == 0, hidden[0], lax.ppermute(hidden[1], "depth", swap), 1)
    return (hidden[None], *totals)


def contract(picked, piece):
    return lax.dot_general(
        picked, piece, (((0,), (0,)), ((), ())), preferred_element_type=jnp.float32
    )


def local_any(tokens, gate_weight, up_weight, grad_hidden):
    features = lax.all_gather(tokens[0], "row", axis=1, tiled=True)
    columns = gate_weight.shape[1]
    picked = features
    gate_part = jnp.dot(picked, gate_weight, preferred_element_type=jnp.float32)
    up_part = jnp.dot(picked, up_weight, preferred_element_type=jnp.float32)
    summed = lax.psum_scatter(
        jnp.concatenate([gate_part, up_part], axis=1), "col", scatter_dimension=0, tiled=True
    )
    gate_sum = summed[:, :columns]
    up_sum = summed[:, columns:]
    squash = jax.nn.sigmoid(gate_sum)
    hidden = (gate_sum * squash * up_sum).astype(jnp.bfloat16)
    cotangent = grad_hidden[0].astype(jnp.float32)
    gate_act = (cotangent * up_sum * squash * (1.0 + gate_sum * (1.0 - squash))).astype(
        jnp.bfloat16
    )
    up_act = (cotangent * gate_sum * squash).astype(jnp.bfloat16)
    picked = features
    gate_total = contract(picked, lax.all_gather(gate_act, "col", axis=0, tiled=True))
    up_total = contract(picked, lax.all_gather(up_act, "col", axis=0, tiled=True))
    grad_gate, grad_up = (
        lax.psum_scatter(gate_total, "depth", scatter_dimension=1, tiled=True),
        lax.psum_scatter(up_total, "depth", scatter_dimension=1, tiled=True),
    )
    return (hidden[None], grad_gate, grad_up)


def solution(mesh):
    in_specs = (
        P("depth", None, ("col", "row")),
        P("col", "row"),
        P("col", "row"),
        P("depth", "col", "row"),
    )
    out_specs = (P("depth", "col", "row"), P("col", ("row", "depth")), P("col", ("row", "depth")))
    sizes = tuple(mesh.shape[name] for name in ("row", "col", "depth"))
    return jax.shard_map(
        local if sizes == (2, 8, 2) else local_any,
        mesh=mesh,
        in_specs=in_specs,
        out_specs=out_specs,
        check_vma=False,
    )
```

```python
import functools
import math

import jax
import jax.numpy as jnp
from jax import lax
from jax.experimental import pallas as pl
from jax.experimental.pallas import tpu as pltpu
from jax.sharding import PartitionSpec as P

WIRE = jnp.float16
LARGEST_TOKEN, LARGEST_WEIGHT = 6.0, 0.0625
VMEM_LIMIT = 48 * 2**20
NO_COST = pl.CostEstimate(flops=0, bytes_accessed=0, transcendentals=0)
SHARES = (4, 3)


def forward_kernel(
    scale, place_ref, mine_ref, theirs_ref, gate_ref, up_ref, gate_far_ref, up_far_ref, out_ref
):
    blocks, _, rows, width = out_ref.shape
    for which, (near, far) in enumerate(((gate_ref, gate_far_ref), (up_ref, up_far_ref))):
        product = jnp.dot(mine_ref[...], near[...], preferred_element_type=jnp.float32)
        product += jnp.dot(theirs_ref[...], far[...], preferred_element_type=jnp.float32)
        out_ref[:, which] = (scale * product).reshape(blocks, rows, width)


def forward(place, mine, theirs, gate_weight, up_weight, far, start, tile, blocks, scale):
    total, depth = mine.shape
    width = far[0].shape[1]
    rows = total // blocks
    whole = pl.BlockSpec((total, depth), lambda j, place: (0, 0))
    weight = pl.BlockSpec((depth, tile), lambda j, place: (0, place[0] + start // tile + j))
    return pl.pallas_call(
        functools.partial(forward_kernel, scale),
        out_shape=jax.ShapeDtypeStruct((blocks, 2, rows, width), jnp.float32),
        grid_spec=pltpu.PrefetchScalarGridSpec(
            num_scalar_prefetch=1,
            grid=(width // tile,),
            in_specs=[
                whole,
                whole,
                weight,
                weight,
                pl.BlockSpec((depth, tile), lambda j, place: (0, j)),
                pl.BlockSpec((depth, tile), lambda j, place: (0, j)),
            ],
            out_specs=pl.BlockSpec((blocks, 2, rows, tile), lambda j, place: (0, 0, 0, j)),
        ),
        compiler_params=pltpu.CompilerParams(vmem_limit_bytes=VMEM_LIMIT),
        cost_estimate=NO_COST,
    )(place, mine, theirs, gate_weight, up_weight, *far)


def gradient_kernel(batches, place_ref, features_ref, *refs):
    acts, outs = refs[:batches], refs[-2:]
    for which, out_ref in enumerate(outs):
        parts = []
        for act_ref in acts:
            blocks, _, _, rows, width = act_ref.shape
            rows = rows * batches // 2
            for i in range(2 // batches):
                part = act_ref[:, 0, which, i * rows : (i + 1) * rows]
                parts.append(part.reshape(blocks * rows, width))
        out_ref[...] = jnp.dot(
            features_ref[...], jnp.concatenate(parts), preferred_element_type=jnp.float32
        )


def gradient(place, features, acts, totals, columns, start, tile):
    depth, total = features.shape
    blocks, cores, _, rows, width = acts[0].shape
    act_spec = pl.BlockSpec((blocks, 1, 2, rows, tile), lambda i, j, place: (0, i, 0, 0, j))
    out_spec = pl.BlockSpec((depth, tile), lambda i, j, place: (0, place[i] + start // tile + j))
    out_shape = jax.ShapeDtypeStruct((depth, columns), jnp.float32)
    in_specs = [pl.BlockSpec((depth, total), lambda i, j, place: (0, 0))]
    in_specs += [act_spec] * len(acts)
    in_specs += [pl.BlockSpec(memory_space=pl.ANY)] * len(totals)
    return pl.pallas_call(
        functools.partial(gradient_kernel, len(acts)),
        out_shape=(out_shape, out_shape),
        grid_spec=pltpu.PrefetchScalarGridSpec(
            num_scalar_prefetch=1,
            grid=(cores, width // tile),
            in_specs=in_specs,
            out_specs=(out_spec, out_spec),
        ),
        input_output_aliases={2 + len(acts) + i: i for i in range(len(totals))},
        compiler_params=pltpu.CompilerParams(vmem_limit_bytes=VMEM_LIMIT),
        cost_estimate=NO_COST,
    )(place, features, *acts, *totals)


def tie(value, *after):
    return lax.optimization_barrier((value, after))[0]


def cut(units, shares):
    edges = [round(units * sum(shares[:i]) / sum(shares)) for i in range(len(shares) + 1)]
    return [(a, b - a) for a, b in zip(edges, edges[1:]) if b > a]


def local(tokens, gate_weight, up_weight, grad_hidden):
    line = 4
    row, col, part = (lax.axis_index(name) for name in ("row", "col", "depth"))
    place, core = col // 2, col % 2
    slab = grad_hidden.shape[1]
    rows = 2 * slab
    depth, columns = gate_weight.shape
    half = columns // 2
    share = half // 2
    tile = 256 if share % 256 == 0 else 128
    largest = depth * 2 * line * LARGEST_TOKEN * LARGEST_WEIGHT
    scale = 2.0 ** math.floor(math.log2(65504 / largest))

    swap = [(0, 1), (1, 0)]
    pairs = [(i, i ^ 1) for i in range(2 * line)]

    def between(hops):
        return [(2 * i + c, 2 * j + c) for i, j in hops for c in (0, 1)]

    inward, outward = between([(0, 1), (3, 2)]), between([(1, 0), (2, 3)])
    side, centre = inward + outward, between([(1, 2), (2, 1)])
    at_end = (place == 0) | (place == line - 1)
    at_far = 2 * place >= line

    def send(value, route):
        return lax.ppermute(value, "col", route)

    def wide(value):
        return value.astype(jnp.float32)

    def add(*terms):
        return functools.reduce(jnp.add, map(wide, terms))

    def by(first, mine, theirs, axis):
        return jnp.where(
            first,
            jnp.concatenate([mine, theirs], axis=axis),
            jnp.concatenate([theirs, mine], axis=axis),
        )

    def columns_of(array, start, width):
        return lax.dynamic_slice_in_dim(array, start, width, array.ndim - 1)

    pieces = []
    for begin, count in cut(share // tile, SHARES):
        for batches in ((0, 1),) if pieces else ((0,), (1,)):
            pieces.append((batches, begin * tile, count * tile))
    last = len(pieces) - 1

    def exchange_weights(k, after):
        _, start, width = pieces[k]
        first = part * half + (1 - core) * share + start
        return [
            send(tie(columns_of(weight, first, width), after), pairs)
            for weight in (gate_weight, up_weight)
        ]

    mine = tokens[0]
    over_row = lax.ppermute(mine, "row", swap)
    over_depth = lax.ppermute(mine, "depth", swap)
    over_both = lax.ppermute(over_row, "depth", swap)
    far_weights = {0: exchange_weights(0, ())}
    far_weights[1] = far_weights[0]
    first_tile = ((part * half + core * share) // tile).astype(jnp.int32).reshape(1)

    def arrange(values):
        values = values.reshape(line, rows, depth)
        return jnp.where(at_far, values[::-1], values)

    def both_cores(values, after):
        values = arrange(tie(values, after))
        return values, send(values, pairs)

    def multiply(k, tokens, after):
        _, start, _ = pieces[k]
        mine, theirs = (value.reshape(-1, depth) for value in tie(tokens, after))
        weights = (gate_weight, up_weight, far_weights[k])
        return forward(first_tile, mine, theirs, *weights, start, tile, line, scale)

    features = [by(row == 0, mine, over_row, 1)]
    spread = [both_cores(features[0], ())]
    terms = multiply(0, spread[0], ())
    payload = terms[3].astype(WIRE)
    in_1 = send(payload, inward)

    over_depth, over_both = tie((over_depth, over_both), payload)
    features.append(by(row == 0, over_depth, over_both, 1))
    spread.append(both_cores(features[1], ()))
    far_weights[2] = exchange_weights(2, spread[1])

    mine_cotangent, cotangent = tie((grad_hidden[0], grad_hidden[0]), in_1)
    cotangent = jnp.stack(
        [
            columns_of(mine_cotangent, part * half, half),
            lax.ppermute(columns_of(cotangent, (1 - part) * half, half), "depth", swap),
        ]
    )
    cotangent = by(
        core == 0,
        columns_of(cotangent, core * share, share),
        send(columns_of(cotangent, (1 - core) * share, share), pairs),
        1,
    )

    def activate(k, summed):
        batches, start, width = pieces[k]
        summed = (summed * (1.0 / scale)).reshape(2, len(batches), rows, width)
        gate_sum, up_sum = summed[0], summed[1]
        squash = jax.nn.sigmoid(gate_sum)
        product = (gate_sum * squash * up_sum).astype(jnp.bfloat16)
        for position, batch in enumerate(batches):
            hidden[batch].append(product[position])
        given = jnp.stack([wide(cotangent[b][:, start : start + width]) for b in batches])
        gate_act = given * up_sum * squash * (1.0 + gate_sum * (1.0 - squash))
        up_act = given * gate_sum * squash
        act = jnp.stack([gate_act, up_act]).astype(jnp.bfloat16)
        return act.reshape(2, len(batches) * rows, width)

    def merge(act, side_1, centre_1, out_2, share_2, out_3):
        blocks = jnp.stack(
            [
                jnp.where(at_end, act, side_1),
                jnp.where(at_end, side_1, act),
                jnp.where(at_end, out_2, centre_1),
                jnp.where(at_end, out_3, share_2),
            ]
        )
        return blocks, send(blocks, pairs)

    turned = jnp.concatenate([tie(near, in_1).reshape(-1, depth) for near, _ in spread]).T
    turned_in_place = jnp.concatenate([tie(value, in_1) for value in features]).T

    def finish(gathered, totals, start):
        own, other = [value for value, _ in gathered], [value for _, value in gathered]
        for values, owner in ((own, core), (other, 1 - core)):
            where = (owner * (share // tile)).astype(jnp.int32).reshape(1)
            values = [value[:, None] for value in values]
            totals = gradient(where, turned, values, totals, half, start, tile)
        return totals

    hidden, totals, waiting = ([], []), (), []
    act = hops = None
    for k in range(-1, last):
        if act is not None:
            side_1, centre_1 = send(act, side), send(act, centre)
        if hops is not None:
            waiting.append(merge(*hops))
            terms = tie(terms, waiting[-1][0])
        far = add(terms[3], in_1).astype(WIRE)
        centre_2 = send(far, centre)
        in_2 = send(tie(terms[2], in_1).astype(WIRE), inward)
        if act is not None:
            out_2, share_2 = send(centre_1, outward), send(side_1, centre)
        following = None
        if k + 2 <= last:
            tokens = spread[1] if k < 0 else [jnp.stack(pair, axis=1) for pair in zip(*spread)]
            following = multiply(k + 2, tokens, (in_1, *(() if act is None else (side_1, centre_1))))
            terms = tie(terms, following)
        near = add(terms[2], in_2).astype(WIRE)
        swapped = jnp.where(at_end, terms[1], add(terms[0], centre_2)).astype(WIRE)
        centre_3, side_3 = send(near, centre), send(swapped, side)
        if following is not None:
            in_1 = send(tie(following[3], near, swapped).astype(WIRE), inward)
        if act is not None:
            out_3 = send(share_2, outward)
        own = jnp.where(at_end, terms[0], terms[1])
        ready = activate(k + 1, add(own, side_3, centre_3))
        if act is not None:
            hops = tie((act, side_1, centre_1, out_2, share_2, out_3), ready)
        act, terms = ready, following

    everything = lax.all_gather(tie(act, share_2), "col", axis=0).reshape(line, 2, *act.shape)
    waiting.append(merge(*hops))
    totals = finish(waiting, totals, pieces[0][1])
    places = jnp.array([0, share // tile], jnp.int32)
    totals = gradient(places, turned_in_place, [everything], totals, half, pieces[last][1], tile)

    hidden = jnp.stack([jnp.concatenate(parts, axis=1) for parts in hidden])
    hidden = hidden.reshape(2, 2, slab, share)
    mine = lax.dynamic_index_in_dim(hidden, core, 1, keepdims=False)
    theirs = lax.dynamic_index_in_dim(hidden, 1 - core, 1, keepdims=False)
    hidden = by(core == 0, mine, send(theirs, pairs), 2)
    hidden = by(part == 0, hidden[0], lax.ppermute(hidden[1], "depth", swap), 1)
    return (hidden[None], *totals)


def contract(picked, piece):
    return lax.dot_general(
        picked, piece, (((0,), (0,)), ((), ())), preferred_element_type=jnp.float32
    )


def local_any(tokens, gate_weight, up_weight, grad_hidden):
    features = lax.all_gather(tokens[0], "row", axis=1, tiled=True)
    columns = gate_weight.shape[1]
    picked = features
    gate_part = jnp.dot(picked, gate_weight, preferred_element_type=jnp.float32)
    up_part = jnp.dot(picked, up_weight, preferred_element_type=jnp.float32)
    summed = lax.psum_scatter(
        jnp.concatenate([gate_part, up_part], axis=1), "col", scatter_dimension=0, tiled=True
    )
    gate_sum = summed[:, :columns]
    up_sum = summed[:, columns:]
    squash = jax.nn.sigmoid(gate_sum)
    hidden = (gate_sum * squash * up_sum).astype(jnp.bfloat16)
    cotangent = grad_hidden[0].astype(jnp.float32)
    gate_act = (cotangent * up_sum * squash * (1.0 + gate_sum * (1.0 - squash))).astype(
        jnp.bfloat16
    )
    up_act = (cotangent * gate_sum * squash).astype(jnp.bfloat16)
    picked = features
    gate_total = contract(picked, lax.all_gather(gate_act, "col", axis=0, tiled=True))
    up_total = contract(picked, lax.all_gather(up_act, "col", axis=0, tiled=True))
    grad_gate, grad_up = (
        lax.psum_scatter(gate_total, "depth", scatter_dimension=1, tiled=True),
        lax.psum_scatter(up_total, "depth", scatter_dimension=1, tiled=True),
    )
    return (hidden[None], grad_gate, grad_up)


def solution(mesh):
    in_specs = (
        P("depth", None, ("col", "row")),
        P("col", "row"),
        P("col", "row"),
        P("depth", "col", "row"),
    )
    out_specs = (P("depth", "col", "row"), P("col", ("row", "depth")), P("col", ("row", "depth")))
    sizes = tuple(mesh.shape[name] for name in ("row", "col", "depth"))
    return jax.shard_map(
        local if sizes == (2, 8, 2) else local_any,
        mesh=mesh,
        in_specs=in_specs,
        out_specs=out_specs,
        check_vma=False,
    )
```

```python
import functools
import math

import jax
import jax.numpy as jnp
from jax import lax
from jax.experimental import pallas as pl
from jax.experimental.pallas import tpu as pltpu
from jax.sharding import PartitionSpec as P

WIRE = jnp.float16
LARGEST_TOKEN, LARGEST_WEIGHT = 6.0, 0.0625
VMEM_LIMIT = 48 * 2**20
NO_COST = pl.CostEstimate(flops=0, bytes_accessed=0, transcendentals=0)
SHARES = (2, 2, 2, 1)


def forward_kernel(
    scale, place_ref, mine_ref, theirs_ref, gate_ref, up_ref, gate_far_ref, up_far_ref, out_ref
):
    blocks, _, rows, width = out_ref.shape
    for which, (near, far) in enumerate(((gate_ref, gate_far_ref), (up_ref, up_far_ref))):
        product = jnp.dot(mine_ref[...], near[...], preferred_element_type=jnp.float32)
        product += jnp.dot(theirs_ref[...], far[...], preferred_element_type=jnp.float32)
        out_ref[:, which] = (scale * product).reshape(blocks, rows, width)


def forward(place, mine, theirs, gate_weight, up_weight, far, start, tile, blocks, scale):
    total, depth = mine.shape
    width = far[0].shape[1]
    rows = total // blocks
    whole = pl.BlockSpec((total, depth), lambda j, place: (0, 0))
    weight = pl.BlockSpec((depth, tile), lambda j, place: (0, place[0] + start // tile + j))
    return pl.pallas_call(
        functools.partial(forward_kernel, scale),
        out_shape=jax.ShapeDtypeStruct((blocks, 2, rows, width), jnp.float32),
        grid_spec=pltpu.PrefetchScalarGridSpec(
            num_scalar_prefetch=1,
            grid=(width // tile,),
            in_specs=[
                whole,
                whole,
                weight,
                weight,
                pl.BlockSpec((depth, tile), lambda j, place: (0, j)),
                pl.BlockSpec((depth, tile), lambda j, place: (0, j)),
            ],
            out_specs=pl.BlockSpec((blocks, 2, rows, tile), lambda j, place: (0, 0, 0, j)),
        ),
        compiler_params=pltpu.CompilerParams(vmem_limit_bytes=VMEM_LIMIT),
        cost_estimate=NO_COST,
    )(place, mine, theirs, gate_weight, up_weight, *far)


def gradient_kernel(batches, place_ref, features_ref, *refs):
    own, other, outs = refs[: 2 * batches], refs[2 * batches : 4 * batches], refs[-2:]

    def fill(acts):
        for which, out_ref in enumerate(outs):
            parts = []
            for batch in range(2):
                for act_ref in acts if batches == 1 else acts[2 * batch : 2 * batch + 2]:
                    blocks, _, rows, width = act_ref.shape
                    rows = rows * batches // 2
                    first = batch * rows if batches == 1 else 0
                    part = act_ref[:, which, first : first + rows]
                    parts.append(part.reshape(blocks * rows, width))
            out_ref[...] = jnp.dot(
                features_ref[...], jnp.concatenate(parts), preferred_element_type=jnp.float32
            )

    for which, acts in enumerate((own, other)):
        pl.when(pl.program_id(0) == which)(functools.partial(fill, acts))


def gradient(place, features, own, other, totals, columns, start, tile):
    depth, total = features.shape
    blocks, _, rows, width = own[0].shape
    tiles = width // tile
    shape = (blocks, 2, rows, tile)
    own_spec = pl.BlockSpec(
        shape, lambda i, j, place: (0, 0, 0, jnp.where(i == 0, j, tiles - 1))
    )
    other_spec = pl.BlockSpec(shape, lambda i, j, place: (0, 0, 0, jnp.where(i == 0, 0, j)))
    out_spec = pl.BlockSpec((depth, tile), lambda i, j, place: (0, place[i] + start // tile + j))
    out_shape = jax.ShapeDtypeStruct((depth, columns), jnp.float32)
    in_specs = [pl.BlockSpec((depth, total), lambda i, j, place: (0, 0))]
    in_specs += [own_spec] * len(own) + [other_spec] * len(other)
    in_specs += [pl.BlockSpec(memory_space=pl.ANY)] * len(totals)
    first = 2 + len(own) + len(other)
    return pl.pallas_call(
        functools.partial(gradient_kernel, len(own) // 2),
        out_shape=(out_shape, out_shape),
        grid_spec=pltpu.PrefetchScalarGridSpec(
            num_scalar_prefetch=1,
            grid=(2, tiles),
            in_specs=in_specs,
            out_specs=(out_spec, out_spec),
        ),
        input_output_aliases={first + i: i for i in range(len(totals))},
        compiler_params=pltpu.CompilerParams(vmem_limit_bytes=VMEM_LIMIT),
        cost_estimate=NO_COST,
    )(place, features, *own, *other, *totals)


def tie(value, *after):
    return lax.optimization_barrier((value, after))[0]


def cut(units, shares):
    edges = [round(units * sum(shares[:i]) / sum(shares)) for i in range(len(shares) + 1)]
    return [(a, b - a) for a, b in zip(edges, edges[1:]) if b > a]


def local(tokens, gate_weight, up_weight, grad_hidden):
    line = 4
    row, col, part = (lax.axis_index(name) for name in ("row", "col", "depth"))
    chip, core = col // 2, col % 2
    slab = grad_hidden.shape[1]
    rows = 2 * slab
    depth, columns = gate_weight.shape
    half = columns // 2
    share = half // 2
    tile = 256 if share % 256 == 0 else 128
    largest = depth * 2 * line * LARGEST_TOKEN * LARGEST_WEIGHT
    scale = 2.0 ** math.floor(math.log2(65504 / largest))

    swap = [(0, 1), (1, 0)]
    pairs = [(i, i ^ 1) for i in range(2 * line)]

    def between(hops):
        return [(2 * i + c, 2 * j + c) for i, j in hops for c in (0, 1)]

    inward, outward = between([(0, 1), (3, 2)]), between([(1, 0), (2, 3)])
    centre = between([(1, 2), (2, 1)])
    at_end = (chip == 0) | (chip == line - 1)
    at_far = 2 * chip >= line

    def send(value, route):
        return lax.ppermute(value, "col", route)

    def wide(value):
        return value.astype(jnp.float32)

    def add(*terms):
        return functools.reduce(jnp.add, map(wide, terms))

    def by(first, mine, theirs, axis):
        return jnp.where(
            first,
            jnp.concatenate([mine, theirs], axis=axis),
            jnp.concatenate([theirs, mine], axis=axis),
        )

    def columns_of(array, start, width):
        return lax.dynamic_slice_in_dim(array, start, width, array.ndim - 1)

    pieces = []
    for begin, count in cut(share // tile, SHARES):
        for batches in ((0, 1),) if pieces else ((0,), (1,)):
            pieces.append((batches, begin * tile, count * tile))
    last = len(pieces) - 1

    def exchange_weights(k, after):
        _, start, width = pieces[k]
        first = part * half + (1 - core) * share + start
        return [
            send(tie(columns_of(weight, first, width), after), pairs)
            for weight in (gate_weight, up_weight)
        ]

    mine = tokens[0]
    over_row = lax.ppermute(mine, "row", swap)
    over_depth = lax.ppermute(mine, "depth", swap)
    over_both = lax.ppermute(over_row, "depth", swap)
    far_weights = {0: exchange_weights(0, ())}
    far_weights[1] = far_weights[0]
    first_tile = ((part * half + core * share) // tile).astype(jnp.int32).reshape(1)

    def arrange(values):
        values = values.reshape(line, rows, depth)
        return jnp.where(at_far, values[::-1], values)

    def both_cores(values, after):
        values = arrange(tie(values, after))
        return values, send(values, pairs)

    def multiply(k, tokens, after):
        _, start, _ = pieces[k]
        mine, theirs = (value.reshape(-1, depth) for value in tie(tokens, after))
        weights = (gate_weight, up_weight, far_weights[k])
        return forward(first_tile, mine, theirs, *weights, start, tile, line, scale)

    features = [by(row == 0, mine, over_row, 1)]
    spread = [both_cores(features[0], ())]
    terms = {0: multiply(0, spread[0], ())}
    payload = terms[0].astype(WIRE)
    inner = {0: send(payload, inward)}

    over_depth, over_both = tie((over_depth, over_both), payload)
    features.append(by(row == 0, over_depth, over_both, 1))
    spread.append(both_cores(features[1], ()))
    for k in range(2, last + 1):
        far_weights[k] = exchange_weights(k, spread[1] if k < 4 else inner[0])

    mine_cotangent, cotangent = tie((grad_hidden[0], grad_hidden[0]), payload)
    cotangent = jnp.stack(
        [
            columns_of(mine_cotangent, part * half, half),
            lax.ppermute(columns_of(cotangent, (1 - part) * half, half), "depth", swap),
        ]
    )
    cotangent = by(
        core == 0,
        columns_of(cotangent, core * share, share),
        send(columns_of(cotangent, (1 - core) * share, share), pairs),
        1,
    )
    cotangent = jnp.stack([send(cotangent, inward), cotangent])

    def activate(k, summed):
        batches, start, width = pieces[k]
        summed = (summed * (1.0 / scale)).reshape(2, 2, len(batches), rows, width)
        gate_sum, up_sum = summed[:, 0], summed[:, 1]
        squash = jax.nn.sigmoid(gate_sum)
        product = (gate_sum * squash * up_sum).astype(jnp.bfloat16)
        given = wide(cotangent[:, batches[0] : batches[-1] + 1, :, start : start + width])
        gate_act = given * up_sum * squash * (1.0 + gate_sum * (1.0 - squash))
        up_act = given * gate_sum * squash
        act = jnp.stack([gate_act, up_act], axis=1).astype(jnp.bfloat16)
        return product, act.reshape(2, 2, len(batches) * rows, width)

    def by_side(values):
        values = values.reshape(line, rows * depth)
        values = jnp.concatenate([values[:2], values[3:], values[2:3]])
        return values.reshape(-1, depth)

    turned = jnp.concatenate([by_side(tie(near, inner[0])) for near, _ in spread]).T
    place = jnp.stack([core, 1 - core]).astype(jnp.int32) * (share // tile)

    def outer_hidden(ks):
        def joined(batch, which):
            chosen = [
                hidden[k][which, pieces[k][0].index(batch)] for k in ks if batch in pieces[k][0]
            ]
            return jnp.concatenate(chosen, axis=1)

        own = [joined(batch, 1) for batch in range(2)]
        theirs = send(jnp.stack([joined(batch, 0) for batch in range(2)]), outward)
        return jnp.where(at_end, theirs, jnp.stack(own))

    got, act, hidden, near_out, far_out, across = {}, {}, {}, {}, {}, {}
    totals, waiting, hiddens = (), [], []
    for t in range(last + 3):
        before = []
        k = t - 1
        if 0 <= k <= last:
            summed = jnp.stack([terms[k][0] + wide(got[k][1]), terms[k][1] + wide(got[k][0])])
            hidden[k], act[k] = activate(k, summed)
            across[k], near_out[k] = send(act[k], centre), send(act[k], outward)
            before.append(act[k])
            if k == last - 1:
                hiddens.append(outer_hidden(range(last)))
            if k == last:
                hiddens.append(outer_hidden([last]))
        k = t - 2
        if 0 <= k <= last:
            near_mine, near_got, far_mine, far_got = tie(
                (act[k], near_out[k], across[k], far_out[k]), before
            )
            mine = [
                jnp.where(at_end, near_got, near_mine),
                jnp.where(at_end, far_got, far_mine),
            ]
            waiting.append((mine, [send(value, pairs) for value in mine]))
        k = t + 1
        if k <= last:
            tokens = spread[1] if k == 1 else [jnp.stack(pair, axis=1) for pair in zip(*spread)]
            terms[k] = multiply(k, tokens, before)
            payload = terms[k].astype(WIRE)
            inner[k] = send(payload, inward)
            before.append(payload)
        k = t - 2
        if 0 <= k <= last and pieces[k][0] != (0,):
            own, other = (sum(values, []) for values in zip(*waiting))
            totals = gradient(place, turned, own, other, totals, half, pieces[k][1], tile)
            waiting = []
            before.append(totals)
        k = t
        if k <= last:
            terms[k] = tie(terms[k], before) + wide(inner[k])
            got[k] = send(terms[k][2:].astype(WIRE), centre)
        k = t - 1
        if 0 <= k <= last:
            far_out[k] = send(across[k], outward)

    hidden = jnp.concatenate(hiddens, axis=2).reshape(2, 2, slab, share)
    mine = lax.dynamic_index_in_dim(hidden, core, 1, keepdims=False)
    theirs = lax.dynamic_index_in_dim(hidden, 1 - core, 1, keepdims=False)
    hidden = by(core == 0, mine, send(theirs, pairs), 2)
    hidden = by(part == 0, hidden[0], lax.ppermute(hidden[1], "depth", swap), 1)
    return (hidden[None], *totals)


def contract(picked, piece):
    return lax.dot_general(
        picked, piece, (((0,), (0,)), ((), ())), preferred_element_type=jnp.float32
    )


def local_any(tokens, gate_weight, up_weight, grad_hidden):
    features = lax.all_gather(tokens[0], "row", axis=1, tiled=True)
    columns = gate_weight.shape[1]
    picked = features
    gate_part = jnp.dot(picked, gate_weight, preferred_element_type=jnp.float32)
    up_part = jnp.dot(picked, up_weight, preferred_element_type=jnp.float32)
    summed = lax.psum_scatter(
        jnp.concatenate([gate_part, up_part], axis=1), "col", scatter_dimension=0, tiled=True
    )
    gate_sum = summed[:, :columns]
    up_sum = summed[:, columns:]
    squash = jax.nn.sigmoid(gate_sum)
    hidden = (gate_sum * squash * up_sum).astype(jnp.bfloat16)
    cotangent = grad_hidden[0].astype(jnp.float32)
    gate_act = (cotangent * up_sum * squash * (1.0 + gate_sum * (1.0 - squash))).astype(
        jnp.bfloat16
    )
    up_act = (cotangent * gate_sum * squash).astype(jnp.bfloat16)
    picked = features
    gate_total = contract(picked, lax.all_gather(gate_act, "col", axis=0, tiled=True))
    up_total = contract(picked, lax.all_gather(up_act, "col", axis=0, tiled=True))
    grad_gate, grad_up = (
        lax.psum_scatter(gate_total, "depth", scatter_dimension=1, tiled=True),
        lax.psum_scatter(up_total, "depth", scatter_dimension=1, tiled=True),
    )
    return (hidden[None], grad_gate, grad_up)


def solution(mesh):
    in_specs = (
        P("depth", None, ("col", "row")),
        P("col", "row"),
        P("col", "row"),
        P("depth", "col", "row"),
    )
    out_specs = (P("depth", "col", "row"), P("col", ("row", "depth")), P("col", ("row", "depth")))
    sizes = tuple(mesh.shape[name] for name in ("row", "col", "depth"))
    return jax.shard_map(
        local if sizes == (2, 8, 2) else local_any,
        mesh=mesh,
        in_specs=in_specs,
        out_specs=out_specs,
        check_vma=False,
    )
```

```python
import functools
import math

import jax
import jax.numpy as jnp
from jax import lax
from jax.experimental import pallas as pl
from jax.experimental.pallas import tpu as pltpu
from jax.sharding import PartitionSpec as P

WIRE = jnp.float16
LARGEST_TOKEN, LARGEST_WEIGHT = 6.0, 0.0625
VMEM_LIMIT = 48 * 2**20
NO_COST = pl.CostEstimate(flops=0, bytes_accessed=0, transcendentals=0)
SHARES = (2, 2, 2, 1)


def forward_kernel(
    scale, place_ref, mine_ref, theirs_ref, gate_ref, up_ref, gate_far_ref, up_far_ref, out_ref
):
    blocks, _, rows, width = out_ref.shape
    for which, (near, far) in enumerate(((gate_ref, gate_far_ref), (up_ref, up_far_ref))):
        product = jnp.dot(mine_ref[...], near[...], preferred_element_type=jnp.float32)
        product += jnp.dot(theirs_ref[...], far[0, 0], preferred_element_type=jnp.float32)
        out_ref[:, which] = (scale * product).reshape(blocks, rows, width)


def forward(place, mine, theirs, gate_weight, up_weight, far, start, tile, blocks, scale):
    total, depth = mine.shape
    width = far[0].shape[3]
    up_index = far[1].shape[1] - 1
    rows = total // blocks
    whole = pl.BlockSpec((total, depth), lambda j, place: (0, 0))
    weight = pl.BlockSpec((depth, tile), lambda j, place: (0, place[0] + start // tile + j))
    return pl.pallas_call(
        functools.partial(forward_kernel, scale),
        out_shape=jax.ShapeDtypeStruct((blocks, 2, rows, width), jnp.float32),
        grid_spec=pltpu.PrefetchScalarGridSpec(
            num_scalar_prefetch=1,
            grid=(width // tile,),
            in_specs=[
                whole,
                whole,
                weight,
                weight,
                pl.BlockSpec((1, 1, depth, tile), lambda j, place: (place[1], 0, 0, j)),
                pl.BlockSpec((1, 1, depth, tile), lambda j, place: (place[1], up_index, 0, j)),
            ],
            out_specs=pl.BlockSpec((blocks, 2, rows, tile), lambda j, place: (0, 0, 0, j)),
        ),
        compiler_params=pltpu.CompilerParams(vmem_limit_bytes=VMEM_LIMIT),
        cost_estimate=NO_COST,
    )(place, mine, theirs, gate_weight, up_weight, *far)


def gradient_kernel(batches, features_ref, *refs):
    acts, outs = refs[: 2 * batches], refs[-2:]
    for which, out_ref in enumerate(outs):
        parts = []
        for batch in range(2):
            for act_ref in acts if batches == 1 else acts[2 * batch : 2 * batch + 2]:
                _, blocks, _, rows, width = act_ref.shape
                rows = rows * batches // 2
                first = batch * rows if batches == 1 else 0
                part = act_ref[0, :, which, first : first + rows]
                parts.append(part.reshape(blocks * rows, width))
        out_ref[...] = jnp.dot(
            features_ref[...], jnp.concatenate(parts), preferred_element_type=jnp.float32
        )


def gradient(features, acts, totals, columns, start, tile):
    depth, total = features.shape
    cores, blocks, _, rows, width = acts[0].shape
    share = columns // cores // tile
    act_spec = pl.BlockSpec((1, blocks, 2, rows, tile), lambda i, j: (i, 0, 0, 0, j))
    out_spec = pl.BlockSpec((depth, tile), lambda i, j: (0, i * share + start // tile + j))
    out_shape = jax.ShapeDtypeStruct((depth, columns), jnp.float32)
    in_specs = [pl.BlockSpec((depth, total), lambda i, j: (0, 0))] + [act_spec] * len(acts)
    in_specs += [pl.BlockSpec(memory_space=pl.ANY)] * len(totals)
    return pl.pallas_call(
        functools.partial(gradient_kernel, len(acts) // 2),
        out_shape=(out_shape, out_shape),
        grid=(cores, width // tile),
        in_specs=in_specs,
        out_specs=(out_spec, out_spec),
        input_output_aliases={1 + len(acts) + i: i for i in range(len(totals))},
        compiler_params=pltpu.CompilerParams(vmem_limit_bytes=VMEM_LIMIT),
        cost_estimate=NO_COST,
    )(features, *acts, *totals)


def tie(value, *after):
    return lax.optimization_barrier((value, after))[0]


def cut(units, shares):
    edges = [round(units * sum(shares[:i]) / sum(shares)) for i in range(len(shares) + 1)]
    return [(a, b - a) for a, b in zip(edges, edges[1:]) if b > a]


def local(tokens, gate_weight, up_weight, grad_hidden):
    line = 4
    row, col, part = (lax.axis_index(name) for name in ("row", "col", "depth"))
    chip, core = col // 2, col % 2
    slab = grad_hidden.shape[1]
    rows = 2 * slab
    depth, columns = gate_weight.shape
    half = columns // 2
    share = half // 2
    tile = 256 if share % 256 == 0 else 128
    largest = depth * 2 * line * LARGEST_TOKEN * LARGEST_WEIGHT
    scale = 2.0 ** math.floor(math.log2(65504 / largest))

    swap = [(0, 1), (1, 0)]
    pairs = [(i, i ^ 1) for i in range(2 * line)]

    def between(hops):
        return [(2 * i + c, 2 * j + c) for i, j in hops for c in (0, 1)]

    inward, outward = between([(0, 1), (3, 2)]), between([(1, 0), (2, 3)])
    centre = between([(1, 2), (2, 1)])
    at_end = (chip == 0) | (chip == line - 1)
    at_far = 2 * chip >= line

    def send(value, route):
        return lax.ppermute(value, "col", route)

    def wide(value):
        return value.astype(jnp.float32)

    def add(*terms):
        return functools.reduce(jnp.add, map(wide, terms))

    def by(first, mine, theirs, axis):
        return jnp.where(
            first,
            jnp.concatenate([mine, theirs], axis=axis),
            jnp.concatenate([theirs, mine], axis=axis),
        )

    def columns_of(array, start, width):
        return lax.dynamic_slice_in_dim(array, start, width, array.ndim - 1)

    pieces = []
    for begin, count in cut(share // tile, SHARES):
        for batches in ((0, 1),) if pieces else ((0,), (1,)):
            pieces.append((batches, begin * tile, count * tile))
    last = len(pieces) - 1

    both = [[2 * i, 2 * i + 1] for i in range(line)]

    def share_pair(value):
        return lax.all_gather(value, "col", axis=0, axis_index_groups=both)

    def exchange_weights(k, after):
        _, start, width = pieces[k]
        first = part * half + (1 - core) * share + start
        chosen = [
            columns_of(weight, first, width) for weight in tie((gate_weight, up_weight), after)
        ]
        if k == 0:
            return [send(value, pairs)[None, None] for value in chosen]
        return [share_pair(jnp.stack(chosen))] * 2

    mine = tokens[0]
    over_row = lax.ppermute(mine, "row", swap)
    cotangent = grad_hidden[0]
    cotangent = jnp.stack(
        [
            columns_of(cotangent, part * half, half),
            lax.ppermute(columns_of(cotangent, (1 - part) * half, half), "depth", swap),
        ]
    )
    over_depth = lax.ppermute(mine, "depth", swap)
    over_both = lax.ppermute(over_row, "depth", swap)
    far_weights = {0: exchange_weights(0, ())}
    far_weights[1] = far_weights[0]
    first_tile = (part * half + core * share) // tile

    cotangent = by(
        core == 0,
        columns_of(cotangent, core * share, share),
        send(columns_of(cotangent, (1 - core) * share, share), pairs),
        1,
    )
    cotangent = jnp.stack([send(cotangent, inward), cotangent])

    def arrange(values):
        values = values.reshape(line, rows, depth)
        return jnp.where(at_far, values[::-1], values)

    def both_cores(values, after):
        values = arrange(tie(values, after))
        return values, send(values, pairs)

    def multiply(k, tokens, after):
        _, start, _ = pieces[k]
        mine, theirs = (value.reshape(-1, depth) for value in tie(tokens, after))
        weights = (gate_weight, up_weight, far_weights[k])
        where = jnp.stack([first_tile, jnp.where(k < 2, 0, 1 - core)]).astype(jnp.int32)
        return forward(where, mine, theirs, *weights, start, tile, line, scale)

    features = [by(row == 0, mine, over_row, 1)]
    spread = [both_cores(features[0], ())]
    terms = {0: multiply(0, spread[0], ())}
    payload = terms[0].astype(WIRE)
    inner = {0: send(payload, inward)}

    over_depth, over_both = tie((over_depth, over_both), payload)
    features.append(by(row == 0, over_depth, over_both, 1))
    spread.append(both_cores(features[1], ()))
    far_weights[2] = exchange_weights(2, payload)
    both_rows = [jnp.stack(pair, axis=1) for pair in zip(*spread)]

    def activate(k, summed):
        batches, start, width = pieces[k]
        summed = (summed * (1.0 / scale)).reshape(2, 2, len(batches), rows, width)
        gate_sum, up_sum = summed[:, 0], summed[:, 1]
        squash = jax.nn.sigmoid(gate_sum)
        product = (gate_sum * squash * up_sum).astype(jnp.bfloat16)
        given = wide(cotangent[:, batches[0] : batches[-1] + 1, :, start : start + width])
        given = given * squash
        gate_act = given * up_sum * (1.0 + gate_sum * (1.0 - squash))
        up_act = given * gate_sum
        is_gate = lax.broadcasted_iota(jnp.int32, (2, 2, *given.shape[1:]), 1) == 0
        act = jnp.where(is_gate, gate_act[:, None], up_act[:, None]).astype(jnp.bfloat16)
        return product, act.reshape(2, 2, len(batches) * rows, width)

    def by_side(values):
        values = values.reshape(line, rows, depth)
        values = jnp.concatenate([values[:2], values[3:], values[2:3]])
        return values.reshape(-1, depth)

    turned = jnp.concatenate([by_side(tie(near, inner[0])) for near, _ in spread]).T

    def outer_hidden(ks):
        def joined(batch, which):
            chosen = [
                hidden[k][which, pieces[k][0].index(batch)] for k in ks if batch in pieces[k][0]
            ]
            return jnp.concatenate(chosen, axis=1)

        own = [joined(batch, 1) for batch in range(2)]
        theirs = send(jnp.stack([joined(batch, 0) for batch in range(2)]), outward)
        return jnp.where(at_end, theirs, jnp.stack(own))

    got, act, hidden, near_out, far_out, across = {}, {}, {}, {}, {}, {}
    totals, waiting, hiddens = (), [], []
    for t in range(last + 3):
        before = []
        k = t - 1
        if 0 <= k <= last:
            hidden[k], act[k] = activate(k, add(terms[k][:2], inner[k][:2], got[k][::-1]))
            across[k], near_out[k] = send(act[k], centre), send(act[k], outward)
            before.append(act[k])
            if k == last - 1:
                hiddens.append(outer_hidden(range(last)))
            if k == last:
                hiddens.append(outer_hidden([last]))
        k = t - 2
        if 0 <= k <= last:
            near_mine, near_got, far_mine, far_got = tie(
                (act[k], near_out[k], across[k], far_out[k]), before
            )
            mine = [
                jnp.where(at_end, near_got, near_mine),
                jnp.where(at_end, far_got, far_mine),
            ]
            waiting += [share_pair(value) for value in mine]
        k = t + 1
        if k <= last:
            tokens = spread[1] if k == 1 else both_rows
            terms[k] = multiply(k, tokens, before)
            payload = terms[k].astype(WIRE)
            inner[k] = send(payload, inward)
            before.append(payload)
            if 2 < k + 2 <= last:
                far_weights[k + 2] = exchange_weights(k + 2, payload)
        k = t - 2
        if 0 <= k <= last and pieces[k][0] != (0,):
            totals = gradient(turned, waiting, totals, half, pieces[k][1], tile)
            waiting = []
            before.append(totals)
        k = t
        if k <= last:
            terms[k] = tie(terms[k], before)
            got[k] = send(add(terms[k][2:], inner[k][2:]).astype(WIRE), centre)
        k = t - 1
        if 0 <= k <= last:
            far_out[k] = send(across[k], outward)

    hidden = jnp.concatenate(hiddens, axis=2).reshape(2, 2, slab, share)
    mine = lax.dynamic_index_in_dim(hidden, core, 1, keepdims=False)
    theirs = lax.dynamic_index_in_dim(hidden, 1 - core, 1, keepdims=False)
    hidden = by(core == 0, mine, send(theirs, pairs), 2)
    hidden = by(part == 0, hidden[0], lax.ppermute(hidden[1], "depth", swap), 1)
    return (hidden[None], *totals)


def contract(picked, piece):
    return lax.dot_general(
        picked, piece, (((0,), (0,)), ((), ())), preferred_element_type=jnp.float32
    )


def local_any(tokens, gate_weight, up_weight, grad_hidden):
    features = lax.all_gather(tokens[0], "row", axis=1, tiled=True)
    columns = gate_weight.shape[1]
    picked = features
    gate_part = jnp.dot(picked, gate_weight, preferred_element_type=jnp.float32)
    up_part = jnp.dot(picked, up_weight, preferred_element_type=jnp.float32)
    summed = lax.psum_scatter(
        jnp.concatenate([gate_part, up_part], axis=1), "col", scatter_dimension=0, tiled=True
    )
    gate_sum = summed[:, :columns]
    up_sum = summed[:, columns:]
    squash = jax.nn.sigmoid(gate_sum)
    hidden = (gate_sum * squash * up_sum).astype(jnp.bfloat16)
    cotangent = grad_hidden[0].astype(jnp.float32)
    gate_act = (cotangent * up_sum * squash * (1.0 + gate_sum * (1.0 - squash))).astype(
        jnp.bfloat16
    )
    up_act = (cotangent * gate_sum * squash).astype(jnp.bfloat16)
    picked = features
    gate_total = contract(picked, lax.all_gather(gate_act, "col", axis=0, tiled=True))
    up_total = contract(picked, lax.all_gather(up_act, "col", axis=0, tiled=True))
    grad_gate, grad_up = (
        lax.psum_scatter(gate_total, "depth", scatter_dimension=1, tiled=True),
        lax.psum_scatter(up_total, "depth", scatter_dimension=1, tiled=True),
    )
    return (hidden[None], grad_gate, grad_up)


def solution(mesh):
    in_specs = (
        P("depth", None, ("col", "row")),
        P("col", "row"),
        P("col", "row"),
        P("depth", "col", "row"),
    )
    out_specs = (P("depth", "col", "row"), P("col", ("row", "depth")), P("col", ("row", "depth")))
    sizes = tuple(mesh.shape[name] for name in ("row", "col", "depth"))
    return jax.shard_map(
        local if sizes == (2, 8, 2) else local_any,
        mesh=mesh,
        in_specs=in_specs,
        out_specs=out_specs,
        check_vma=False,
    )
```

```python
import functools
import math

import jax
import jax.numpy as jnp
from jax import lax
from jax.experimental import pallas as pl
from jax.experimental.pallas import tpu as pltpu
from jax.sharding import PartitionSpec as P

WIRE = jnp.float16
LARGEST_TOKEN, LARGEST_WEIGHT = 6.0, 0.0625
VMEM_LIMIT = 48 * 2**20
SHARES = (2, 2, 2, 1)


def forward_kernel(
    scale, place_ref, mine_ref, theirs_ref, gate_ref, up_ref, gate_far_ref, up_far_ref, out_ref
):
    blocks, _, rows, width = out_ref.shape
    for which, (near, far) in enumerate(((gate_ref, gate_far_ref), (up_ref, up_far_ref))):
        product = jnp.dot(mine_ref[...], near[...], preferred_element_type=jnp.float32)
        product += jnp.dot(theirs_ref[...], far[...], preferred_element_type=jnp.float32)
        out_ref[:, which] = (scale * product).reshape(blocks, rows, width)


def forward(place, mine, theirs, gate_weight, up_weight, far, start, tile, blocks, scale):
    total, depth = mine.shape
    width = far[0].shape[1]
    rows = total // blocks
    whole = pl.BlockSpec((total, depth), lambda j, place: (0, 0))
    weight = pl.BlockSpec((depth, tile), lambda j, place: (0, place[0] + start // tile + j))
    return pl.pallas_call(
        functools.partial(forward_kernel, scale),
        out_shape=jax.ShapeDtypeStruct((blocks, 2, rows, width), jnp.float32),
        grid_spec=pltpu.PrefetchScalarGridSpec(
            num_scalar_prefetch=1,
            grid=(width // tile,),
            in_specs=[
                whole,
                whole,
                weight,
                weight,
                pl.BlockSpec((depth, tile), lambda j, place: (0, j)),
                pl.BlockSpec((depth, tile), lambda j, place: (0, j)),
            ],
            out_specs=pl.BlockSpec((blocks, 2, rows, tile), lambda j, place: (0, 0, 0, j)),
        ),
        compiler_params=pltpu.CompilerParams(vmem_limit_bytes=VMEM_LIMIT),
        cost_estimate=pl.CostEstimate(
            flops=8 * total * depth * width,
            bytes_accessed=8 * depth * width + 8 * total * width + 4 * total * depth,
            transcendentals=0,
        ),
    )(place, mine, theirs, gate_weight, up_weight, *far)


def gradient_kernel(batches, place_ref, features_ref, *refs):
    own, other, outs = refs[: 2 * batches], refs[2 * batches : 4 * batches], refs[-2:]

    def fill(acts):
        for which, out_ref in enumerate(outs):
            parts = []
            for batch in range(2):
                for act_ref in acts if batches == 1 else acts[2 * batch : 2 * batch + 2]:
                    blocks, _, rows, width = act_ref.shape
                    rows = rows * batches // 2
                    first = batch * rows if batches == 1 else 0
                    part = act_ref[:, which, first : first + rows]
                    parts.append(part.reshape(blocks * rows, width))
            out_ref[...] = jnp.dot(
                features_ref[...], jnp.concatenate(parts), preferred_element_type=jnp.float32
            )

    for which, acts in enumerate((own, other)):
        pl.when(pl.program_id(0) == which)(functools.partial(fill, acts))


def gradient(place, features, own, other, totals, columns, start, tile):
    depth, total = features.shape
    blocks, _, rows, width = own[0].shape
    tiles = width // tile
    shape = (blocks, 2, rows, tile)
    own_spec = pl.BlockSpec(
        shape, lambda i, j, place: (0, 0, 0, jnp.where(i == 0, j, tiles - 1))
    )
    other_spec = pl.BlockSpec(shape, lambda i, j, place: (0, 0, 0, jnp.where(i == 0, 0, j)))
    out_spec = pl.BlockSpec((depth, tile), lambda i, j, place: (0, place[i] + start // tile + j))
    out_shape = jax.ShapeDtypeStruct((depth, columns), jnp.float32)
    in_specs = [pl.BlockSpec((depth, total), lambda i, j, place: (0, 0))]
    in_specs += [own_spec] * len(own) + [other_spec] * len(other)
    in_specs += [pl.BlockSpec(memory_space=pl.ANY)] * len(totals)
    first = 2 + len(own) + len(other)
    return pl.pallas_call(
        functools.partial(gradient_kernel, len(own) // 2),
        out_shape=(out_shape, out_shape),
        grid_spec=pltpu.PrefetchScalarGridSpec(
            num_scalar_prefetch=1,
            grid=(2, tiles),
            in_specs=in_specs,
            out_specs=(out_spec, out_spec),
        ),
        input_output_aliases={first + i: i for i in range(len(totals))},
        compiler_params=pltpu.CompilerParams(vmem_limit_bytes=VMEM_LIMIT),
        cost_estimate=pl.CostEstimate(
            flops=8 * total * depth * width,
            bytes_accessed=(16 * depth + 8 * total) * width + 2 * total * depth,
            transcendentals=0,
        ),
    )(place, features, *own, *other, *totals)


def tie(value, *after):
    return lax.optimization_barrier((value, after))[0]


def cut(units, shares):
    edges = [round(units * sum(shares[:i]) / sum(shares)) for i in range(len(shares) + 1)]
    return [(a, b - a) for a, b in zip(edges, edges[1:]) if b > a]


def local(tokens, gate_weight, up_weight, grad_hidden):
    line = 4
    row, col, part = (lax.axis_index(name) for name in ("row", "col", "depth"))
    chip, core = col // 2, col % 2
    slab = grad_hidden.shape[1]
    rows = 2 * slab
    depth, columns = gate_weight.shape
    half = columns // 2
    share = half // 2
    tile = 256 if share % 256 == 0 else 128
    largest = depth * 2 * line * LARGEST_TOKEN * LARGEST_WEIGHT
    scale = 2.0 ** math.floor(math.log2(65504 / largest))

    swap = [(0, 1), (1, 0)]
    pairs = [(i, i ^ 1) for i in range(2 * line)]

    def between(hops):
        return [(2 * i + c, 2 * j + c) for i, j in hops for c in (0, 1)]

    inward, outward = between([(0, 1), (3, 2)]), between([(1, 0), (2, 3)])
    centre = between([(1, 2), (2, 1)])
    at_end = (chip == 0) | (chip == line - 1)
    at_far = 2 * chip >= line

    def send(value, route):
        return lax.ppermute(value, "col", route)

    def wide(value):
        return value.astype(jnp.float32)

    def add(*terms):
        return functools.reduce(jnp.add, map(wide, terms))

    def by(first, mine, theirs, axis):
        return jnp.where(
            first,
            jnp.concatenate([mine, theirs], axis=axis),
            jnp.concatenate([theirs, mine], axis=axis),
        )

    def columns_of(array, start, width):
        return lax.dynamic_slice_in_dim(array, start, width, array.ndim - 1)

    pieces = []
    for begin, count in cut(share // tile, SHARES):
        for batches in ((0, 1),) if pieces else ((0,), (1,)):
            pieces.append((batches, begin * tile, count * tile))
    last = len(pieces) - 1

    def exchange_weights(k, after):
        _, start, width = pieces[k]
        first = part * half + (1 - core) * share + start
        chosen = [
            columns_of(weight, first, width) for weight in tie((gate_weight, up_weight), after)
        ]
        return [send(value, pairs) for value in chosen]

    mine = tokens[0]
    over_row = lax.ppermute(mine, "row", swap)
    cotangent = grad_hidden[0]
    cotangent = jnp.stack(
        [
            columns_of(cotangent, part * half, half),
            lax.ppermute(columns_of(cotangent, (1 - part) * half, half), "depth", swap),
        ]
    )
    over_depth = lax.ppermute(mine, "depth", swap)
    over_both = lax.ppermute(over_row, "depth", swap)
    far_weights = {0: exchange_weights(0, ())}
    far_weights[1] = far_weights[0]
    first_tile = ((part * half + core * share) // tile).astype(jnp.int32).reshape(1)

    cotangent = by(
        core == 0,
        columns_of(cotangent, core * share, share),
        send(columns_of(cotangent, (1 - core) * share, share), pairs),
        1,
    )
    cotangent = jnp.stack([send(cotangent, inward), cotangent])

    def arrange(values):
        values = values.reshape(line, rows, depth)
        return jnp.where(at_far, values[::-1], values)

    def both_cores(values, after):
        values = arrange(tie(values, after))
        return values, send(values, pairs)

    def multiply(k, tokens, after):
        _, start, _ = pieces[k]
        mine, theirs = (value.reshape(-1, depth) for value in tie(tokens, after))
        weights = (gate_weight, up_weight, far_weights[k])
        return forward(first_tile, mine, theirs, *weights, start, tile, line, scale)

    features = [by(row == 0, mine, over_row, 1)]
    spread = [both_cores(features[0], ())]
    terms = {0: multiply(0, spread[0], ())}
    payload = terms[0].astype(WIRE)
    inner = {0: send(payload, inward)}

    over_depth, over_both = tie((over_depth, over_both), payload)
    features.append(by(row == 0, over_depth, over_both, 1))
    spread.append(both_cores(features[1], ()))
    far_weights[2] = exchange_weights(2, payload)
    both_rows = [jnp.stack(pair, axis=1) for pair in zip(*spread)]

    def activate(k, summed):
        batches, start, width = pieces[k]
        summed = (summed * (1.0 / scale)).reshape(2, 2, len(batches), rows, width)
        gate_sum, up_sum = summed[:, 0], summed[:, 1]
        squash = jax.nn.sigmoid(gate_sum)
        product = (gate_sum * squash * up_sum).astype(jnp.bfloat16)
        given = wide(cotangent[:, batches[0] : batches[-1] + 1, :, start : start + width])
        given = given * squash
        gate_act = given * up_sum * (1.0 + gate_sum * (1.0 - squash))
        up_act = given * gate_sum
        is_gate = lax.broadcasted_iota(jnp.int32, (2, 2, *given.shape[1:]), 1) == 0
        act = jnp.where(is_gate, gate_act[:, None], up_act[:, None]).astype(jnp.bfloat16)
        return product, act.reshape(2, 2, len(batches) * rows, width)

    def by_side(values):
        values = values.reshape(line, rows, depth)
        values = jnp.concatenate([values[:2], values[3:], values[2:3]])
        return values.reshape(-1, depth)

    turned = jnp.concatenate([by_side(tie(near, inner[0])) for near, _ in spread]).T

    def outer_hidden(ks):
        def joined(batch, which):
            chosen = [
                hidden[k][which, pieces[k][0].index(batch)] for k in ks if batch in pieces[k][0]
            ]
            return jnp.concatenate(chosen, axis=1)

        own = [joined(batch, 1) for batch in range(2)]
        theirs = send(jnp.stack([joined(batch, 0) for batch in range(2)]), outward)
        return jnp.where(at_end, theirs, jnp.stack(own))

    order = jnp.stack([core, 1 - core]).astype(jnp.int32) * (share // tile)
    got, act, hidden, near_out, far_out, across = {}, {}, {}, {}, {}, {}
    totals, waiting, hiddens = (), [], []
    outer = over_centre = inner[0]
    for t in range(last + 3):
        k = t
        if k <= last:
            if k < last:
                tokens = spread[1] if k == 0 else both_rows
                terms[k + 1] = multiply(k + 1, tokens, ())
                payload = terms[k + 1].astype(WIRE)
                inner[k + 1] = send(tie(payload, inner[k]), inward)
            if k + 3 <= last:
                far_weights[k + 3] = exchange_weights(k + 3, payload)
            mine = tie(terms[k], over_centre, totals)
            got[k] = over_centre = send(add(mine[2:], inner[k][2:]).astype(WIRE), centre)
        k = t - 1
        if 0 <= k <= last:
            hidden[k], act[k] = activate(k, add(terms[k][:2], inner[k][:2], got[k][::-1]))
            across[k] = over_centre = send(tie(act[k], over_centre), centre)
            near_out[k] = outer = send(tie(act[k], outer), outward)
            if k == last:
                hiddens.append(outer_hidden([last]))
        k = t - 2
        if 0 <= k <= last:
            mine = [
                jnp.where(at_end, near_out[k], act[k]),
                jnp.where(at_end, far_out[k], across[k]),
            ]
            waiting.append((mine, [send(value, pairs) for value in mine]))
            if pieces[k][0] != (0,):
                own, other = (sum(values, []) for values in zip(*waiting))
                totals = gradient(order, turned, own, other, totals, half, pieces[k][1], tile)
                waiting = []
        k = t - 1
        if 0 <= k <= last:
            far_out[k] = outer = send(tie(across[k], outer, totals), outward)
            if k == last - 1:
                hiddens.append(outer_hidden(range(last)))

    hidden = jnp.concatenate(hiddens, axis=2).reshape(2, 2, slab, share)
    mine = lax.dynamic_index_in_dim(hidden, core, 1, keepdims=False)
    theirs = lax.dynamic_index_in_dim(hidden, 1 - core, 1, keepdims=False)
    hidden = by(core == 0, mine, send(theirs, pairs), 2)
    hidden = by(part == 0, hidden[0], lax.ppermute(hidden[1], "depth", swap), 1)
    return (hidden[None], *totals)


def contract(picked, piece):
    return lax.dot_general(
        picked, piece, (((0,), (0,)), ((), ())), preferred_element_type=jnp.float32
    )


def local_any(tokens, gate_weight, up_weight, grad_hidden):
    features = lax.all_gather(tokens[0], "row", axis=1, tiled=True)
    columns = gate_weight.shape[1]
    picked = features
    gate_part = jnp.dot(picked, gate_weight, preferred_element_type=jnp.float32)
    up_part = jnp.dot(picked, up_weight, preferred_element_type=jnp.float32)
    summed = lax.psum_scatter(
        jnp.concatenate([gate_part, up_part], axis=1), "col", scatter_dimension=0, tiled=True
    )
    gate_sum = summed[:, :columns]
    up_sum = summed[:, columns:]
    squash = jax.nn.sigmoid(gate_sum)
    hidden = (gate_sum * squash * up_sum).astype(jnp.bfloat16)
    cotangent = grad_hidden[0].astype(jnp.float32)
    gate_act = (cotangent * up_sum * squash * (1.0 + gate_sum * (1.0 - squash))).astype(
        jnp.bfloat16
    )
    up_act = (cotangent * gate_sum * squash).astype(jnp.bfloat16)
    picked = features
    gate_total = contract(picked, lax.all_gather(gate_act, "col", axis=0, tiled=True))
    up_total = contract(picked, lax.all_gather(up_act, "col", axis=0, tiled=True))
    grad_gate, grad_up = (
        lax.psum_scatter(gate_total, "depth", scatter_dimension=1, tiled=True),
        lax.psum_scatter(up_total, "depth", scatter_dimension=1, tiled=True),
    )
    return (hidden[None], grad_gate, grad_up)


def solution(mesh):
    in_specs = (
        P("depth", None, ("col", "row")),
        P("col", "row"),
        P("col", "row"),
        P("depth", "col", "row"),
    )
    out_specs = (P("depth", "col", "row"), P("col", ("row", "depth")), P("col", ("row", "depth")))
    sizes = tuple(mesh.shape[name] for name in ("row", "col", "depth"))
    return jax.shard_map(
        local if sizes == (2, 8, 2) else local_any,
        mesh=mesh,
        in_specs=in_specs,
        out_specs=out_specs,
        check_vma=False,
    )
```

```python
import functools
import math

import jax
import jax.numpy as jnp
from jax import lax
from jax.experimental import pallas as pl
from jax.experimental.pallas import tpu as pltpu
from jax.sharding import PartitionSpec as P

WIRE = jnp.float16
LARGEST_TOKEN, LARGEST_WEIGHT = 6.0, 0.0625
VMEM_LIMIT = 48 * 2**20
LAST_SHARES = (2, 1)
SHARES = (4, 3)


def forward_kernel(scale, place_ref, *refs):
    tokens, weights, out_ref = refs[: len(refs) // 3], refs[len(refs) // 3 : -1], refs[-1]
    blocks, _, rows, width = out_ref.shape
    for which in range(2):
        product = sum(
            jnp.dot(rows_ref[...], weight_ref[...], preferred_element_type=jnp.float32)
            for rows_ref, weight_ref in zip(tokens, weights[which::2])
        )
        out_ref[:, which] = (scale * product).reshape(blocks, rows, width)


def forward(place, tokens, weights, start, width, tile, blocks, scale):
    total, depth = tokens[0].shape
    rows = total // blocks
    far = len(tokens) - 1
    in_specs = [pl.BlockSpec((total, depth), lambda j, place: (0, 0))] * len(tokens)
    in_specs += [
        pl.BlockSpec((depth, tile), lambda j, place: (0, place[0] + start // tile + j))
    ] * 2
    in_specs += [pl.BlockSpec((depth, tile), lambda j, place: (0, j))] * (2 * far)
    return pl.pallas_call(
        functools.partial(forward_kernel, scale),
        out_shape=jax.ShapeDtypeStruct((blocks, 2, rows, width), jnp.float32),
        grid_spec=pltpu.PrefetchScalarGridSpec(
            num_scalar_prefetch=1,
            grid=(width // tile,),
            in_specs=in_specs,
            out_specs=pl.BlockSpec((blocks, 2, rows, tile), lambda j, place: (0, 0, 0, j)),
        ),
        compiler_params=pltpu.CompilerParams(vmem_limit_bytes=VMEM_LIMIT),
        cost_estimate=pl.CostEstimate(
            flops=4 * (far + 1) * total * depth * width,
            bytes_accessed=(far + 1) * (4 * width + 2 * total) * depth + 8 * total * width,
            transcendentals=0,
        ),
    )(place, *tokens, *weights)


def gradient_kernel(batches, place_ref, features_ref, *refs):
    acts, outs = refs[:batches], refs[-2:]
    for which, out_ref in enumerate(outs):
        parts = []
        for act_ref in acts:
            blocks, _, _, rows, width = act_ref.shape
            rows = rows * batches // 2
            for i in range(2 // batches):
                part = act_ref[:, 0, which, i * rows : (i + 1) * rows]
                parts.append(part.reshape(blocks * rows, width))
        out_ref[...] = jnp.dot(
            features_ref[...], jnp.concatenate(parts), preferred_element_type=jnp.float32
        )


def gradient(place, features, acts, totals, columns, start, tile):
    depth, total = features.shape
    blocks, cores, _, rows, width = acts[0].shape
    act_spec = pl.BlockSpec((blocks, 1, 2, rows, tile), lambda i, j, place: (0, i, 0, 0, j))
    out_spec = pl.BlockSpec((depth, tile), lambda i, j, place: (0, place[i] + start // tile + j))
    out_shape = jax.ShapeDtypeStruct((depth, columns), jnp.float32)
    in_specs = [pl.BlockSpec((depth, total), lambda i, j, place: (0, 0))]
    in_specs += [act_spec] * len(acts)
    in_specs += [pl.BlockSpec(memory_space=pl.ANY)] * len(totals)
    return pl.pallas_call(
        functools.partial(gradient_kernel, len(acts)),
        out_shape=(out_shape, out_shape),
        grid_spec=pltpu.PrefetchScalarGridSpec(
            num_scalar_prefetch=1,
            grid=(cores, width // tile),
            in_specs=in_specs,
            out_specs=(out_spec, out_spec),
        ),
        input_output_aliases={2 + len(acts) + i: i for i in range(len(totals))},
        compiler_params=pltpu.CompilerParams(vmem_limit_bytes=VMEM_LIMIT),
        cost_estimate=pl.CostEstimate(
            flops=4 * cores * total * depth * width,
            bytes_accessed=cores * (8 * depth + 4 * total) * width + 2 * total * depth,
            transcendentals=0,
        ),
    )(place, features, *acts, *totals)


def tie(value, *after):
    return lax.optimization_barrier((value, after))[0]


def cut(units, shares):
    edges = [round(units * sum(shares[:i]) / sum(shares)) for i in range(len(shares) + 1)]
    return [(a, b - a) for a, b in zip(edges, edges[1:]) if b > a]


def local(tokens, gate_weight, up_weight, grad_hidden):
    line = 4
    row, col, part = (lax.axis_index(name) for name in ("row", "col", "depth"))
    place, core = col // 2, col % 2
    slab = grad_hidden.shape[1]
    rows = 2 * slab
    depth, columns = gate_weight.shape
    half = columns // 2
    share = half // 2
    tile = 256 if share % 256 == 0 else 128
    largest = depth * 2 * line * LARGEST_TOKEN * LARGEST_WEIGHT
    scale = 2.0 ** math.floor(math.log2(65504 / largest))

    swap = [(0, 1), (1, 0)]
    pairs = [(i, i ^ 1) for i in range(2 * line)]

    def between(hops):
        return [(2 * i + c, 2 * j + c) for i, j in hops for c in (0, 1)]

    inward, outward = between([(0, 1), (3, 2)]), between([(1, 0), (2, 3)])
    side, centre = inward + outward, between([(1, 2), (2, 1)])
    at_end = (place == 0) | (place == line - 1)
    at_far = 2 * place >= line

    def send(value, route):
        return lax.ppermute(value, "col", route)

    def wide(value):
        return value.astype(jnp.float32)

    def add(*terms):
        return functools.reduce(jnp.add, map(wide, terms))

    def by(first, mine, theirs, axis):
        return jnp.where(
            first,
            jnp.concatenate([mine, theirs], axis=axis),
            jnp.concatenate([theirs, mine], axis=axis),
        )

    def columns_of(array, start, width):
        return lax.dynamic_slice_in_dim(array, start, width, array.ndim - 1)

    pieces = []
    for begin, count in cut(share // tile, SHARES):
        for batches in ((0, 1),) if pieces else ((0,), (1,)):
            pieces.append((batches, begin * tile, count * tile))
    last = len(pieces) - 1

    def exchange_weights(k, after):
        _, start, width = pieces[k]
        first = part * half + (1 - core) * share + start
        return [
            send(tie(columns_of(weight, first, width), after), pairs)
            for weight in (gate_weight, up_weight)
        ]

    mine = tokens[0]
    over_row = lax.ppermute(mine, "row", swap)
    over_depth = lax.ppermute(mine, "depth", swap)
    over_both = lax.ppermute(over_row, "depth", swap)
    own_tile, other_tile = [
        ((part * half + owner * share) // tile).astype(jnp.int32).reshape(1)
        for owner in (core, 1 - core)
    ]

    def arrange(values):
        values = values.reshape(line, rows, depth)
        return jnp.where(at_far, values[::-1], values)

    def own_features(tokens, k, after):
        _, start, width = pieces[k]
        tokens = tie(tokens, after).reshape(-1, depth)
        weights = (gate_weight, up_weight)
        common = (weights, start, width, tile, line, scale)
        theirs = send(forward(other_tile, [tokens], *common).astype(WIRE), pairs)
        return forward(own_tile, [tie(tokens, theirs[:0])], *common), theirs

    def all_features(tokens, k, after):
        _, start, width = pieces[k]
        tokens = [value.reshape(-1, depth) for value in tie(tokens, after)]
        weights = (gate_weight, up_weight, *far_weights)
        return forward(own_tile, tokens, weights, start, width, tile, line, scale), None

    def take(terms, block):
        own, theirs = terms
        return own[block] if theirs is None else own[block] + wide(theirs[block])

    features = [arrange(by(row == 0, mine, over_row, 1))]
    terms = own_features(features[0], 0, ())
    payload = take(terms, 3).astype(WIRE)
    in_1 = send(payload, inward)

    over_depth, over_both = tie((over_depth, over_both), payload)
    features.append(arrange(by(row == 0, over_depth, over_both, 1)))
    far_weights = exchange_weights(2, in_1)
    far_features = [send(tie(value, in_1), pairs) for value in features]

    mine_cotangent, cotangent = tie((grad_hidden[0], grad_hidden[0]), in_1)
    cotangent = jnp.stack(
        [
            columns_of(mine_cotangent, part * half, half),
            lax.ppermute(columns_of(cotangent, (1 - part) * half, half), "depth", swap),
        ]
    )
    cotangent = by(
        core == 0,
        columns_of(cotangent, core * share, share),
        send(columns_of(cotangent, (1 - core) * share, share), pairs),
        1,
    )

    def activate(k, summed):
        batches, start, width = pieces[k]
        summed = (summed * (1.0 / scale)).reshape(2, len(batches), rows, width)
        gate_sum, up_sum = summed[0], summed[1]
        squash = jax.nn.sigmoid(gate_sum)
        product = (gate_sum * squash * up_sum).astype(jnp.bfloat16)
        for position, batch in enumerate(batches):
            hidden[batch].append(product[position])
        given = jnp.stack([wide(cotangent[b][:, start : start + width]) for b in batches])
        gate_act = given * up_sum * squash * (1.0 + gate_sum * (1.0 - squash))
        up_act = given * gate_sum * squash
        act = jnp.stack([gate_act, up_act]).astype(jnp.bfloat16)
        return act.reshape(2, len(batches) * rows, width)

    def merge(act, side_1, centre_1, out_2, share_2, out_3):
        blocks = jnp.stack(
            [
                jnp.where(at_end, act, side_1),
                jnp.where(at_end, side_1, act),
                jnp.where(at_end, out_2, centre_1),
                jnp.where(at_end, out_3, share_2),
            ]
        )
        return blocks, send(blocks, pairs)

    near_features = [tie(value, in_1) for value in features]
    turned, turned_in_place = [
        jnp.concatenate([value.reshape(-1, depth) for value in values]).T
        for values in (
            near_features,
            [jnp.where(at_far, value[::-1], value) for value in near_features],
        )
    ]

    def finish(gathered, totals, start):
        own, other = [value for value, _ in gathered], [value for _, value in gathered]
        for values, owner in ((own, core), (other, 1 - core)):
            where = (owner * (share // tile)).astype(jnp.int32).reshape(1)
            values = [value[:, None] for value in values]
            totals = gradient(where, turned, values, totals, half, start, tile)
        return totals

    hidden, totals, waiting = ([], []), (), []
    act = hops = None
    for k in range(-1, last):
        gathering = act is not None
        if gathering:
            side_1, centre_1 = send(act, side), send(act, centre)
        if hops is not None:
            waiting.append(merge(*hops))
            terms = tie(terms, waiting[-1][0])
        centre_2 = send(add(take(terms, 3), in_1).astype(WIRE), centre)
        in_2 = send(take(tie(terms, in_1), 2).astype(WIRE), inward)
        arrived = ()
        if gathering:
            side_1, centre_1 = tie((side_1, centre_1), in_1)
            out_2, share_2 = send(centre_1, outward), send(side_1, centre)
            arrived = (side_1, centre_1)
        following = None
        if k + 2 <= last:
            if k < 0:
                following = own_features(features[1], 1, in_1)
            else:
                tokens = [jnp.stack(values, axis=1) for values in (features, far_features)]
                following = all_features(tokens, k + 2, in_1)
        terms = tie(terms, arrived, following)
        near = add(take(terms, 2), in_2).astype(WIRE)
        swapped = jnp.where(at_end, take(terms, 1), add(take(terms, 0), centre_2)).astype(WIRE)
        centre_3, side_3 = send(near, centre), send(swapped, side)
        if following is not None:
            in_1 = send(take(tie(following, near, swapped), 3).astype(WIRE), inward)
        arrived = ()
        if gathering:
            out_2, share_2 = tie((out_2, share_2), in_2, centre_2)
            out_3 = send(share_2, outward)
            arrived = (out_2, share_2)
        terms = tie(terms, arrived)
        own = jnp.where(at_end, take(terms, 0), take(terms, 1))
        ready = activate(k + 1, add(own, side_3, centre_3))
        if gathering:
            hops = tie((act, side_1, centre_1, out_2, share_2, out_3), ready)
        act, terms = ready, following

    start, width = pieces[last][1:]
    gathered = []
    for begin, count in cut(width // tile, LAST_SHARES):
        chosen = act[:, :, begin * tile : (begin + count) * tile]
        chosen = lax.all_gather(tie(chosen, out_3), "col", axis=0)
        gathered.append((start + begin * tile, chosen.reshape(line, 2, *chosen.shape[1:])))
    waiting.append(merge(*hops))
    totals = finish(waiting, totals, pieces[0][1])
    places = jnp.array([0, share // tile], jnp.int32)
    for start, acts in gathered:
        totals = gradient(places, turned_in_place, [acts], totals, half, start, tile)

    hidden = jnp.stack([jnp.concatenate(parts, axis=1) for parts in hidden])
    hidden = hidden.reshape(2, 2, slab, share)
    mine = lax.dynamic_index_in_dim(hidden, core, 1, keepdims=False)
    theirs = lax.dynamic_index_in_dim(hidden, 1 - core, 1, keepdims=False)
    hidden = by(core == 0, mine, send(theirs, pairs), 2)
    hidden = by(part == 0, hidden[0], lax.ppermute(hidden[1], "depth", swap), 1)
    return (hidden[None], *totals)


def contract(picked, piece):
    return lax.dot_general(
        picked, piece, (((0,), (0,)), ((), ())), preferred_element_type=jnp.float32
    )


def local_any(tokens, gate_weight, up_weight, grad_hidden):
    features = lax.all_gather(tokens[0], "row", axis=1, tiled=True)
    columns = gate_weight.shape[1]
    picked = features
    gate_part = jnp.dot(picked, gate_weight, preferred_element_type=jnp.float32)
    up_part = jnp.dot(picked, up_weight, preferred_element_type=jnp.float32)
    summed = lax.psum_scatter(
        jnp.concatenate([gate_part, up_part], axis=1), "col", scatter_dimension=0, tiled=True
    )
    gate_sum = summed[:, :columns]
    up_sum = summed[:, columns:]
    squash = jax.nn.sigmoid(gate_sum)
    hidden = (gate_sum * squash * up_sum).astype(jnp.bfloat16)
    cotangent = grad_hidden[0].astype(jnp.float32)
    gate_act = (cotangent * up_sum * squash * (1.0 + gate_sum * (1.0 - squash))).astype(
        jnp.bfloat16
    )
    up_act = (cotangent * gate_sum * squash).astype(jnp.bfloat16)
    picked = features
    gate_total = contract(picked, lax.all_gather(gate_act, "col", axis=0, tiled=True))
    up_total = contract(picked, lax.all_gather(up_act, "col", axis=0, tiled=True))
    grad_gate, grad_up = (
        lax.psum_scatter(gate_total, "depth", scatter_dimension=1, tiled=True),
        lax.psum_scatter(up_total, "depth", scatter_dimension=1, tiled=True),
    )
    return (hidden[None], grad_gate, grad_up)


def solution(mesh):
    in_specs = (
        P("depth", None, ("col", "row")),
        P("col", "row"),
        P("col", "row"),
        P("depth", "col", "row"),
    )
    out_specs = (P("depth", "col", "row"), P("col", ("row", "depth")), P("col", ("row", "depth")))
    sizes = tuple(mesh.shape[name] for name in ("row", "col", "depth"))
    return jax.shard_map(
        local if sizes == (2, 8, 2) else local_any,
        mesh=mesh,
        in_specs=in_specs,
        out_specs=out_specs,
        check_vma=False,
    )
```

```python
import functools
import math

import jax
import jax.numpy as jnp
from jax import lax
from jax.experimental import pallas as pl
from jax.experimental.pallas import tpu as pltpu
from jax.sharding import PartitionSpec as P

WIRE = jnp.float16
LARGEST_TOKEN, LARGEST_WEIGHT = 6.0, 0.0625
VMEM_LIMIT = 48 * 2**20
NO_COST = pl.CostEstimate(flops=0, bytes_accessed=0, transcendentals=0)
SHARES = (5, 2)


def forward_kernel(scale, place_ref, *refs):
    tokens, weights, out_ref = refs[: len(refs) // 3], refs[len(refs) // 3 : -1], refs[-1]
    blocks, _, rows, width = out_ref.shape
    for which in range(2):
        product = sum(
            jnp.dot(
                rows_ref[...],
                weight_ref[...].reshape(weight_ref.shape[-2:]),
                preferred_element_type=jnp.float32,
            )
            for rows_ref, weight_ref in zip(tokens, weights[which::2])
        )
        out_ref[:, which] = (scale * product).reshape(blocks, rows, width)


def forward(place, tokens, weights, start, width, tile, blocks, scale):
    total, depth = tokens[0].shape
    rows = total // blocks
    far = len(tokens) - 1
    in_specs = [pl.BlockSpec((total, depth), lambda j, place: (0, 0))] * len(tokens)
    in_specs += [
        pl.BlockSpec((depth, tile), lambda j, place: (0, place[0] + start // tile + j))
    ] * 2
    in_specs += [
        pl.BlockSpec((1, depth, tile), lambda j, place, which=which: (which, 0, j))
        for which in range(2 * far)
    ]
    return pl.pallas_call(
        functools.partial(forward_kernel, scale),
        out_shape=jax.ShapeDtypeStruct((blocks, 2, rows, width), jnp.float32),
        grid_spec=pltpu.PrefetchScalarGridSpec(
            num_scalar_prefetch=1,
            grid=(width // tile,),
            in_specs=in_specs,
            out_specs=pl.BlockSpec((blocks, 2, rows, tile), lambda j, place: (0, 0, 0, j)),
        ),
        compiler_params=pltpu.CompilerParams(vmem_limit_bytes=VMEM_LIMIT),
        cost_estimate=NO_COST,
    )(place, *tokens, *weights)


def gradient_kernel(batches, place_ref, features_ref, *refs):
    acts, outs = refs[:batches], refs[-2:]
    for which, out_ref in enumerate(outs):
        parts = []
        for act_ref in acts:
            blocks, _, _, rows, width = act_ref.shape
            rows = rows * batches // 2
            for i in range(2 // batches):
                part = act_ref[:, 0, which, i * rows : (i + 1) * rows]
                parts.append(part.reshape(blocks * rows, width))
        out_ref[...] = jnp.dot(
            features_ref[...], jnp.concatenate(parts), preferred_element_type=jnp.float32
        )


def gradient(place, features, acts, totals, columns, start, tile):
    depth, total = features.shape
    blocks, cores, _, rows, width = acts[0].shape
    act_spec = pl.BlockSpec((blocks, 1, 2, rows, tile), lambda i, j, place: (0, i, 0, 0, j))
    out_spec = pl.BlockSpec((depth, tile), lambda i, j, place: (0, place[i] + start // tile + j))
    out_shape = jax.ShapeDtypeStruct((depth, columns), jnp.float32)
    in_specs = [pl.BlockSpec((depth, total), lambda i, j, place: (0, 0))]
    in_specs += [act_spec] * len(acts)
    in_specs += [pl.BlockSpec(memory_space=pl.ANY)] * len(totals)
    return pl.pallas_call(
        functools.partial(gradient_kernel, len(acts)),
        out_shape=(out_shape, out_shape),
        grid_spec=pltpu.PrefetchScalarGridSpec(
            num_scalar_prefetch=1,
            grid=(cores, width // tile),
            in_specs=in_specs,
            out_specs=(out_spec, out_spec),
        ),
        input_output_aliases={2 + len(acts) + i: i for i in range(len(totals))},
        compiler_params=pltpu.CompilerParams(vmem_limit_bytes=VMEM_LIMIT),
        cost_estimate=NO_COST,
    )(place, features, *acts, *totals)


def tie(value, *after):
    return lax.optimization_barrier((value, after))[0]


def cut(units, shares):
    edges = [round(units * sum(shares[:i]) / sum(shares)) for i in range(len(shares) + 1)]
    return [(a, b - a) for a, b in zip(edges, edges[1:]) if b > a]


def local(tokens, gate_weight, up_weight, grad_hidden):
    line = 4
    row, col, part = (lax.axis_index(name) for name in ("row", "col", "depth"))
    place, core = col // 2, col % 2
    slab = grad_hidden.shape[1]
    rows = 2 * slab
    depth, columns = gate_weight.shape
    half = columns // 2
    share = half // 2
    tile = 256 if share % 256 == 0 else 128
    largest = depth * 2 * line * LARGEST_TOKEN * LARGEST_WEIGHT
    scale = 2.0 ** math.floor(math.log2(65504 / largest))

    swap = [(0, 1), (1, 0)]
    pairs = [(i, i ^ 1) for i in range(2 * line)]

    def between(hops):
        return [(2 * i + c, 2 * j + c) for i, j in hops for c in (0, 1)]

    inward, outward = between([(0, 1), (3, 2)]), between([(1, 0), (2, 3)])
    side, centre = inward + outward, between([(1, 2), (2, 1)])
    at_end = (place == 0) | (place == line - 1)
    at_far = 2 * place >= line

    def send(value, route):
        return lax.ppermute(value, "col", route)

    def wide(value):
        return value.astype(jnp.float32)

    def add(*terms):
        return functools.reduce(jnp.add, map(wide, terms))

    def by(first, mine, theirs, axis):
        return jnp.where(
            first,
            jnp.concatenate([mine, theirs], axis=axis),
            jnp.concatenate([theirs, mine], axis=axis),
        )

    def columns_of(array, start, width):
        return lax.dynamic_slice_in_dim(array, start, width, array.ndim - 1)

    pieces = []
    for begin, count in cut(share // tile, SHARES):
        for batches in ((0, 1),) if pieces else ((0,), (1,)):
            pieces.append((batches, begin * tile, count * tile))
    last = len(pieces) - 1

    def exchange_weights(k, after):
        _, start, width = pieces[k]
        first = part * half + (1 - core) * share + start
        chosen = [
            columns_of(weight, first, width) for weight in tie((gate_weight, up_weight), after)
        ]
        return send(jnp.stack(chosen), pairs)

    mine = tokens[0]
    over_row = lax.ppermute(mine, "row", swap)
    over_depth = lax.ppermute(mine, "depth", swap)
    over_both = lax.ppermute(over_row, "depth", swap)
    own_tile, other_tile = [
        ((part * half + owner * share) // tile).astype(jnp.int32).reshape(1)
        for owner in (core, 1 - core)
    ]

    def arrange(values):
        values = values.reshape(line, rows, depth)
        return jnp.where(at_far, values[::-1], values)

    def own_features(tokens, k, after):
        _, start, width = pieces[k]
        tokens = tie(tokens, after).reshape(-1, depth)
        common = ((gate_weight, up_weight), start, width, tile, line, scale)
        payload = forward(other_tile, [tokens], *common).astype(WIRE)

        def own(after):
            return forward(own_tile, [tie(tokens, payload, after)], *common)

        return payload, own

    def all_features(tokens, k, after):
        _, start, width = pieces[k]
        tokens = [value.reshape(-1, depth) for value in tie(tokens, after)]
        weights = (gate_weight, up_weight, far_weights, far_weights)
        return forward(own_tile, tokens, weights, start, width, tile, line, scale), None

    def take(terms, block):
        own, theirs = terms
        return own[block] if theirs is None else own[block] + wide(theirs[block])

    features = [arrange(by(row == 0, mine, over_row, 1))]
    theirs, own = own_features(features[0], 0, ())
    terms = (own((over_depth, over_both)), send(theirs, pairs))
    payload = take(terms, 3).astype(WIRE)
    in_1 = send(payload, inward)

    over_depth, over_both = tie((over_depth, over_both), payload)
    features.append(arrange(by(row == 0, over_depth, over_both, 1)))
    theirs, own = own_features(features[1], 1, ())
    terms = tie(terms, theirs)

    def activate(k, summed):
        batches, start, width = pieces[k]
        summed = (summed * (1.0 / scale)).reshape(2, len(batches), rows, width)
        gate_sum, up_sum = summed[0], summed[1]
        squash = jax.nn.sigmoid(gate_sum)
        product = (gate_sum * squash * up_sum).astype(jnp.bfloat16)
        for position, batch in enumerate(batches):
            hidden[batch].append(product[position])
        given = jnp.stack([wide(cotangent[b][:, start : start + width]) for b in batches])
        gate_act = given * up_sum * squash * (1.0 + gate_sum * (1.0 - squash))
        up_act = given * gate_sum * squash
        act = jnp.stack([gate_act, up_act]).astype(jnp.bfloat16)
        return act.reshape(2, len(batches) * rows, width)

    def merge(act, side_1, centre_1, out_2, share_2, out_3):
        blocks = jnp.stack(
            [
                jnp.where(at_end, act, side_1),
                jnp.where(at_end, side_1, act),
                jnp.where(at_end, out_2, centre_1),
                jnp.where(at_end, out_3, share_2),
            ]
        )
        return blocks, send(blocks, pairs)

    turned = jnp.concatenate([tie(value, in_1).reshape(-1, depth) for value in features]).T

    def add_gradients(acts, owner, totals, start):
        where = (owner * (share // tile)).astype(jnp.int32).reshape(1)
        acts = [value[:, None] for value in acts]
        return gradient(where, turned, acts, totals, half, start, tile)

    hidden, totals, merged, products = ([], []), (), [], {}
    act = hops = None
    for k in range(-1, last + 1):
        adding, gathering = k < last, act is not None
        if gathering:
            side_1, centre_1 = send(act, side), send(act, centre)
        if hops is not None:
            merged.append(merge(*hops))
            if adding:
                terms = tie(terms, merged[-1][0])
            elif last > 1:
                side_1, centre_1 = tie((side_1, centre_1), merged[-1][0])
        before = ()
        if adding:
            far, near = add(take(terms, 3), in_1).astype(WIRE), take(tie(terms, in_1), 2)
            near = near.astype(WIRE)
            centre_2, in_2 = send(far, centre), send(near, inward)
            before = (in_1,)
        if gathering:
            side_1, centre_1 = tie((side_1, centre_1), before)
            out_2, share_2 = send(centre_1, outward), send(side_1, centre)
        if k < 0:
            products[1] = (own((far, near)), send(theirs, pairs))
            cotangent = tie(grad_hidden[0], far, near)
            theirs = lax.ppermute(columns_of(cotangent, (1 - part) * half, half), "depth", swap)
            cotangent = jnp.stack([columns_of(cotangent, part * half, half), theirs])
            terms = tie(terms, products[1][0], theirs)
        if k == 0:
            products[2] = all_features(tokens, 2, (side_1, centre_1))
            terms = tie(terms, products[2])
        if not adding:
            own_acts, other_acts = zip(*merged)
            totals = add_gradients(own_acts, core, (), pieces[0][1])
            share_2 = tie(share_2, totals)
        before = ()
        if adding:
            if gathering:
                terms = tie(terms, side_1, centre_1)
            near = add(take(terms, 2), in_2).astype(WIRE)
            swapped = jnp.where(at_end, take(terms, 1), add(take(terms, 0), centre_2))
            swapped = swapped.astype(WIRE)
            centre_3, side_3 = send(near, centre), send(swapped, side)
            if k + 2 <= last:
                payload = take(tie(products[k + 2], near, swapped), 3).astype(WIRE)
                in_1 = send(payload, inward)
            before = (in_2, centre_2)
        if k < 0:
            cotangent = tie(cotangent, near, swapped)
            cotangent = by(
                core == 0,
                columns_of(cotangent, core * share, share),
                send(columns_of(cotangent, (1 - core) * share, share), pairs),
                1,
            )
            far_weights = exchange_weights(2, (near, swapped))
            tokens = jnp.stack(tie(features, near, swapped), axis=1)
            tokens = (tokens, send(tokens, pairs))
            terms = tie(terms, turned)
        if gathering:
            out_2, share_2 = tie((out_2, share_2), before)
            out_3 = send(share_2, outward)
        if not adding:
            totals = add_gradients(other_acts, 1 - core, totals, pieces[0][1])
            out_3 = tie(out_3, totals)
        if adding:
            if gathering:
                terms = tie(terms, out_2, share_2)
            own = jnp.where(at_end, take(terms, 0), take(terms, 1))
            ready = activate(k + 1, add(own, side_3, centre_3))
            if gathering:
                hops = tie((act, side_1, centre_1, out_2, share_2, out_3), ready)
            act, terms = ready, products.get(k + 2)
        else:
            own_acts, other_acts = merge(act, side_1, centre_1, out_2, share_2, out_3)
    totals = add_gradients([own_acts], core, totals, pieces[last][1])
    totals = add_gradients([other_acts], 1 - core, totals, pieces[last][1])

    hidden = jnp.stack([jnp.concatenate(parts, axis=1) for parts in hidden])
    hidden = hidden.reshape(2, 2, slab, share)
    mine = lax.dynamic_index_in_dim(hidden, core, 1, keepdims=False)
    theirs = lax.dynamic_index_in_dim(hidden, 1 - core, 1, keepdims=False)
    hidden = by(core == 0, mine, send(theirs, pairs), 2)
    hidden = by(part == 0, hidden[0], lax.ppermute(hidden[1], "depth", swap), 1)
    return (hidden[None], *totals)


def contract(picked, piece):
    return lax.dot_general(
        picked, piece, (((0,), (0,)), ((), ())), preferred_element_type=jnp.float32
    )


def local_any(tokens, gate_weight, up_weight, grad_hidden):
    features = lax.all_gather(tokens[0], "row", axis=1, tiled=True)
    columns = gate_weight.shape[1]
    picked = features
    gate_part = jnp.dot(picked, gate_weight, preferred_element_type=jnp.float32)
    up_part = jnp.dot(picked, up_weight, preferred_element_type=jnp.float32)
    summed = lax.psum_scatter(
        jnp.concatenate([gate_part, up_part], axis=1), "col", scatter_dimension=0, tiled=True
    )
    gate_sum = summed[:, :columns]
    up_sum = summed[:, columns:]
    squash = jax.nn.sigmoid(gate_sum)
    hidden = (gate_sum * squash * up_sum).astype(jnp.bfloat16)
    cotangent = grad_hidden[0].astype(jnp.float32)
    gate_act = (cotangent * up_sum * squash * (1.0 + gate_sum * (1.0 - squash))).astype(
        jnp.bfloat16
    )
    up_act = (cotangent * gate_sum * squash).astype(jnp.bfloat16)
    picked = features
    gate_total = contract(picked, lax.all_gather(gate_act, "col", axis=0, tiled=True))
    up_total = contract(picked, lax.all_gather(up_act, "col", axis=0, tiled=True))
    grad_gate, grad_up = (
        lax.psum_scatter(gate_total, "depth", scatter_dimension=1, tiled=True),
        lax.psum_scatter(up_total, "depth", scatter_dimension=1, tiled=True),
    )
    return (hidden[None], grad_gate, grad_up)


def solution(mesh):
    in_specs = (
        P("depth", None, ("col", "row")),
        P("col", "row"),
        P("col", "row"),
        P("depth", "col", "row"),
    )
    out_specs = (P("depth", "col", "row"), P("col", ("row", "depth")), P("col", ("row", "depth")))
    sizes = tuple(mesh.shape[name] for name in ("row", "col", "depth"))
    return jax.shard_map(
        local if sizes == (2, 8, 2) else local_any,
        mesh=mesh,
        in_specs=in_specs,
        out_specs=out_specs,
        check_vma=False,
    )
```

```python
import functools
import math

import jax
import jax.numpy as jnp
from jax import lax
from jax.experimental import pallas as pl
from jax.experimental.pallas import tpu as pltpu
from jax.sharding import PartitionSpec as P

WIRE = jnp.float16
LARGEST_TOKEN, LARGEST_WEIGHT = 6.0, 0.0625
VMEM_LIMIT = 48 * 2**20
NO_COST = pl.CostEstimate(flops=0, bytes_accessed=0, transcendentals=0)
SHARES = (5, 2)


def forward_kernel(scale, place_ref, *refs):
    tokens, weights, out_ref = refs[: len(refs) // 3], refs[len(refs) // 3 : -1], refs[-1]
    blocks, _, rows, width = out_ref.shape
    for which in range(2):
        product = sum(
            jnp.dot(
                rows_ref[...],
                weight_ref[...].reshape(weight_ref.shape[-2:]),
                preferred_element_type=jnp.float32,
            )
            for rows_ref, weight_ref in zip(tokens, weights[which::2])
        )
        out_ref[:, which] = (scale * product).reshape(blocks, rows, width)


def forward(place, tokens, weights, start, width, tile, blocks, scale):
    total, depth = tokens[0].shape
    rows = total // blocks
    far = len(tokens) - 1
    in_specs = [pl.BlockSpec((total, depth), lambda j, place: (0, 0))] * len(tokens)
    in_specs += [
        pl.BlockSpec((depth, tile), lambda j, place: (0, place[0] + start // tile + j))
    ] * 2
    in_specs += [
        pl.BlockSpec((1, depth, tile), lambda j, place, which=which: (which, 0, j))
        for which in range(2 * far)
    ]
    return pl.pallas_call(
        functools.partial(forward_kernel, scale),
        out_shape=jax.ShapeDtypeStruct((blocks, 2, rows, width), jnp.float32),
        grid_spec=pltpu.PrefetchScalarGridSpec(
            num_scalar_prefetch=1,
            grid=(width // tile,),
            in_specs=in_specs,
            out_specs=pl.BlockSpec((blocks, 2, rows, tile), lambda j, place: (0, 0, 0, j)),
        ),
        compiler_params=pltpu.CompilerParams(vmem_limit_bytes=VMEM_LIMIT),
        cost_estimate=NO_COST,
    )(place, *tokens, *weights)


def gradient_kernel(batches, place_ref, features_ref, *refs):
    acts, outs = refs[:batches], refs[-2:]
    for which, out_ref in enumerate(outs):
        parts = []
        for act_ref in acts:
            blocks, _, _, rows, width = act_ref.shape
            rows = rows * batches // 2
            for i in range(2 // batches):
                part = act_ref[:, 0, which, i * rows : (i + 1) * rows]
                parts.append(part.reshape(blocks * rows, width))
        out_ref[...] = jnp.dot(
            features_ref[...], jnp.concatenate(parts), preferred_element_type=jnp.float32
        )


def gradient(place, features, acts, totals, columns, start, tile):
    depth, total = features.shape
    blocks, cores, _, rows, width = acts[0].shape
    act_spec = pl.BlockSpec((blocks, 1, 2, rows, tile), lambda i, j, place: (0, i, 0, 0, j))
    out_spec = pl.BlockSpec((depth, tile), lambda i, j, place: (0, place[i] + start // tile + j))
    out_shape = jax.ShapeDtypeStruct((depth, columns), jnp.float32)
    in_specs = [pl.BlockSpec((depth, total), lambda i, j, place: (0, 0))]
    in_specs += [act_spec] * len(acts)
    in_specs += [pl.BlockSpec(memory_space=pl.ANY)] * len(totals)
    return pl.pallas_call(
        functools.partial(gradient_kernel, len(acts)),
        out_shape=(out_shape, out_shape),
        grid_spec=pltpu.PrefetchScalarGridSpec(
            num_scalar_prefetch=1,
            grid=(cores, width // tile),
            in_specs=in_specs,
            out_specs=(out_spec, out_spec),
        ),
        input_output_aliases={2 + len(acts) + i: i for i in range(len(totals))},
        compiler_params=pltpu.CompilerParams(vmem_limit_bytes=VMEM_LIMIT),
        cost_estimate=NO_COST,
    )(place, features, *acts, *totals)


def tie(value, *after):
    return lax.optimization_barrier((value, after))[0]


def cut(units, shares):
    edges = [round(units * sum(shares[:i]) / sum(shares)) for i in range(len(shares) + 1)]
    return [(a, b - a) for a, b in zip(edges, edges[1:]) if b > a]


def local(tokens, gate_weight, up_weight, grad_hidden):
    line = 4
    row, col, part = (lax.axis_index(name) for name in ("row", "col", "depth"))
    place, core = col // 2, col % 2
    slab = grad_hidden.shape[1]
    rows = 2 * slab
    depth, columns = gate_weight.shape
    half = columns // 2
    share = half // 2
    tile = 256 if share % 256 == 0 else 128
    largest = depth * 2 * line * LARGEST_TOKEN * LARGEST_WEIGHT
    scale = 2.0 ** math.floor(math.log2(65504 / largest))

    swap = [(0, 1), (1, 0)]
    pairs = [(i, i ^ 1) for i in range(2 * line)]

    def between(hops):
        return [(2 * i + c, 2 * j + c) for i, j in hops for c in (0, 1)]

    inward, outward = between([(0, 1), (3, 2)]), between([(1, 0), (2, 3)])
    side, centre = inward + outward, between([(1, 2), (2, 1)])
    at_end = (place == 0) | (place == line - 1)
    at_far = 2 * place >= line

    def send(value, route):
        return lax.ppermute(value, "col", route)

    def wide(value):
        return value.astype(jnp.float32)

    def add(*terms):
        return functools.reduce(jnp.add, map(wide, terms))

    def by(first, mine, theirs, axis):
        return jnp.where(
            first,
            jnp.concatenate([mine, theirs], axis=axis),
            jnp.concatenate([theirs, mine], axis=axis),
        )

    def columns_of(array, start, width):
        return lax.dynamic_slice_in_dim(array, start, width, array.ndim - 1)

    pieces = []
    for begin, count in cut(share // tile, SHARES):
        for batches in ((0, 1),) if pieces else ((0,), (1,)):
            pieces.append((batches, begin * tile, count * tile))
    last = len(pieces) - 1

    def exchange_weights(k, after):
        _, start, width = pieces[k]
        first = part * half + (1 - core) * share + start
        chosen = [
            columns_of(weight, first, width) for weight in tie((gate_weight, up_weight), after)
        ]
        return send(jnp.stack(chosen), pairs)

    mine = tokens[0]
    over_row = lax.ppermute(mine, "row", swap)
    over_depth = lax.ppermute(mine, "depth", swap)
    over_both = lax.ppermute(over_row, "depth", swap)
    own_tile, other_tile = [
        ((part * half + owner * share) // tile).astype(jnp.int32).reshape(1)
        for owner in (core, 1 - core)
    ]

    def arrange(values):
        values = values.reshape(line, rows, depth)
        return jnp.where(at_far, values[::-1], values)

    def own_features(tokens, k, after):
        _, start, width = pieces[k]
        tokens = tie(tokens, after).reshape(-1, depth)
        common = ((gate_weight, up_weight), start, width, tile, line, scale)
        payload = forward(other_tile, [tokens], *common).astype(WIRE)

        def own(after):
            return forward(own_tile, [tie(tokens, payload, after)], *common)

        return payload, own

    def all_features(tokens, k, after):
        _, start, width = pieces[k]
        tokens = [value.reshape(-1, depth) for value in tie(tokens, after)]
        weights = (gate_weight, up_weight, far_weights, far_weights)
        return forward(own_tile, tokens, weights, start, width, tile, line, scale), None

    def take(terms, block):
        own, theirs = terms
        return own[block] if theirs is None else own[block] + wide(theirs[block])

    over_row = tie(over_row, over_depth)
    features = [arrange(by(row == 0, mine, over_row, 1))]
    theirs, own = own_features(features[0], 0, ())
    terms = (own(()), send(theirs, pairs))
    payload = take(terms, 3).astype(WIRE)
    in_1 = send(payload, inward)

    over_depth, over_both = tie((over_depth, over_both), payload)
    features.append(arrange(by(row == 0, over_depth, over_both, 1)))
    theirs, own = own_features(features[1], 1, ())
    terms = tie(terms, theirs)

    def activate(k, summed):
        batches, start, width = pieces[k]
        summed = (summed * (1.0 / scale)).reshape(2, len(batches), rows, width)
        gate_sum, up_sum = summed[0], summed[1]
        squash = jax.nn.sigmoid(gate_sum)
        product = (gate_sum * squash * up_sum).astype(jnp.bfloat16)
        for position, batch in enumerate(batches):
            hidden[batch].append(product[position])
        given = jnp.stack([wide(cotangent[b][:, start : start + width]) for b in batches])
        gate_act = given * up_sum * squash * (1.0 + gate_sum * (1.0 - squash))
        up_act = given * gate_sum * squash
        act = jnp.stack([gate_act, up_act]).astype(jnp.bfloat16)
        return act.reshape(2, len(batches) * rows, width)

    def merge(act, side_1, centre_1, out_2, share_2, out_3):
        blocks = jnp.stack(
            [
                jnp.where(at_end, act, side_1),
                jnp.where(at_end, side_1, act),
                jnp.where(at_end, out_2, centre_1),
                jnp.where(at_end, out_3, share_2),
            ]
        )
        return blocks, send(blocks, pairs)

    turned = jnp.concatenate([tie(value, in_1).reshape(-1, depth) for value in features]).T

    def add_gradients(acts, owner, totals, start):
        where = (owner * (share // tile)).astype(jnp.int32).reshape(1)
        acts = [value[:, None] for value in acts]
        return gradient(where, turned, acts, totals, half, start, tile)

    hidden, totals, merged, products = ([], []), (), [], {}
    act = hops = None
    for k in range(-1, last + 1):
        adding, gathering = k < last, act is not None
        if gathering:
            side_1, centre_1 = send(act, side), send(act, centre)
        if hops is not None:
            merged.append(merge(*hops))
            if adding:
                terms = tie(terms, merged[-1][0])
            elif last > 1:
                side_1, centre_1 = tie((side_1, centre_1), merged[-1][0])
        before = ()
        if adding:
            far, near = add(take(terms, 3), in_1).astype(WIRE), take(tie(terms, in_1), 2)
            near = near.astype(WIRE)
            centre_2, in_2 = send(far, centre), send(near, inward)
            before = (in_1,)
        if gathering:
            side_1, centre_1 = tie((side_1, centre_1), before)
            out_2, share_2 = send(centre_1, outward), send(side_1, centre)
        if k < 0:
            products[1] = (own((far, near)), send(theirs, pairs))
            cotangent = tie(grad_hidden[0], far, near)
            theirs = lax.ppermute(columns_of(cotangent, (1 - part) * half, half), "depth", swap)
            cotangent = jnp.stack([columns_of(cotangent, part * half, half), theirs])
            terms = tie(terms, products[1][0], theirs)
        if k == 0:
            products[2] = all_features(tokens, 2, (side_1, centre_1))
            terms = tie(terms, products[2])
        if not adding:
            hidden = jnp.stack([jnp.concatenate(parts, axis=1) for parts in hidden])
            hidden = hidden.reshape(2, 2, slab, share)
            mine = lax.dynamic_index_in_dim(hidden, core, 1, keepdims=False)
            theirs = lax.dynamic_index_in_dim(hidden, 1 - core, 1, keepdims=False)
            theirs = send(theirs, pairs)
            own_acts, other_acts = zip(*merged)
            totals = add_gradients(own_acts, core, (), pieces[0][1])
            share_2 = tie(share_2, totals, theirs)
            hidden = by(core == 0, mine, theirs, 2)
            theirs = lax.ppermute(tie(hidden[1], side_1), "depth", swap)
        before = ()
        if adding:
            if gathering:
                terms = tie(terms, side_1, centre_1)
            near = add(take(terms, 2), in_2).astype(WIRE)
            swapped = jnp.where(at_end, take(terms, 1), add(take(terms, 0), centre_2))
            swapped = swapped.astype(WIRE)
            centre_3, side_3 = send(near, centre), send(swapped, side)
            if k + 2 <= last:
                payload = take(tie(products[k + 2], near, swapped), 3).astype(WIRE)
                in_1 = send(payload, inward)
            before = (in_2, centre_2)
        if k < 0:
            cotangent = tie(cotangent, near, swapped)
            cotangent = by(
                core == 0,
                columns_of(cotangent, core * share, share),
                send(columns_of(cotangent, (1 - core) * share, share), pairs),
                1,
            )
            far_weights = exchange_weights(2, (near, swapped))
            tokens = jnp.stack(tie(features, near, swapped), axis=1)
            tokens = (tokens, send(tokens, pairs))
            terms = tie(terms, turned)
        if gathering:
            out_2, share_2 = tie((out_2, share_2), before)
            out_3 = send(share_2, outward)
        if not adding:
            totals = add_gradients(other_acts, 1 - core, totals, pieces[0][1])
            out_3 = tie(out_3, totals, theirs)
            hidden = by(part == 0, hidden[0], theirs, 1)
        if adding:
            if gathering:
                terms = tie(terms, out_2, share_2)
            own = jnp.where(at_end, take(terms, 0), take(terms, 1))
            ready = activate(k + 1, add(own, side_3, centre_3))
            if gathering:
                hops = tie((act, side_1, centre_1, out_2, share_2, out_3), ready)
            act, terms = ready, products.get(k + 2)
        else:
            own_acts, other_acts = merge(act, side_1, centre_1, out_2, share_2, out_3)
    totals = add_gradients([own_acts], core, totals, pieces[last][1])
    totals = add_gradients([other_acts], 1 - core, totals, pieces[last][1])

    return (hidden[None], *totals)


def contract(picked, piece):
    return lax.dot_general(
        picked, piece, (((0,), (0,)), ((), ())), preferred_element_type=jnp.float32
    )


def local_any(tokens, gate_weight, up_weight, grad_hidden):
    features = lax.all_gather(tokens[0], "row", axis=1, tiled=True)
    columns = gate_weight.shape[1]
    picked = features
    gate_part = jnp.dot(picked, gate_weight, preferred_element_type=jnp.float32)
    up_part = jnp.dot(picked, up_weight, preferred_element_type=jnp.float32)
    summed = lax.psum_scatter(
        jnp.concatenate([gate_part, up_part], axis=1), "col", scatter_dimension=0, tiled=True
    )
    gate_sum = summed[:, :columns]
    up_sum = summed[:, columns:]
    squash = jax.nn.sigmoid(gate_sum)
    hidden = (gate_sum * squash * up_sum).astype(jnp.bfloat16)
    cotangent = grad_hidden[0].astype(jnp.float32)
    gate_act = (cotangent * up_sum * squash * (1.0 + gate_sum * (1.0 - squash))).astype(
        jnp.bfloat16
    )
    up_act = (cotangent * gate_sum * squash).astype(jnp.bfloat16)
    picked = features
    gate_total = contract(picked, lax.all_gather(gate_act, "col", axis=0, tiled=True))
    up_total = contract(picked, lax.all_gather(up_act, "col", axis=0, tiled=True))
    grad_gate, grad_up = (
        lax.psum_scatter(gate_total, "depth", scatter_dimension=1, tiled=True),
        lax.psum_scatter(up_total, "depth", scatter_dimension=1, tiled=True),
    )
    return (hidden[None], grad_gate, grad_up)


def solution(mesh):
    in_specs = (
        P("depth", None, ("col", "row")),
        P("col", "row"),
        P("col", "row"),
        P("depth", "col", "row"),
    )
    out_specs = (P("depth", "col", "row"), P("col", ("row", "depth")), P("col", ("row", "depth")))
    sizes = tuple(mesh.shape[name] for name in ("row", "col", "depth"))
    return jax.shard_map(
        local if sizes == (2, 8, 2) else local_any,
        mesh=mesh,
        in_specs=in_specs,
        out_specs=out_specs,
        check_vma=False,
    )
```

```python
import functools
import math

import jax
import jax.numpy as jnp
from jax import lax
from jax.experimental import pallas as pl
from jax.experimental.pallas import tpu as pltpu
from jax.sharding import PartitionSpec as P

WIRE = jnp.float16
LARGEST_TOKEN, LARGEST_WEIGHT = 6.0, 0.0625
VMEM_LIMIT = 48 * 2**20
NO_COST = pl.CostEstimate(flops=0, bytes_accessed=0, transcendentals=0)
SHARES = (5, 2)


def forward_kernel(scale, place_ref, *refs):
    tokens, weights, out_ref = refs[: len(refs) // 3], refs[len(refs) // 3 : -1], refs[-1]
    blocks, _, rows, width = out_ref.shape
    for which in range(2):
        product = sum(
            jnp.dot(
                rows_ref[...],
                weight_ref[...].reshape(weight_ref.shape[-2:]),
                preferred_element_type=jnp.float32,
            )
            for rows_ref, weight_ref in zip(tokens, weights[which::2])
        )
        out_ref[:, which] = (scale * product).reshape(blocks, rows, width)


def forward(place, tokens, weights, start, width, tile, blocks, scale):
    total, depth = tokens[0].shape
    rows = total // blocks
    far = len(tokens) - 1
    in_specs = [pl.BlockSpec((total, depth), lambda j, place: (0, 0))] * len(tokens)
    in_specs += [
        pl.BlockSpec((depth, tile), lambda j, place: (0, place[0] + start // tile + j))
    ] * 2
    in_specs += [
        pl.BlockSpec((1, depth, tile), lambda j, place, which=which: (which, 0, j))
        for which in range(2 * far)
    ]
    return pl.pallas_call(
        functools.partial(forward_kernel, scale),
        out_shape=jax.ShapeDtypeStruct((blocks, 2, rows, width), jnp.float32),
        grid_spec=pltpu.PrefetchScalarGridSpec(
            num_scalar_prefetch=1,
            grid=(width // tile,),
            in_specs=in_specs,
            out_specs=pl.BlockSpec((blocks, 2, rows, tile), lambda j, place: (0, 0, 0, j)),
        ),
        compiler_params=pltpu.CompilerParams(vmem_limit_bytes=VMEM_LIMIT),
        cost_estimate=NO_COST,
    )(place, *tokens, *weights)


def gradient_kernel(batches, place_ref, features_ref, *refs):
    acts, outs = refs[:batches], refs[-2:]
    for which, out_ref in enumerate(outs):
        parts = []
        for act_ref in acts:
            blocks, _, _, rows, width = act_ref.shape
            rows = rows * batches // 2
            for i in range(2 // batches):
                part = act_ref[:, 0, which, i * rows : (i + 1) * rows]
                parts.append(part.reshape(blocks * rows, width))
        out_ref[...] = jnp.dot(
            features_ref[...], jnp.concatenate(parts), preferred_element_type=jnp.float32
        )


def gradient(place, features, acts, totals, columns, start, tile):
    depth, total = features.shape
    blocks, cores, _, rows, width = acts[0].shape
    act_spec = pl.BlockSpec((blocks, 1, 2, rows, tile), lambda i, j, place: (0, i, 0, 0, j))
    out_spec = pl.BlockSpec((depth, tile), lambda i, j, place: (0, place[i] + start // tile + j))
    out_shape = jax.ShapeDtypeStruct((depth, columns), jnp.float32)
    in_specs = [pl.BlockSpec((depth, total), lambda i, j, place: (0, 0))]
    in_specs += [act_spec] * len(acts)
    in_specs += [pl.BlockSpec(memory_space=pl.ANY)] * len(totals)
    return pl.pallas_call(
        functools.partial(gradient_kernel, len(acts)),
        out_shape=(out_shape, out_shape),
        grid_spec=pltpu.PrefetchScalarGridSpec(
            num_scalar_prefetch=1,
            grid=(cores, width // tile),
            in_specs=in_specs,
            out_specs=(out_spec, out_spec),
        ),
        input_output_aliases={2 + len(acts) + i: i for i in range(len(totals))},
        compiler_params=pltpu.CompilerParams(vmem_limit_bytes=VMEM_LIMIT),
        cost_estimate=NO_COST,
    )(place, features, *acts, *totals)


def tie(value, *after):
    return lax.optimization_barrier((value, after))[0]


def cut(units, shares):
    edges = [round(units * sum(shares[:i]) / sum(shares)) for i in range(len(shares) + 1)]
    return [(a, b - a) for a, b in zip(edges, edges[1:]) if b > a]


def local(tokens, gate_weight, up_weight, grad_hidden):
    line = 4
    row, col, part = (lax.axis_index(name) for name in ("row", "col", "depth"))
    place, core = col // 2, col % 2
    slab = grad_hidden.shape[1]
    rows = 2 * slab
    depth, columns = gate_weight.shape
    half = columns // 2
    share = half // 2
    tile = 256 if share % 256 == 0 else 128
    largest = depth * 2 * line * LARGEST_TOKEN * LARGEST_WEIGHT
    scale = 2.0 ** math.floor(math.log2(65504 / largest))

    swap = [(0, 1), (1, 0)]
    pairs = [(i, i ^ 1) for i in range(2 * line)]

    def between(hops):
        return [(2 * i + c, 2 * j + c) for i, j in hops for c in (0, 1)]

    inward, outward = between([(0, 1), (3, 2)]), between([(1, 0), (2, 3)])
    side, centre = inward + outward, between([(1, 2), (2, 1)])
    at_end = (place == 0) | (place == line - 1)
    at_far = 2 * place >= line

    def send(value, route):
        return lax.ppermute(value, "col", route)

    def wide(value):
        return value.astype(jnp.float32)

    def add(*terms):
        return functools.reduce(jnp.add, map(wide, terms))

    def by(first, mine, theirs, axis):
        return jnp.where(
            first,
            jnp.concatenate([mine, theirs], axis=axis),
            jnp.concatenate([theirs, mine], axis=axis),
        )

    def columns_of(array, start, width):
        return lax.dynamic_slice_in_dim(array, start, width, array.ndim - 1)

    pieces = []
    for begin, count in cut(share // tile, SHARES):
        for batches in ((0, 1),) if pieces else ((0,), (1,)):
            pieces.append((batches, begin * tile, count * tile))
    last = len(pieces) - 1

    def exchange_weights(k, after):
        _, start, width = pieces[k]
        first = part * half + (1 - core) * share + start
        chosen = [
            columns_of(weight, first, width) for weight in tie((gate_weight, up_weight), after)
        ]
        return send(jnp.stack(chosen), pairs)

    mine = tokens[0]
    over_row = lax.ppermute(mine, "row", swap)
    over_depth = lax.ppermute(mine, "depth", swap)
    over_both = lax.ppermute(over_row, "depth", swap)
    own_tile, other_tile = [
        ((part * half + owner * share) // tile).astype(jnp.int32).reshape(1)
        for owner in (core, 1 - core)
    ]

    def arrange(values):
        values = values.reshape(line, rows, depth)
        return jnp.where(at_far, values[::-1], values)

    def own_features(tokens, k, after, wire):
        _, start, width = pieces[k]
        tokens = tie(tokens, after).reshape(-1, depth)
        common = ((gate_weight, up_weight), start, width, tile, line, scale)
        payload = forward(other_tile, [tokens], *common).astype(wire)

        def own(after):
            return forward(own_tile, [tie(tokens, payload, after)], *common)

        return payload, own

    def all_features(tokens, k, after):
        _, start, width = pieces[k]
        tokens = [value.reshape(-1, depth) for value in tie(tokens, after)]
        weights = (gate_weight, up_weight, far_weights, far_weights)
        return forward(own_tile, tokens, weights, start, width, tile, line, scale), None

    def take(terms, block):
        own, theirs = terms
        return own[block] if theirs is None else own[block] + wide(theirs[block])

    over_row = tie(over_row, over_depth)
    features = [arrange(by(row == 0, mine, over_row, 1))]
    theirs, own = own_features(features[0], 0, (), WIRE)
    cotangent = tie(grad_hidden[0], features[0])
    cotangent = jnp.stack(
        [
            columns_of(cotangent, part * half, half),
            lax.ppermute(columns_of(cotangent, (1 - part) * half, half), "depth", swap),
        ]
    )
    terms = tie((own(()), send(theirs, pairs)), cotangent)
    payload = take(terms, 3).astype(WIRE)
    in_1 = send(payload, inward)

    over_depth, over_both = tie((over_depth, over_both), payload)
    features.append(arrange(by(row == 0, over_depth, over_both, 1)))
    theirs, own = own_features(features[1], 1, (), WIRE)
    terms = tie(terms, theirs)

    def activate(k, summed):
        batches, start, width = pieces[k]
        summed = (summed * (1.0 / scale)).reshape(2, len(batches), rows, width)
        gate_sum, up_sum = summed[0], summed[1]
        squash = jax.nn.sigmoid(gate_sum)
        product = (gate_sum * squash * up_sum).astype(jnp.bfloat16)
        for position, batch in enumerate(batches):
            hidden[batch].append(product[position])
        given = jnp.stack([wide(cotangent[b][:, start : start + width]) for b in batches])
        gate_act = given * up_sum * squash * (1.0 + gate_sum * (1.0 - squash))
        up_act = given * gate_sum * squash
        act = jnp.stack([gate_act, up_act]).astype(jnp.bfloat16)
        return act.reshape(2, len(batches) * rows, width)

    def merge(act, side_1, centre_1, out_2, share_2, out_3):
        blocks = jnp.stack(
            [
                jnp.where(at_end, act, side_1),
                jnp.where(at_end, side_1, act),
                jnp.where(at_end, out_2, centre_1),
                jnp.where(at_end, out_3, share_2),
            ]
        )
        return blocks, send(blocks, pairs)

    def add_gradients(acts, owner, totals, start):
        where = (owner * (share // tile)).astype(jnp.int32).reshape(1)
        acts = [value[:, None] for value in acts]
        return gradient(where, turned, acts, totals, half, start, tile)

    hidden, totals, merged, products = ([], []), (), [], {}
    act = hops = None
    for k in range(-1, last + 1):
        adding, gathering = k < last, act is not None
        if gathering:
            side_1, centre_1 = send(act, side), send(act, centre)
        if adding:
            if hops is not None:
                merged.append(merge(*hops))
                terms = tie(terms, merged[-1][0])
            if k == 0:
                products[2] = all_features(tokens, 2, act)
                terms = tie(terms, products[2])
            far, near = add(take(terms, 3), in_1).astype(WIRE), take(tie(terms, in_1), 2)
            near = near.astype(WIRE)
            centre_2, in_2 = send(far, centre), send(near, inward)
            before = (in_1,)
        else:
            hidden = jnp.stack([jnp.concatenate(parts, axis=1) for parts in hidden])
            hidden = hidden.reshape(2, 2, slab, share)
            mine = lax.dynamic_index_in_dim(hidden, core, 1, keepdims=False)
            theirs = lax.dynamic_index_in_dim(hidden, 1 - core, 1, keepdims=False)
            theirs = send(theirs, pairs)
            before = (theirs,)
        if gathering:
            side_1, centre_1 = tie((side_1, centre_1), before)
            out_2, share_2 = send(centre_1, outward), send(side_1, centre)
        if k < 0:
            products[1] = (own((far, near)), send(theirs, pairs))
            terms = tie(terms, products[1])
        if not adding:
            merged.append(merge(*tie(hops, side_1, centre_1)))
            own_acts, other_acts = zip(*merged)
            totals = add_gradients(own_acts, core, (), pieces[0][1])
            share_2 = tie(share_2, totals)
            hidden = by(core == 0, mine, theirs, 2)
            theirs = lax.ppermute(tie(hidden[1], side_1), "depth", swap)
        if adding:
            if gathering:
                terms = tie(terms, side_1, centre_1)
            near = add(take(terms, 2), in_2).astype(WIRE)
            swapped = jnp.where(at_end, take(terms, 1), add(take(terms, 0), centre_2))
            swapped = swapped.astype(WIRE)
            centre_3, side_3 = send(near, centre), send(swapped, side)
            if k + 2 <= last:
                payload = take(tie(products[k + 2], near, swapped), 3).astype(WIRE)
                in_1 = send(payload, inward)
            before = (in_2, centre_2)
        if k < 0:
            cotangent = tie(cotangent, near, swapped)
            cotangent = by(
                core == 0,
                columns_of(cotangent, core * share, share),
                send(columns_of(cotangent, (1 - core) * share, share), pairs),
                1,
            )
            far_weights = exchange_weights(2, (near, swapped))
            tokens = jnp.stack(tie(features, near, swapped), axis=1)
            tokens = (tokens, send(tokens, pairs))
        if k == 0:
            turned = [value.reshape(-1, depth) for value in tie(features, near, swapped)]
            turned = jnp.concatenate(turned).T
            terms = tie(terms, turned)
        if gathering:
            out_2, share_2 = tie((out_2, share_2), before)
            out_3 = send(share_2, outward)
        if adding:
            if gathering:
                terms = tie(terms, out_2, share_2)
            own_sum = jnp.where(at_end, take(terms, 0), take(terms, 1))
            ready = activate(k + 1, add(own_sum, side_3, centre_3))
            if gathering:
                hops = tie((act, side_1, centre_1, out_2, share_2, out_3), ready)
            act, terms = ready, products.get(k + 2)
        else:
            totals = add_gradients(other_acts, 1 - core, totals, pieces[0][1])
            hidden = by(part == 0, hidden[0], theirs, 1)
            out_3 = tie(out_3, totals, hidden)
            own_acts, other_acts = merge(act, side_1, centre_1, out_2, share_2, out_3)
    totals = add_gradients([own_acts], core, totals, pieces[last][1])
    totals = add_gradients([other_acts], 1 - core, totals, pieces[last][1])

    return (hidden[None], *totals)


def contract(picked, piece):
    return lax.dot_general(
        picked, piece, (((0,), (0,)), ((), ())), preferred_element_type=jnp.float32
    )


def local_any(tokens, gate_weight, up_weight, grad_hidden):
    features = lax.all_gather(tokens[0], "row", axis=1, tiled=True)
    columns = gate_weight.shape[1]
    picked = features
    gate_part = jnp.dot(picked, gate_weight, preferred_element_type=jnp.float32)
    up_part = jnp.dot(picked, up_weight, preferred_element_type=jnp.float32)
    summed = lax.psum_scatter(
        jnp.concatenate([gate_part, up_part], axis=1), "col", scatter_dimension=0, tiled=True
    )
    gate_sum = summed[:, :columns]
    up_sum = summed[:, columns:]
    squash = jax.nn.sigmoid(gate_sum)
    hidden = (gate_sum * squash * up_sum).astype(jnp.bfloat16)
    cotangent = grad_hidden[0].astype(jnp.float32)
    gate_act = (cotangent * up_sum * squash * (1.0 + gate_sum * (1.0 - squash))).astype(
        jnp.bfloat16
    )
    up_act = (cotangent * gate_sum * squash).astype(jnp.bfloat16)
    picked = features
    gate_total = contract(picked, lax.all_gather(gate_act, "col", axis=0, tiled=True))
    up_total = contract(picked, lax.all_gather(up_act, "col", axis=0, tiled=True))
    grad_gate, grad_up = (
        lax.psum_scatter(gate_total, "depth", scatter_dimension=1, tiled=True),
        lax.psum_scatter(up_total, "depth", scatter_dimension=1, tiled=True),
    )
    return (hidden[None], grad_gate, grad_up)


def solution(mesh):
    in_specs = (
        P("depth", None, ("col", "row")),
        P("col", "row"),
        P("col", "row"),
        P("depth", "col", "row"),
    )
    out_specs = (P("depth", "col", "row"), P("col", ("row", "depth")), P("col", ("row", "depth")))
    sizes = tuple(mesh.shape[name] for name in ("row", "col", "depth"))
    return jax.shard_map(
        local if sizes == (2, 8, 2) else local_any,
        mesh=mesh,
        in_specs=in_specs,
        out_specs=out_specs,
        check_vma=False,
    )
```

```python
import functools
import math

import jax
import jax.numpy as jnp
from jax import lax
from jax.experimental import pallas as pl
from jax.experimental.pallas import tpu as pltpu
from jax.sharding import PartitionSpec as P

WIRE = jnp.float16
LARGEST_TOKEN, LARGEST_WEIGHT = 6.0, 0.0625
VMEM_LIMIT = 48 * 2**20
NO_COST = pl.CostEstimate(flops=0, bytes_accessed=0, transcendentals=0)
SHARES = (5, 2)


def forward_kernel(scale, place_ref, *refs):
    tokens, weights, out_ref = refs[: len(refs) // 3], refs[len(refs) // 3 : -1], refs[-1]
    blocks, _, rows, width = out_ref.shape
    for which in range(2):
        product = sum(
            jnp.dot(
                rows_ref[...],
                weight_ref[...].reshape(weight_ref.shape[-2:]),
                preferred_element_type=jnp.float32,
            )
            for rows_ref, weight_ref in zip(tokens, weights[which::2])
        )
        out_ref[:, which] = (scale * product).reshape(blocks, rows, width)


def forward(place, tokens, weights, start, width, tile, blocks, scale):
    total, depth = tokens[0].shape
    rows = total // blocks
    far = len(tokens) - 1
    in_specs = [pl.BlockSpec((total, depth), lambda j, place: (0, 0))] * len(tokens)
    in_specs += [
        pl.BlockSpec((depth, tile), lambda j, place: (0, place[0] + start // tile + j))
    ] * 2
    in_specs += [
        pl.BlockSpec((1, depth, tile), lambda j, place, which=which: (which, 0, j))
        for which in range(2 * far)
    ]
    return pl.pallas_call(
        functools.partial(forward_kernel, scale),
        out_shape=jax.ShapeDtypeStruct((blocks, 2, rows, width), jnp.float32),
        grid_spec=pltpu.PrefetchScalarGridSpec(
            num_scalar_prefetch=1,
            grid=(width // tile,),
            in_specs=in_specs,
            out_specs=pl.BlockSpec((blocks, 2, rows, tile), lambda j, place: (0, 0, 0, j)),
        ),
        compiler_params=pltpu.CompilerParams(vmem_limit_bytes=VMEM_LIMIT),
        cost_estimate=NO_COST,
    )(place, *tokens, *weights)


def gradient_kernel(batches, place_ref, features_ref, *refs):
    acts, outs = refs[:batches], refs[-2:]
    for which, out_ref in enumerate(outs):
        parts = []
        for act_ref in acts:
            blocks, _, _, rows, width = act_ref.shape
            rows = rows * batches // 2
            for i in range(2 // batches):
                part = act_ref[:, 0, which, i * rows : (i + 1) * rows]
                parts.append(part.reshape(blocks * rows, width))
        out_ref[...] = jnp.dot(
            features_ref[...], jnp.concatenate(parts), preferred_element_type=jnp.float32
        )


def gradient(place, features, acts, totals, columns, start, tile):
    depth, total = features.shape
    blocks, cores, _, rows, width = acts[0].shape
    act_spec = pl.BlockSpec((blocks, 1, 2, rows, tile), lambda i, j, place: (0, i, 0, 0, j))
    out_spec = pl.BlockSpec((depth, tile), lambda i, j, place: (0, place[i] + start // tile + j))
    out_shape = jax.ShapeDtypeStruct((depth, columns), jnp.float32)
    in_specs = [pl.BlockSpec((depth, total), lambda i, j, place: (0, 0))]
    in_specs += [act_spec] * len(acts)
    in_specs += [pl.BlockSpec(memory_space=pl.ANY)] * len(totals)
    return pl.pallas_call(
        functools.partial(gradient_kernel, len(acts)),
        out_shape=(out_shape, out_shape),
        grid_spec=pltpu.PrefetchScalarGridSpec(
            num_scalar_prefetch=1,
            grid=(cores, width // tile),
            in_specs=in_specs,
            out_specs=(out_spec, out_spec),
        ),
        input_output_aliases={2 + len(acts) + i: i for i in range(len(totals))},
        compiler_params=pltpu.CompilerParams(vmem_limit_bytes=VMEM_LIMIT),
        cost_estimate=pl.CostEstimate(
            flops=4 * cores * total * depth * width,
            bytes_accessed=cores * (8 * depth + 4 * total) * width + 2 * total * depth,
            transcendentals=0,
        ),
    )(place, features, *acts, *totals)


def gather_kernel(at_end_ref, act, side_1, centre_1, out_2, share_2, out_3, out_ref):
    def fill(*blocks):
        for block, block_ref in enumerate(blocks):
            out_ref[block] = block_ref[...]

    pl.when(at_end_ref[0] == 1)(functools.partial(fill, act, side_1, out_2, out_3))
    pl.when(at_end_ref[0] == 0)(functools.partial(fill, side_1, act, centre_1, share_2))


def gather_blocks(at_end, *hops):
    _, rows, width = hops[0].shape
    spec = pl.BlockSpec((1, rows, width), lambda i, at_end: (i, 0, 0))
    return pl.pallas_call(
        gather_kernel,
        out_shape=jax.ShapeDtypeStruct((4, 2, rows, width), hops[0].dtype),
        grid_spec=pltpu.PrefetchScalarGridSpec(
            num_scalar_prefetch=1,
            grid=(2,),
            in_specs=[spec] * len(hops),
            out_specs=pl.BlockSpec((4, 1, rows, width), lambda i, at_end: (0, i, 0, 0)),
        ),
        compiler_params=pltpu.CompilerParams(vmem_limit_bytes=VMEM_LIMIT),
        cost_estimate=NO_COST,
    )(at_end, *hops)


def tie(value, *after):
    return lax.optimization_barrier((value, after))[0]


def cut(units, shares):
    edges = [round(units * sum(shares[:i]) / sum(shares)) for i in range(len(shares) + 1)]
    return [(a, b - a) for a, b in zip(edges, edges[1:]) if b > a]


def local(tokens, gate_weight, up_weight, grad_hidden):
    line = 4
    row, col, part = (lax.axis_index(name) for name in ("row", "col", "depth"))
    place, core = col // 2, col % 2
    slab = grad_hidden.shape[1]
    rows = 2 * slab
    depth, columns = gate_weight.shape
    half = columns // 2
    share = half // 2
    tile = 256 if share % 256 == 0 else 128
    largest = depth * 2 * line * LARGEST_TOKEN * LARGEST_WEIGHT
    scale = 2.0 ** math.floor(math.log2(65504 / largest))

    swap = [(0, 1), (1, 0)]
    pairs = [(i, i ^ 1) for i in range(2 * line)]

    def between(hops):
        return [(2 * i + c, 2 * j + c) for i, j in hops for c in (0, 1)]

    inward, outward = between([(0, 1), (3, 2)]), between([(1, 0), (2, 3)])
    side, centre = inward + outward, between([(1, 2), (2, 1)])
    at_end = (place == 0) | (place == line - 1)
    at_far = 2 * place >= line

    def send(value, route):
        return lax.ppermute(value, "col", route)

    def wide(value):
        return value.astype(jnp.float32)

    def add(*terms):
        return functools.reduce(jnp.add, map(wide, terms))

    def by(first, mine, theirs, axis):
        return jnp.where(
            first,
            jnp.concatenate([mine, theirs], axis=axis),
            jnp.concatenate([theirs, mine], axis=axis),
        )

    def columns_of(array, start, width):
        return lax.dynamic_slice_in_dim(array, start, width, array.ndim - 1)

    pieces = []
    for begin, count in cut(share // tile, SHARES):
        for batches in ((0, 1),) if pieces else ((0,), (1,)):
            pieces.append((batches, begin * tile, count * tile))
    last = len(pieces) - 1

    def exchange_weights(k, after):
        _, start, width = pieces[k]
        first = part * half + (1 - core) * share + start
        chosen = [
            columns_of(weight, first, width) for weight in tie((gate_weight, up_weight), after)
        ]
        return send(jnp.stack(chosen), pairs)

    mine = tokens[0]
    over_row = lax.ppermute(mine, "row", swap)
    over_depth = lax.ppermute(mine, "depth", swap)
    over_both = lax.ppermute(over_row, "depth", swap)
    own_tile, other_tile = [
        ((part * half + owner * share) // tile).astype(jnp.int32).reshape(1)
        for owner in (core, 1 - core)
    ]

    def arrange(values):
        values = values.reshape(line, rows, depth)
        return jnp.where(at_far, values[::-1], values)

    def own_features(tokens, k, after, wire):
        _, start, width = pieces[k]
        tokens = tie(tokens, after).reshape(-1, depth)
        common = ((gate_weight, up_weight), start, width, tile, line, scale)
        payload = forward(other_tile, [tokens], *common).astype(wire)

        def own(after):
            return forward(own_tile, [tie(tokens, payload, after)], *common)

        return payload, own

    def all_features(tokens, k, after):
        _, start, width = pieces[k]
        tokens = [value.reshape(-1, depth) for value in tie(tokens, after)]
        weights = (gate_weight, up_weight, far_weights, far_weights)
        return forward(own_tile, tokens, weights, start, width, tile, line, scale), None

    def take(terms, block):
        own, theirs = terms
        return own[block] if theirs is None else own[block] + wide(theirs[block])

    cotangent = grad_hidden[0]
    cotangent = (
        columns_of(cotangent, part * half, half),
        lax.ppermute(columns_of(cotangent, (1 - part) * half, half), "depth", swap),
    )
    over_row = tie(over_row, over_depth, cotangent)
    features = [arrange(by(row == 0, mine, over_row, 1))]
    theirs, own = own_features(features[0], 0, (), WIRE)
    terms = (own(()), send(theirs, pairs))
    payload = take(terms, 3).astype(WIRE)
    in_1 = send(payload, inward)

    over_depth, over_both = tie((over_depth, over_both), payload)
    features.append(arrange(by(row == 0, over_depth, over_both, 1)))
    theirs, own = own_features(features[1], 1, (), WIRE)
    terms = tie(terms, theirs)

    def activate(k, summed):
        batches, start, width = pieces[k]
        summed = (summed * (1.0 / scale)).reshape(2, len(batches), rows, width)
        gate_sum, up_sum = summed[0], summed[1]
        squash = jax.nn.sigmoid(gate_sum)
        product = (gate_sum * squash * up_sum).astype(jnp.bfloat16)
        for position, batch in enumerate(batches):
            hidden[batch].append(product[position])
        given = jnp.stack([wide(cotangent[b][:, start : start + width]) for b in batches])
        gate_act = given * up_sum * squash * (1.0 + gate_sum * (1.0 - squash))
        up_act = given * gate_sum * squash
        act = jnp.stack([gate_act, up_act]).astype(jnp.bfloat16)
        return act.reshape(2, len(batches) * rows, width)

    def merge(*hops):
        blocks = gather_blocks(at_end.astype(jnp.int32).reshape(1), *hops)
        return blocks, send(blocks, pairs)

    def add_gradients(acts, owner, totals, start):
        where = (owner * (share // tile)).astype(jnp.int32).reshape(1)
        acts = [value[:, None] for value in acts]
        return gradient(where, turned, acts, totals, half, start, tile)

    hidden, totals, merged, products = ([], []), (), [], {}
    act = hops = None
    for k in range(-1, last + 1):
        adding, gathering = k < last, act is not None
        if gathering:
            side_1, centre_1 = send(act, side), send(act, centre)
        if adding:
            if hops is not None:
                merged.append(merge(*hops))
                terms = tie(terms, merged[-1][0])
            if k == 0:
                products[2] = all_features(tokens, 2, act)
                terms = tie(terms, products[2])
            far, near = add(take(terms, 3), in_1).astype(WIRE), take(tie(terms, in_1), 2)
            near = near.astype(WIRE)
            centre_2, in_2 = send(far, centre), send(near, inward)
            before = (in_1,)
        else:
            hidden = jnp.stack([jnp.concatenate(parts, axis=1) for parts in hidden])
            hidden = hidden.reshape(2, 2, slab, share)
            mine = lax.dynamic_index_in_dim(hidden, core, 1, keepdims=False)
            theirs = lax.dynamic_index_in_dim(hidden, 1 - core, 1, keepdims=False)
            theirs = send(theirs, pairs)
            merged.append(merge(*tie(hops, theirs)))
            before = (theirs, merged[-1][0])
        if gathering:
            side_1, centre_1 = tie((side_1, centre_1), before)
            out_2, share_2 = send(centre_1, outward), send(side_1, centre)
        if k < 0:
            products[1] = (own((far, near)), send(theirs, pairs))
            terms = tie(terms, products[1])
        if not adding:
            own_acts, other_acts = zip(*merged)
            totals = add_gradients(own_acts, core, (), pieces[0][1])
            share_2 = tie(share_2, totals)
            hidden = by(core == 0, *tie((mine, theirs), side_1, centre_1), 2)
            theirs = lax.ppermute(hidden[1], "depth", swap)
            hidden = by(part == 0, hidden[0], theirs, 1)
            other_acts = tie(other_acts, theirs)
        if adding:
            if gathering:
                terms = tie(terms, side_1, centre_1)
            near = add(take(terms, 2), in_2).astype(WIRE)
            swapped = jnp.where(at_end, take(terms, 1), add(take(terms, 0), centre_2))
            swapped = swapped.astype(WIRE)
            centre_3, side_3 = send(near, centre), send(swapped, side)
            if k + 2 <= last:
                payload = take(tie(products[k + 2], near, swapped), 3).astype(WIRE)
                in_1 = send(payload, inward)
            before = (in_2, centre_2)
        if k < 0:
            cotangent = jnp.stack(tie(cotangent, near, swapped))
            cotangent = by(
                core == 0,
                columns_of(cotangent, core * share, share),
                send(columns_of(cotangent, (1 - core) * share, share), pairs),
                1,
            )
            far_weights = exchange_weights(2, (near, swapped))
            tokens = jnp.stack(tie(features, near, swapped), axis=1)
            tokens = (tokens, send(tokens, pairs))
        if k == 0:
            turned = [value.reshape(-1, depth) for value in tie(features, near, swapped)]
            turned = jnp.concatenate(turned).T
            terms = tie(terms, turned)
        if gathering:
            out_2, share_2 = tie((out_2, share_2), before)
            out_3 = send(share_2, outward)
        if adding:
            if gathering:
                terms = tie(terms, out_2, share_2)
            own_sum = jnp.where(at_end, take(terms, 0), take(terms, 1))
            ready = activate(k + 1, add(own_sum, side_3, centre_3))
            if gathering:
                hops = tie((act, side_1, centre_1, out_2, share_2, out_3), ready)
            act, terms = ready, products.get(k + 2)
        else:
            totals = add_gradients(other_acts, 1 - core, totals, pieces[0][1])
            out_3 = tie(out_3, totals)
            own_acts, other_acts = merge(act, side_1, centre_1, out_2, share_2, out_3)
    totals = add_gradients([own_acts], core, totals, pieces[last][1])
    totals = add_gradients([other_acts], 1 - core, totals, pieces[last][1])

    return (hidden[None], *totals)


def contract(picked, piece):
    return lax.dot_general(
        picked, piece, (((0,), (0,)), ((), ())), preferred_element_type=jnp.float32
    )


def local_any(tokens, gate_weight, up_weight, grad_hidden):
    features = lax.all_gather(tokens[0], "row", axis=1, tiled=True)
    columns = gate_weight.shape[1]
    picked = features
    gate_part = jnp.dot(picked, gate_weight, preferred_element_type=jnp.float32)
    up_part = jnp.dot(picked, up_weight, preferred_element_type=jnp.float32)
    summed = lax.psum_scatter(
        jnp.concatenate([gate_part, up_part], axis=1), "col", scatter_dimension=0, tiled=True
    )
    gate_sum = summed[:, :columns]
    up_sum = summed[:, columns:]
    squash = jax.nn.sigmoid(gate_sum)
    hidden = (gate_sum * squash * up_sum).astype(jnp.bfloat16)
    cotangent = grad_hidden[0].astype(jnp.float32)
    gate_act = (cotangent * up_sum * squash * (1.0 + gate_sum * (1.0 - squash))).astype(
        jnp.bfloat16
    )
    up_act = (cotangent * gate_sum * squash).astype(jnp.bfloat16)
    picked = features
    gate_total = contract(picked, lax.all_gather(gate_act, "col", axis=0, tiled=True))
    up_total = contract(picked, lax.all_gather(up_act, "col", axis=0, tiled=True))
    grad_gate, grad_up = (
        lax.psum_scatter(gate_total, "depth", scatter_dimension=1, tiled=True),
        lax.psum_scatter(up_total, "depth", scatter_dimension=1, tiled=True),
    )
    return (hidden[None], grad_gate, grad_up)


def solution(mesh):
    in_specs = (
        P("depth", None, ("col", "row")),
        P("col", "row"),
        P("col", "row"),
        P("depth", "col", "row"),
    )
    out_specs = (P("depth", "col", "row"), P("col", ("row", "depth")), P("col", ("row", "depth")))
    sizes = tuple(mesh.shape[name] for name in ("row", "col", "depth"))
    return jax.shard_map(
        local if sizes == (2, 8, 2) else local_any,
        mesh=mesh,
        in_specs=in_specs,
        out_specs=out_specs,
        check_vma=False,
    )
```

```python
import functools
import math

import jax
import jax.numpy as jnp
from jax import lax
from jax.experimental import pallas as pl
from jax.experimental.pallas import tpu as pltpu
from jax.sharding import PartitionSpec as P

WIRE = jnp.float16
LARGEST_TOKEN, LARGEST_WEIGHT = 6.0, 0.0625
VMEM_LIMIT = 48 * 2**20
NO_COST = pl.CostEstimate(flops=0, bytes_accessed=0, transcendentals=0)
LONG = pl.CostEstimate(flops=6 * 10**9, bytes_accessed=0, transcendentals=0)
SHARES = (5, 2)


def forward_kernel(scale, start, cores, place_ref, *refs):
    tokens, weights = refs[:cores], refs[cores : cores + 2 * cores]
    out_ref, held, arrived = refs[3 * cores :]
    tiles, _, tile = held.shape[1:]
    blocks, _, rows, _ = out_ref.shape

    def copy(j, which):
        first = start + j * tile
        if which < 2:
            columns = pl.ds(pl.multiple_of(place_ref[0] * tile + first, tile), tile)
            source = weights[which].at[:, columns]
        else:
            source = weights[which].at[which - 2, :, pl.ds(j * tile, tile)]
        return pltpu.make_async_copy(source, held.at[which, j], arrived.at[which, j])

    for j in range(tiles):
        for which in range(2 * cores):
            copy(j, which).start()
    for j in range(tiles):
        for which in range(2 * cores):
            copy(j, which).wait()
        for which in range(2):
            product = sum(
                jnp.dot(
                    tokens[i][...], held[which + 2 * i, j], preferred_element_type=jnp.float32
                )
                for i in range(cores)
            )
            product = (scale * product).reshape(blocks, rows, tile)
            out_ref[:, which, :, j * tile : (j + 1) * tile] = product


def forward(place, tokens, weights, start, width, tile, blocks, scale, cost=NO_COST):
    total, depth = tokens[0].shape
    cores = len(tokens)
    shape = (blocks, 2, total // blocks, width)
    return pl.pallas_call(
        functools.partial(forward_kernel, scale, start, cores),
        out_shape=jax.ShapeDtypeStruct(shape, jnp.float32),
        in_specs=[pl.BlockSpec(memory_space=pltpu.SMEM)]
        + [pl.BlockSpec(memory_space=pltpu.VMEM)] * cores
        + [pl.BlockSpec(memory_space=pl.ANY)] * (2 * cores),
        out_specs=pl.BlockSpec(memory_space=pltpu.VMEM),
        scratch_shapes=[
            pltpu.VMEM((2 * cores, width // tile, depth, tile), jnp.bfloat16),
            pltpu.SemaphoreType.DMA((2 * cores, width // tile)),
        ],
        compiler_params=pltpu.CompilerParams(vmem_limit_bytes=VMEM_LIMIT),
        cost_estimate=cost,
    )(place, *tokens, *weights)


def gradient_kernel(batches, place_ref, features_ref, *refs):
    acts, outs = refs[:batches], refs[-2:]
    for which, out_ref in enumerate(outs):
        parts = []
        for act_ref in acts:
            blocks, _, _, rows, width = act_ref.shape
            rows = rows * batches // 2
            for i in range(2 // batches):
                part = act_ref[:, 0, which, i * rows : (i + 1) * rows]
                parts.append(part.reshape(blocks * rows, width))
        out_ref[...] = jnp.dot(
            features_ref[...], jnp.concatenate(parts), preferred_element_type=jnp.float32
        )


def gradient(place, features, acts, totals, columns, start, tile):
    depth, total = features.shape
    blocks, cores, _, rows, width = acts[0].shape
    act_spec = pl.BlockSpec((blocks, 1, 2, rows, tile), lambda i, j, place: (0, i, 0, 0, j))
    out_spec = pl.BlockSpec((depth, tile), lambda i, j, place: (0, place[i] + start // tile + j))
    out_shape = jax.ShapeDtypeStruct((depth, columns), jnp.float32)
    in_specs = [pl.BlockSpec((depth, total), lambda i, j, place: (0, 0))]
    in_specs += [act_spec] * len(acts)
    in_specs += [pl.BlockSpec(memory_space=pl.ANY)] * len(totals)
    return pl.pallas_call(
        functools.partial(gradient_kernel, len(acts)),
        out_shape=(out_shape, out_shape),
        grid_spec=pltpu.PrefetchScalarGridSpec(
            num_scalar_prefetch=1,
            grid=(cores, width // tile),
            in_specs=in_specs,
            out_specs=(out_spec, out_spec),
        ),
        input_output_aliases={2 + len(acts) + i: i for i in range(len(totals))},
        compiler_params=pltpu.CompilerParams(vmem_limit_bytes=VMEM_LIMIT),
        cost_estimate=pl.CostEstimate(
            flops=4 * cores * total * depth * width,
            bytes_accessed=cores * (8 * depth + 4 * total) * width + 2 * total * depth,
            transcendentals=0,
        ),
    )(place, features, *acts, *totals)


def gather_kernel(at_end_ref, act, side_1, centre_1, out_2, share_2, out_3, out_ref):
    def fill(*blocks):
        for block, block_ref in enumerate(blocks):
            out_ref[block] = block_ref[...]

    pl.when(at_end_ref[0] == 1)(functools.partial(fill, act, side_1, out_2, out_3))
    pl.when(at_end_ref[0] == 0)(functools.partial(fill, side_1, act, centre_1, share_2))


def gather_blocks(at_end, *hops):
    _, rows, width = hops[0].shape
    spec = pl.BlockSpec((1, rows, width), lambda i, at_end: (i, 0, 0))
    return pl.pallas_call(
        gather_kernel,
        out_shape=jax.ShapeDtypeStruct((4, 2, rows, width), hops[0].dtype),
        grid_spec=pltpu.PrefetchScalarGridSpec(
            num_scalar_prefetch=1,
            grid=(2,),
            in_specs=[spec] * len(hops),
            out_specs=pl.BlockSpec((4, 1, rows, width), lambda i, at_end: (0, i, 0, 0)),
        ),
        compiler_params=pltpu.CompilerParams(vmem_limit_bytes=VMEM_LIMIT),
        cost_estimate=NO_COST,
    )(at_end, *hops)


def tie(value, *after):
    return lax.optimization_barrier((value, after))[0]


def cut(units, shares):
    edges = [round(units * sum(shares[:i]) / sum(shares)) for i in range(len(shares) + 1)]
    return [(a, b - a) for a, b in zip(edges, edges[1:]) if b > a]


def local(tokens, gate_weight, up_weight, grad_hidden):
    line = 4
    row, col, part = (lax.axis_index(name) for name in ("row", "col", "depth"))
    place, core = col // 2, col % 2
    slab = grad_hidden.shape[1]
    rows = 2 * slab
    depth, columns = gate_weight.shape
    half = columns // 2
    share = half // 2
    tile = 256 if share % 256 == 0 else 128
    largest = depth * 2 * line * LARGEST_TOKEN * LARGEST_WEIGHT
    scale = 2.0 ** math.floor(math.log2(65504 / largest))

    swap = [(0, 1), (1, 0)]
    pairs = [(i, i ^ 1) for i in range(2 * line)]

    def between(hops):
        return [(2 * i + c, 2 * j + c) for i, j in hops for c in (0, 1)]

    inward, outward = between([(0, 1), (3, 2)]), between([(1, 0), (2, 3)])
    side, centre = inward + outward, between([(1, 2), (2, 1)])
    at_end = (place == 0) | (place == line - 1)
    at_far = 2 * place >= line

    def send(value, route):
        return lax.ppermute(value, "col", route)

    def wide(value):
        return value.astype(jnp.float32)

    def add(*terms):
        return functools.reduce(jnp.add, map(wide, terms))

    def by(first, mine, theirs, axis):
        return jnp.where(
            first,
            jnp.concatenate([mine, theirs], axis=axis),
            jnp.concatenate([theirs, mine], axis=axis),
        )

    def columns_of(array, start, width):
        return lax.dynamic_slice_in_dim(array, start, width, array.ndim - 1)

    pieces = []
    for begin, count in cut(share // tile, SHARES):
        for batches in ((0, 1),) if pieces else ((0,), (1,)):
            pieces.append((batches, begin * tile, count * tile))
    last = len(pieces) - 1

    def exchange_weights(k, after):
        _, start, width = pieces[k]
        first = part * half + (1 - core) * share + start
        chosen = [
            columns_of(weight, first, width) for weight in tie((gate_weight, up_weight), after)
        ]
        return send(jnp.stack(chosen), pairs)

    mine = tokens[0]
    over_row = lax.ppermute(mine, "row", swap)
    over_depth = lax.ppermute(mine, "depth", swap)
    over_both = lax.ppermute(over_row, "depth", swap)
    own_tile, other_tile = [
        ((part * half + owner * share) // tile).astype(jnp.int32).reshape(1)
        for owner in (core, 1 - core)
    ]

    def arrange(values):
        values = values.reshape(line, rows, depth)
        return jnp.where(at_far, values[::-1], values)

    def own_features(tokens, k, after, wire):
        _, start, width = pieces[k]
        tokens = tie(tokens, after).reshape(-1, depth)
        common = ((gate_weight, up_weight), start, width, tile, line, scale)
        payload = forward(other_tile, [tokens], *common).astype(wire)

        def own(after, cost=NO_COST):
            return forward(own_tile, [tie(tokens, payload, after)], *common, cost)

        return payload, own

    def all_features(tokens, k, after):
        _, start, width = pieces[k]
        tokens = [value.reshape(-1, depth) for value in tie(tokens, after)]
        weights = (gate_weight, up_weight, far_weights, far_weights)
        return forward(own_tile, tokens, weights, start, width, tile, line, scale), None

    def take(terms, block):
        own, theirs = terms
        return own[block] if theirs is None else own[block] + wide(theirs[block])

    over_row = tie(over_row, over_depth)
    features = [arrange(by(row == 0, mine, over_row, 1))]
    theirs, own = own_features(features[0], 0, (), WIRE)
    terms = (own(()), send(theirs, pairs))
    payload = take(terms, 3).astype(WIRE)
    in_1 = send(payload, inward)

    over_depth, over_both = tie((over_depth, over_both), payload)
    features.append(arrange(by(row == 0, over_depth, over_both, 1)))
    theirs, own = own_features(features[1], 1, (), WIRE)
    terms = tie(terms, theirs)

    def activate(k, summed):
        batches, start, width = pieces[k]
        summed = (summed * (1.0 / scale)).reshape(2, len(batches), rows, width)
        gate_sum, up_sum = summed[0], summed[1]
        squash = jax.nn.sigmoid(gate_sum)
        product = (gate_sum * squash * up_sum).astype(jnp.bfloat16)
        for position, batch in enumerate(batches):
            hidden[batch].append(product[position])
        given = jnp.stack([wide(cotangent[b][:, start : start + width]) for b in batches])
        gate_act = given * up_sum * squash * (1.0 + gate_sum * (1.0 - squash))
        up_act = given * gate_sum * squash
        act = jnp.stack([gate_act, up_act]).astype(jnp.bfloat16)
        return act.reshape(2, len(batches) * rows, width)

    def merge(*hops):
        blocks = gather_blocks(at_end.astype(jnp.int32).reshape(1), *hops)
        return blocks, send(blocks, pairs)

    def add_gradients(acts, owner, totals, start):
        where = (owner * (share // tile)).astype(jnp.int32).reshape(1)
        acts = [value[:, None] for value in acts]
        return gradient(where, turned, acts, totals, half, start, tile)

    hidden, totals, merged, products = ([], []), (), [], {}
    act = hops = None
    for k in range(-1, last + 1):
        adding, gathering = k < last, act is not None
        if gathering:
            side_1, centre_1 = send(act, side), send(act, centre)
        if adding:
            if hops is not None:
                merged.append(merge(*hops))
                terms = tie(terms, merged[-1][0])
            if k == 0:
                products[2] = all_features(tokens, 2, act)
                terms = tie(terms, products[2])
            far, near = add(take(terms, 3), in_1).astype(WIRE), take(tie(terms, in_1), 2)
            near = near.astype(WIRE)
            centre_2, in_2 = send(far, centre), send(near, inward)
            before = (in_1,)
        else:
            hidden = jnp.stack([jnp.concatenate(parts, axis=1) for parts in hidden])
            hidden = hidden.reshape(2, 2, slab, share)
            mine = lax.dynamic_index_in_dim(hidden, core, 1, keepdims=False)
            theirs = lax.dynamic_index_in_dim(hidden, 1 - core, 1, keepdims=False)
            theirs = send(theirs, pairs)
            merged.append(merge(*tie(hops, theirs)))
            before = (theirs, merged[-1][0])
        if gathering:
            side_1, centre_1 = tie((side_1, centre_1), before)
            out_2, share_2 = send(centre_1, outward), send(side_1, centre)
        if k < 0:
            products[1] = (own((far, near), LONG), send(theirs, pairs))
            cotangent = tie(grad_hidden[0], far, near)
            cotangent = (
                columns_of(cotangent, part * half, half),
                lax.ppermute(columns_of(cotangent, (1 - part) * half, half), "depth", swap),
            )
            terms = tie(terms, products[1], cotangent[1])
        if not adding:
            own_acts, other_acts = zip(*merged)
            totals = add_gradients(own_acts, core, (), pieces[0][1])
            share_2 = tie(share_2, totals)
            hidden = by(core == 0, *tie((mine, theirs), side_1, centre_1), 2)
            theirs = lax.ppermute(hidden[1], "depth", swap)
            hidden = by(part == 0, hidden[0], theirs, 1)
            other_acts = tie(other_acts, theirs)
        if adding:
            if gathering:
                terms = tie(terms, side_1, centre_1)
            near = add(take(terms, 2), in_2).astype(WIRE)
            swapped = jnp.where(at_end, take(terms, 1), add(take(terms, 0), centre_2))
            swapped = swapped.astype(WIRE)
            centre_3, side_3 = send(near, centre), send(swapped, side)
            if k + 2 <= last:
                payload = take(tie(products[k + 2], near, swapped), 3).astype(WIRE)
                in_1 = send(payload, inward)
            before = (in_2, centre_2)
        if k < 0:
            cotangent = jnp.stack(tie(cotangent, near, swapped))
            cotangent = by(
                core == 0,
                columns_of(cotangent, core * share, share),
                send(columns_of(cotangent, (1 - core) * share, share), pairs),
                1,
            )
            far_weights = exchange_weights(2, (near, swapped))
            tokens = jnp.stack(tie(features, near, swapped), axis=1)
            tokens = (tokens, send(tokens, pairs))
        if k == 0:
            turned = [value.reshape(-1, depth) for value in tie(features, near, swapped)]
            turned = jnp.concatenate(turned).T
            terms = tie(terms, turned)
        if gathering:
            out_2, share_2 = tie((out_2, share_2), before)
            out_3 = send(share_2, outward)
        if adding:
            if gathering:
                terms = tie(terms, out_2, share_2)
            own_sum = jnp.where(at_end, take(terms, 0), take(terms, 1))
            ready = activate(k + 1, add(own_sum, side_3, centre_3))
            if gathering:
                hops = tie((act, side_1, centre_1, out_2, share_2, out_3), ready)
            act, terms = ready, products.get(k + 2)
        else:
            totals = add_gradients(other_acts, 1 - core, totals, pieces[0][1])
            out_3 = tie(out_3, totals)
            own_acts, other_acts = merge(act, side_1, centre_1, out_2, share_2, out_3)
    totals = add_gradients([own_acts], core, totals, pieces[last][1])
    totals = add_gradients([other_acts], 1 - core, totals, pieces[last][1])

    return (hidden[None], *totals)


def contract(picked, piece):
    return lax.dot_general(
        picked, piece, (((0,), (0,)), ((), ())), preferred_element_type=jnp.float32
    )


def local_any(tokens, gate_weight, up_weight, grad_hidden):
    features = lax.all_gather(tokens[0], "row", axis=1, tiled=True)
    columns = gate_weight.shape[1]
    picked = features
    gate_part = jnp.dot(picked, gate_weight, preferred_element_type=jnp.float32)
    up_part = jnp.dot(picked, up_weight, preferred_element_type=jnp.float32)
    summed = lax.psum_scatter(
        jnp.concatenate([gate_part, up_part], axis=1), "col", scatter_dimension=0, tiled=True
    )
    gate_sum = summed[:, :columns]
    up_sum = summed[:, columns:]
    squash = jax.nn.sigmoid(gate_sum)
    hidden = (gate_sum * squash * up_sum).astype(jnp.bfloat16)
    cotangent = grad_hidden[0].astype(jnp.float32)
    gate_act = (cotangent * up_sum * squash * (1.0 + gate_sum * (1.0 - squash))).astype(
        jnp.bfloat16
    )
    up_act = (cotangent * gate_sum * squash).astype(jnp.bfloat16)
    picked = features
    gate_total = contract(picked, lax.all_gather(gate_act, "col", axis=0, tiled=True))
    up_total = contract(picked, lax.all_gather(up_act, "col", axis=0, tiled=True))
    grad_gate, grad_up = (
        lax.psum_scatter(gate_total, "depth", scatter_dimension=1, tiled=True),
        lax.psum_scatter(up_total, "depth", scatter_dimension=1, tiled=True),
    )
    return (hidden[None], grad_gate, grad_up)


def solution(mesh):
    in_specs = (
        P("depth", None, ("col", "row")),
        P("col", "row"),
        P("col", "row"),
        P("depth", "col", "row"),
    )
    out_specs = (P("depth", "col", "row"), P("col", ("row", "depth")), P("col", ("row", "depth")))
    sizes = tuple(mesh.shape[name] for name in ("row", "col", "depth"))
    return jax.shard_map(
        local if sizes == (2, 8, 2) else local_any,
        mesh=mesh,
        in_specs=in_specs,
        out_specs=out_specs,
        check_vma=False,
    )
```

```python
import functools
import math

import jax
import jax.numpy as jnp
from jax import lax
from jax.experimental import pallas as pl
from jax.experimental.pallas import tpu as pltpu
from jax.sharding import PartitionSpec as P

WIRE = jnp.float16
LARGEST_TOKEN, LARGEST_WEIGHT = 6.0, 0.0625
VMEM_LIMIT = 48 * 2**20
NO_COST = pl.CostEstimate(flops=0, bytes_accessed=0, transcendentals=0)
LONG = pl.CostEstimate(flops=6 * 10**9, bytes_accessed=0, transcendentals=0)
SHARES = (5, 2)


def forward_kernel(scale, start, cores, place_ref, *refs):
    tokens, weights = refs[:cores], refs[cores : cores + 2 * cores]
    out_ref, held, arrived = refs[3 * cores :]
    tiles, _, tile = held.shape[1:]
    tile //= 2
    blocks, _, rows, _ = out_ref.shape

    def copy(j, which):
        first = start + j * tile
        if which < 2:
            columns = pl.ds(pl.multiple_of(place_ref[0] * tile + first, tile), tile)
            source = weights[which].at[:, columns]
        else:
            source = weights[which].at[which - 2, :, pl.ds(j * tile, tile)]
        place = pl.ds(which % 2 * tile, tile)
        held_here = held.at[which // 2, j, :, place]
        return pltpu.make_async_copy(source, held_here, arrived.at[which, j])

    for j in range(tiles):
        for which in range(2 * cores):
            copy(j, which).start()
    for j in range(tiles):
        for which in range(2 * cores):
            copy(j, which).wait()
        product = scale * sum(
            jnp.dot(tokens[i][...], held[i, j], preferred_element_type=jnp.float32)
            for i in range(cores)
        )
        for which in range(2):
            half = product[:, which * tile : (which + 1) * tile].reshape(blocks, rows, tile)
            out_ref[:, which, :, j * tile : (j + 1) * tile] = half


def forward(place, tokens, weights, start, width, tile, blocks, scale, cost=NO_COST):
    total, depth = tokens[0].shape
    cores = len(tokens)
    shape = (blocks, 2, total // blocks, width)
    return pl.pallas_call(
        functools.partial(forward_kernel, scale, start, cores),
        out_shape=jax.ShapeDtypeStruct(shape, jnp.float32),
        in_specs=[pl.BlockSpec(memory_space=pltpu.SMEM)]
        + [pl.BlockSpec(memory_space=pltpu.VMEM)] * cores
        + [pl.BlockSpec(memory_space=pl.ANY)] * (2 * cores),
        out_specs=pl.BlockSpec(memory_space=pltpu.VMEM),
        scratch_shapes=[
            pltpu.VMEM((cores, width // tile, depth, 2 * tile), jnp.bfloat16),
            pltpu.SemaphoreType.DMA((2 * cores, width // tile)),
        ],
        compiler_params=pltpu.CompilerParams(vmem_limit_bytes=VMEM_LIMIT),
        cost_estimate=cost,
    )(place, *tokens, *weights)


def gradient_kernel(batches, place_ref, features_ref, *refs):
    acts, outs = refs[:batches], refs[-2:]
    halves = []
    for which in range(2):
        parts = []
        for act_ref in acts:
            blocks, _, _, rows, width = act_ref.shape
            rows = rows * batches // 2
            for i in range(2 // batches):
                part = act_ref[:, 0, which, i * rows : (i + 1) * rows]
                parts.append(part.reshape(blocks * rows, width))
        halves.append(jnp.concatenate(parts))
    both = jnp.dot(
        features_ref[...], jnp.concatenate(halves, axis=1), preferred_element_type=jnp.float32
    )
    for which, out_ref in enumerate(outs):
        out_ref[...] = both[:, which * width : (which + 1) * width]


def gradient(place, features, acts, totals, columns, start, tile):
    depth, total = features.shape
    blocks, cores, _, rows, width = acts[0].shape
    act_spec = pl.BlockSpec((blocks, 1, 2, rows, tile), lambda i, j, place: (0, i, 0, 0, j))
    out_spec = pl.BlockSpec((depth, tile), lambda i, j, place: (0, place[i] + start // tile + j))
    out_shape = jax.ShapeDtypeStruct((depth, columns), jnp.float32)
    in_specs = [pl.BlockSpec((depth, total), lambda i, j, place: (0, 0))]
    in_specs += [act_spec] * len(acts)
    in_specs += [pl.BlockSpec(memory_space=pl.ANY)] * len(totals)
    return pl.pallas_call(
        functools.partial(gradient_kernel, len(acts)),
        out_shape=(out_shape, out_shape),
        grid_spec=pltpu.PrefetchScalarGridSpec(
            num_scalar_prefetch=1,
            grid=(cores, width // tile),
            in_specs=in_specs,
            out_specs=(out_spec, out_spec),
        ),
        input_output_aliases={2 + len(acts) + i: i for i in range(len(totals))},
        compiler_params=pltpu.CompilerParams(vmem_limit_bytes=VMEM_LIMIT),
        cost_estimate=pl.CostEstimate(
            flops=4 * cores * total * depth * width,
            bytes_accessed=cores * (8 * depth + 4 * total) * width + 2 * total * depth,
            transcendentals=0,
        ),
    )(place, features, *acts, *totals)


def gather_kernel(at_end_ref, act, side_1, centre_1, out_2, share_2, out_3, out_ref):
    def fill(*blocks):
        for block, block_ref in enumerate(blocks):
            out_ref[block] = block_ref[...]

    pl.when(at_end_ref[0] == 1)(functools.partial(fill, act, side_1, out_2, out_3))
    pl.when(at_end_ref[0] == 0)(functools.partial(fill, side_1, act, centre_1, share_2))


def gather_blocks(at_end, *hops):
    _, rows, width = hops[0].shape
    spec = pl.BlockSpec((1, rows, width), lambda i, at_end: (i, 0, 0))
    return pl.pallas_call(
        gather_kernel,
        out_shape=jax.ShapeDtypeStruct((4, 2, rows, width), hops[0].dtype),
        grid_spec=pltpu.PrefetchScalarGridSpec(
            num_scalar_prefetch=1,
            grid=(2,),
            in_specs=[spec] * len(hops),
            out_specs=pl.BlockSpec((4, 1, rows, width), lambda i, at_end: (0, i, 0, 0)),
        ),
        compiler_params=pltpu.CompilerParams(vmem_limit_bytes=VMEM_LIMIT),
        cost_estimate=NO_COST,
    )(at_end, *hops)


def tie(value, *after):
    return lax.optimization_barrier((value, after))[0]


def cut(units, shares):
    edges = [round(units * sum(shares[:i]) / sum(shares)) for i in range(len(shares) + 1)]
    return [(a, b - a) for a, b in zip(edges, edges[1:]) if b > a]


def local(tokens, gate_weight, up_weight, grad_hidden):
    line = 4
    row, col, part = (lax.axis_index(name) for name in ("row", "col", "depth"))
    place, core = col // 2, col % 2
    slab = grad_hidden.shape[1]
    rows = 2 * slab
    depth, columns = gate_weight.shape
    half = columns // 2
    share = half // 2
    tile = 256 if share % 256 == 0 else 128
    largest = depth * 2 * line * LARGEST_TOKEN * LARGEST_WEIGHT
    scale = 2.0 ** math.floor(math.log2(65504 / largest))

    swap = [(0, 1), (1, 0)]
    pairs = [(i, i ^ 1) for i in range(2 * line)]

    def between(hops):
        return [(2 * i + c, 2 * j + c) for i, j in hops for c in (0, 1)]

    inward, outward = between([(0, 1), (3, 2)]), between([(1, 0), (2, 3)])
    side, centre = inward + outward, between([(1, 2), (2, 1)])
    at_end = (place == 0) | (place == line - 1)
    at_far = 2 * place >= line

    def send(value, route):
        return lax.ppermute(value, "col", route)

    def wide(value):
        return value.astype(jnp.float32)

    def add(*terms):
        return functools.reduce(jnp.add, map(wide, terms))

    def by(first, mine, theirs, axis):
        return jnp.where(
            first,
            jnp.concatenate([mine, theirs], axis=axis),
            jnp.concatenate([theirs, mine], axis=axis),
        )

    def columns_of(array, start, width):
        return lax.dynamic_slice_in_dim(array, start, width, array.ndim - 1)

    pieces = []
    for begin, count in cut(share // tile, SHARES):
        for batches in ((0, 1),) if pieces else ((0,), (1,)):
            pieces.append((batches, begin * tile, count * tile))
    last = len(pieces) - 1

    def exchange_weights(k, after):
        _, start, width = pieces[k]
        first = part * half + (1 - core) * share + start
        chosen = [
            columns_of(weight, first, width) for weight in tie((gate_weight, up_weight), after)
        ]
        return send(jnp.stack(chosen), pairs)

    mine = tokens[0]
    over_row = lax.ppermute(mine, "row", swap)
    over_depth = lax.ppermute(mine, "depth", swap)
    over_both = lax.ppermute(over_row, "depth", swap)
    own_tile, other_tile = [
        ((part * half + owner * share) // tile).astype(jnp.int32).reshape(1)
        for owner in (core, 1 - core)
    ]

    def arrange(values):
        values = values.reshape(line, rows, depth)
        return jnp.where(at_far, values[::-1], values)

    def own_features(tokens, k, after, wire):
        _, start, width = pieces[k]
        tokens = tie(tokens, after).reshape(-1, depth)
        common = ((gate_weight, up_weight), start, width, tile, line, scale)
        payload = forward(other_tile, [tokens], *common).astype(wire)

        def own(after, cost=NO_COST):
            return forward(own_tile, [tie(tokens, payload, after)], *common, cost)

        return payload, own

    def all_features(tokens, k, after):
        _, start, width = pieces[k]
        tokens = [value.reshape(-1, depth) for value in tie(tokens, after)]
        weights = (gate_weight, up_weight, far_weights, far_weights)
        return forward(own_tile, tokens, weights, start, width, tile, line, scale), None

    def take(terms, block):
        own, theirs = terms
        return own[block] if theirs is None else own[block] + wide(theirs[block])

    over_row = tie(over_row, over_depth)
    features = [arrange(by(row == 0, mine, over_row, 1))]
    theirs, own = own_features(features[0], 0, (), WIRE)
    terms = (own(()), send(theirs, pairs))
    payload = take(terms, 3).astype(WIRE)
    in_1 = send(payload, inward)

    over_depth, over_both = tie((over_depth, over_both), payload)
    features.append(arrange(by(row == 0, over_depth, over_both, 1)))
    theirs, own = own_features(features[1], 1, (), WIRE)
    terms = tie(terms, theirs)

    def activate(k, summed):
        batches, start, width = pieces[k]
        summed = (summed * (1.0 / scale)).reshape(2, len(batches), rows, width)
        gate_sum, up_sum = summed[0], summed[1]
        squash = jax.nn.sigmoid(gate_sum)
        product = (gate_sum * squash * up_sum).astype(jnp.bfloat16)
        for position, batch in enumerate(batches):
            hidden[batch].append(product[position])
        given = jnp.stack([wide(cotangent[b][:, start : start + width]) for b in batches])
        gate_act = given * up_sum * squash * (1.0 + gate_sum * (1.0 - squash))
        up_act = given * gate_sum * squash
        act = jnp.stack([gate_act, up_act]).astype(jnp.bfloat16)
        return act.reshape(2, len(batches) * rows, width)

    def merge(*hops):
        blocks = gather_blocks(at_end.astype(jnp.int32).reshape(1), *hops)
        return blocks, send(blocks, pairs)

    def add_gradients(acts, owner, totals, start):
        where = (owner * (share // tile)).astype(jnp.int32).reshape(1)
        acts = [value[:, None] for value in acts]
        return gradient(where, turned, acts, totals, half, start, tile)

    hidden, totals, merged, products = ([], []), (), [], {}
    act = hops = None
    for k in range(-1, last + 1):
        adding, gathering = k < last, act is not None
        if gathering:
            side_1, centre_1 = send(act, side), send(act, centre)
        if adding:
            if hops is not None:
                merged.append(merge(*hops))
                terms = tie(terms, merged[-1][0])
            if k == 0:
                products[2] = all_features(tokens, 2, act)
                terms = tie(terms, products[2])
            far, near = add(take(terms, 3), in_1).astype(WIRE), take(tie(terms, in_1), 2)
            near = near.astype(WIRE)
            centre_2, in_2 = send(far, centre), send(near, inward)
            before = (in_1,)
        else:
            hidden = jnp.stack([jnp.concatenate(parts, axis=1) for parts in hidden])
            hidden = hidden.reshape(2, 2, slab, share)
            mine = lax.dynamic_index_in_dim(hidden, core, 1, keepdims=False)
            theirs = lax.dynamic_index_in_dim(hidden, 1 - core, 1, keepdims=False)
            theirs = send(theirs, pairs)
            merged.append(merge(*tie(hops, theirs)))
            before = (theirs, merged[-1][0])
        if gathering:
            side_1, centre_1 = tie((side_1, centre_1), before)
            out_2, share_2 = send(centre_1, outward), send(side_1, centre)
        if k < 0:
            products[1] = (own((far, near), LONG), send(theirs, pairs))
            cotangent = tie(grad_hidden[0], far, near)
            cotangent = (
                columns_of(cotangent, part * half, half),
                lax.ppermute(columns_of(cotangent, (1 - part) * half, half), "depth", swap),
            )
            terms = tie(terms, products[1], cotangent[1])
        if not adding:
            own_acts, other_acts = zip(*merged)
            totals = add_gradients(own_acts, core, (), pieces[0][1])
            share_2 = tie(share_2, totals)
            hidden = by(core == 0, *tie((mine, theirs), side_1, centre_1), 2)
            theirs = lax.ppermute(hidden[1], "depth", swap)
            hidden = by(part == 0, hidden[0], theirs, 1)
            other_acts = tie(other_acts, theirs)
        if adding:
            if gathering:
                terms = tie(terms, side_1, centre_1)
            near = add(take(terms, 2), in_2).astype(WIRE)
            swapped = jnp.where(at_end, take(terms, 1), add(take(terms, 0), centre_2))
            swapped = swapped.astype(WIRE)
            centre_3, side_3 = send(near, centre), send(swapped, side)
            if k + 2 <= last:
                payload = take(tie(products[k + 2], near, swapped), 3).astype(WIRE)
                in_1 = send(payload, inward)
            before = (in_2, centre_2)
        if k < 0:
            cotangent = jnp.stack(tie(cotangent, near, swapped))
            cotangent = by(
                core == 0,
                columns_of(cotangent, core * share, share),
                send(columns_of(cotangent, (1 - core) * share, share), pairs),
                1,
            )
            far_weights = exchange_weights(2, (near, swapped))
            tokens = jnp.stack(tie(features, near, swapped), axis=1)
            tokens = (tokens, send(tokens, pairs))
        if k == 0:
            turned = [value.reshape(-1, depth) for value in tie(features, near, swapped)]
            turned = jnp.concatenate(turned).T
            terms = tie(terms, turned)
        if gathering:
            out_2, share_2 = tie((out_2, share_2), before)
            out_3 = send(share_2, outward)
        if adding:
            if gathering:
                terms = tie(terms, out_2, share_2)
            own_sum = jnp.where(at_end, take(terms, 0), take(terms, 1))
            ready = activate(k + 1, add(own_sum, side_3, centre_3))
            if gathering:
                hops = tie((act, side_1, centre_1, out_2, share_2, out_3), ready)
            act, terms = ready, products.get(k + 2)
        else:
            totals = add_gradients(other_acts, 1 - core, totals, pieces[0][1])
            out_3, hidden = lax.optimization_barrier((tie(out_3, totals), hidden))
            own_acts, other_acts = merge(act, side_1, centre_1, out_2, share_2, out_3)
    totals = add_gradients([own_acts], core, totals, pieces[last][1])
    totals = add_gradients([other_acts], 1 - core, totals, pieces[last][1])

    return (hidden[None], *totals)


def contract(picked, piece):
    return lax.dot_general(
        picked, piece, (((0,), (0,)), ((), ())), preferred_element_type=jnp.float32
    )


def local_any(tokens, gate_weight, up_weight, grad_hidden):
    features = lax.all_gather(tokens[0], "row", axis=1, tiled=True)
    columns = gate_weight.shape[1]
    picked = features
    gate_part = jnp.dot(picked, gate_weight, preferred_element_type=jnp.float32)
    up_part = jnp.dot(picked, up_weight, preferred_element_type=jnp.float32)
    summed = lax.psum_scatter(
        jnp.concatenate([gate_part, up_part], axis=1), "col", scatter_dimension=0, tiled=True
    )
    gate_sum = summed[:, :columns]
    up_sum = summed[:, columns:]
    squash = jax.nn.sigmoid(gate_sum)
    hidden = (gate_sum * squash * up_sum).astype(jnp.bfloat16)
    cotangent = grad_hidden[0].astype(jnp.float32)
    gate_act = (cotangent * up_sum * squash * (1.0 + gate_sum * (1.0 - squash))).astype(
        jnp.bfloat16
    )
    up_act = (cotangent * gate_sum * squash).astype(jnp.bfloat16)
    picked = features
    gate_total = contract(picked, lax.all_gather(gate_act, "col", axis=0, tiled=True))
    up_total = contract(picked, lax.all_gather(up_act, "col", axis=0, tiled=True))
    grad_gate, grad_up = (
        lax.psum_scatter(gate_total, "depth", scatter_dimension=1, tiled=True),
        lax.psum_scatter(up_total, "depth", scatter_dimension=1, tiled=True),
    )
    return (hidden[None], grad_gate, grad_up)


def solution(mesh):
    in_specs = (
        P("depth", None, ("col", "row")),
        P("col", "row"),
        P("col", "row"),
        P("depth", "col", "row"),
    )
    out_specs = (P("depth", "col", "row"), P("col", ("row", "depth")), P("col", ("row", "depth")))
    sizes = tuple(mesh.shape[name] for name in ("row", "col", "depth"))
    return jax.shard_map(
        local if sizes == (2, 8, 2) else local_any,
        mesh=mesh,
        in_specs=in_specs,
        out_specs=out_specs,
        check_vma=False,
    )
```

```python
import functools
import math

import jax
import jax.numpy as jnp
from jax import lax
from jax.experimental import pallas as pl
from jax.experimental.pallas import tpu as pltpu
from jax.sharding import PartitionSpec as P

WIRE = jnp.float16
LARGEST_TOKEN, LARGEST_WEIGHT = 6.0, 0.0625
VMEM_LIMIT = 48 * 2**20
NO_COST = pl.CostEstimate(flops=0, bytes_accessed=0, transcendentals=0)
LONG = pl.CostEstimate(flops=6 * 10**9, bytes_accessed=0, transcendentals=0)
SHARES = (5, 2)


def forward_kernel(scale, start, unit, cores, place_ref, *refs):
    tokens, weights = refs[:cores], refs[cores : cores + 2 * cores]
    out_ref, held, arrived = refs[3 * cores :]
    tiles, _, tile = held.shape[1:]
    tile //= 2
    blocks, _, rows, _ = out_ref.shape

    def copy(j, which):
        first = start + j * tile
        if which < 2:
            columns = pl.ds(pl.multiple_of(place_ref[0] * unit + first, 128), tile)
            source = weights[which].at[:, columns]
        else:
            source = weights[which].at[which - 2, :, pl.ds(j * tile, tile)]
        place = pl.ds(which % 2 * tile, tile)
        held_here = held.at[which // 2, j, :, place]
        return pltpu.make_async_copy(source, held_here, arrived.at[which, j])

    for j in range(tiles):
        for which in range(2 * cores):
            copy(j, which).start()
    for j in range(tiles):
        for which in range(2 * cores):
            copy(j, which).wait()
        product = scale * sum(
            jnp.dot(tokens[i][...], held[i, j], preferred_element_type=jnp.float32)
            for i in range(cores)
        )
        for which in range(2):
            half = product[:, which * tile : (which + 1) * tile].reshape(blocks, rows, tile)
            out_ref[:, which, :, j * tile : (j + 1) * tile] = half


def forward(place, tokens, weights, start, width, tile, blocks, scale, cost=NO_COST):
    total, depth = tokens[0].shape
    cores = len(tokens)
    shape = (blocks, 2, total // blocks, width)
    steps = 2 if width % 256 == 0 else 1
    return pl.pallas_call(
        functools.partial(forward_kernel, scale, start, tile, cores),
        out_shape=jax.ShapeDtypeStruct(shape, jnp.float32),
        in_specs=[pl.BlockSpec(memory_space=pltpu.SMEM)]
        + [pl.BlockSpec(memory_space=pltpu.VMEM)] * cores
        + [pl.BlockSpec(memory_space=pl.ANY)] * (2 * cores),
        out_specs=pl.BlockSpec(memory_space=pltpu.VMEM),
        scratch_shapes=[
            pltpu.VMEM((cores, steps, depth, 2 * (width // steps)), jnp.bfloat16),
            pltpu.SemaphoreType.DMA((2 * cores, steps)),
        ],
        compiler_params=pltpu.CompilerParams(vmem_limit_bytes=VMEM_LIMIT),
        cost_estimate=cost,
    )(place, *tokens, *weights)


def gradient_kernel(batches, place_ref, features_ref, *refs):
    acts, outs = refs[:batches], refs[-2:]
    halves = []
    for which in range(2):
        parts = []
        for act_ref in acts:
            blocks, _, _, rows, width = act_ref.shape
            rows = rows * batches // 2
            for i in range(2 // batches):
                part = act_ref[:, 0, which, i * rows : (i + 1) * rows]
                parts.append(part.reshape(blocks * rows, width))
        halves.append(jnp.concatenate(parts))
    both = jnp.dot(
        features_ref[...], jnp.concatenate(halves, axis=1), preferred_element_type=jnp.float32
    )
    for which, out_ref in enumerate(outs):
        out_ref[...] = both[:, which * width : (which + 1) * width]


def gradient(place, features, acts, totals, columns, start, tile):
    depth, total = features.shape
    blocks, cores, _, rows, width = acts[0].shape
    act_spec = pl.BlockSpec((blocks, 1, 2, rows, tile), lambda i, j, place: (0, i, 0, 0, j))
    out_spec = pl.BlockSpec((depth, tile), lambda i, j, place: (0, place[i] + start // tile + j))
    out_shape = jax.ShapeDtypeStruct((depth, columns), jnp.float32)
    in_specs = [pl.BlockSpec((depth, total), lambda i, j, place: (0, 0))]
    in_specs += [act_spec] * len(acts)
    in_specs += [pl.BlockSpec(memory_space=pl.ANY)] * len(totals)
    return pl.pallas_call(
        functools.partial(gradient_kernel, len(acts)),
        out_shape=(out_shape, out_shape),
        grid_spec=pltpu.PrefetchScalarGridSpec(
            num_scalar_prefetch=1,
            grid=(cores, width // tile),
            in_specs=in_specs,
            out_specs=(out_spec, out_spec),
        ),
        input_output_aliases={2 + len(acts) + i: i for i in range(len(totals))},
        compiler_params=pltpu.CompilerParams(vmem_limit_bytes=VMEM_LIMIT),
        cost_estimate=pl.CostEstimate(
            flops=4 * cores * total * depth * width,
            bytes_accessed=cores * (8 * depth + 4 * total) * width + 2 * total * depth,
            transcendentals=0,
        ),
    )(place, features, *acts, *totals)


def gather_kernel(at_end_ref, act, side_1, centre_1, out_2, share_2, out_3, out_ref):
    def fill(*blocks):
        for block, block_ref in enumerate(blocks):
            out_ref[block] = block_ref[...]

    pl.when(at_end_ref[0] == 1)(functools.partial(fill, act, side_1, out_2, out_3))
    pl.when(at_end_ref[0] == 0)(functools.partial(fill, side_1, act, centre_1, share_2))


def gather_blocks(at_end, *hops):
    _, rows, width = hops[0].shape
    spec = pl.BlockSpec((1, rows, width), lambda i, at_end: (i, 0, 0))
    return pl.pallas_call(
        gather_kernel,
        out_shape=jax.ShapeDtypeStruct((4, 2, rows, width), hops[0].dtype),
        grid_spec=pltpu.PrefetchScalarGridSpec(
            num_scalar_prefetch=1,
            grid=(2,),
            in_specs=[spec] * len(hops),
            out_specs=pl.BlockSpec((4, 1, rows, width), lambda i, at_end: (0, i, 0, 0)),
        ),
        compiler_params=pltpu.CompilerParams(vmem_limit_bytes=VMEM_LIMIT),
        cost_estimate=NO_COST,
    )(at_end, *hops)


def tie(value, *after):
    return lax.optimization_barrier((value, after))[0]


def cut(units, shares):
    edges = [round(units * sum(shares[:i]) / sum(shares)) for i in range(len(shares) + 1)]
    return [(a, b - a) for a, b in zip(edges, edges[1:]) if b > a]


def local(tokens, gate_weight, up_weight, grad_hidden):
    line = 4
    row, col, part = (lax.axis_index(name) for name in ("row", "col", "depth"))
    place, core = col // 2, col % 2
    slab = grad_hidden.shape[1]
    rows = 2 * slab
    depth, columns = gate_weight.shape
    half = columns // 2
    share = half // 2
    tile = 256 if share % 256 == 0 else 128
    largest = depth * 2 * line * LARGEST_TOKEN * LARGEST_WEIGHT
    scale = 2.0 ** math.floor(math.log2(65504 / largest))

    swap = [(0, 1), (1, 0)]
    pairs = [(i, i ^ 1) for i in range(2 * line)]

    def between(hops):
        return [(2 * i + c, 2 * j + c) for i, j in hops for c in (0, 1)]

    inward, outward = between([(0, 1), (3, 2)]), between([(1, 0), (2, 3)])
    side, centre = inward + outward, between([(1, 2), (2, 1)])
    at_end = (place == 0) | (place == line - 1)
    at_far = 2 * place >= line

    def send(value, route):
        return lax.ppermute(value, "col", route)

    def wide(value):
        return value.astype(jnp.float32)

    def add(*terms):
        return functools.reduce(jnp.add, map(wide, terms))

    def by(first, mine, theirs, axis):
        return jnp.where(
            first,
            jnp.concatenate([mine, theirs], axis=axis),
            jnp.concatenate([theirs, mine], axis=axis),
        )

    def columns_of(array, start, width):
        return lax.dynamic_slice_in_dim(array, start, width, array.ndim - 1)

    pieces = []
    for begin, count in cut(share // tile, SHARES):
        for batches in ((0, 1),) if pieces else ((0,), (1,)):
            pieces.append((batches, begin * tile, count * tile))
    last = len(pieces) - 1

    def exchange_weights(k, after):
        _, start, width = pieces[k]
        first = part * half + (1 - core) * share + start
        chosen = [
            columns_of(weight, first, width) for weight in tie((gate_weight, up_weight), after)
        ]
        return send(jnp.stack(chosen), pairs)

    mine = tokens[0]
    over_row = lax.ppermute(mine, "row", swap)
    over_depth = lax.ppermute(mine, "depth", swap)
    over_both = lax.ppermute(over_row, "depth", swap)
    own_tile, other_tile = [
        ((part * half + owner * share) // tile).astype(jnp.int32).reshape(1)
        for owner in (core, 1 - core)
    ]

    def arrange(values):
        values = values.reshape(line, rows, depth)
        return jnp.where(at_far, values[::-1], values)

    def own_features(tokens, k, after, wire):
        _, start, width = pieces[k]
        tokens = tie(tokens, after).reshape(-1, depth)
        common = ((gate_weight, up_weight), start, width, tile, line, scale)
        payload = forward(other_tile, [tokens], *common).astype(wire)

        def own(after, cost=NO_COST):
            return forward(own_tile, [tie(tokens, payload, after)], *common, cost)

        return payload, own

    def all_features(tokens, k, after):
        _, start, width = pieces[k]
        tokens = [value.reshape(-1, depth) for value in tie(tokens, after)]
        weights = (gate_weight, up_weight, far_weights, far_weights)
        return forward(own_tile, tokens, weights, start, width, tile, line, scale), None

    def take(terms, block):
        own, theirs = terms
        return own[block] if theirs is None else own[block] + wide(theirs[block])

    over_row = tie(over_row, over_depth)
    features = [arrange(by(row == 0, mine, over_row, 1))]
    theirs, own = own_features(features[0], 0, (), WIRE)
    terms = (own((), LONG), send(theirs, pairs))
    payload = take(terms, 3).astype(WIRE)
    in_1 = send(payload, inward)

    over_depth, over_both = tie((over_depth, over_both), payload)
    features.append(arrange(by(row == 0, over_depth, over_both, 1)))
    theirs, own = own_features(features[1], 1, (), WIRE)
    terms = tie(terms, theirs)

    def activate(k, summed):
        batches, start, width = pieces[k]
        summed = (summed * (1.0 / scale)).reshape(2, len(batches), rows, width)
        gate_sum, up_sum = summed[0], summed[1]
        squash = jax.nn.sigmoid(gate_sum)
        product = (gate_sum * squash * up_sum).astype(jnp.bfloat16)
        for position, batch in enumerate(batches):
            hidden[batch].append(product[position])
        given = jnp.stack([wide(cotangent[b][:, start : start + width]) for b in batches])
        gate_act = given * up_sum * squash * (1.0 + gate_sum * (1.0 - squash))
        up_act = given * gate_sum * squash
        act = jnp.stack([gate_act, up_act]).astype(jnp.bfloat16)
        return act.reshape(2, len(batches) * rows, width)

    def merge(*hops):
        blocks = gather_blocks(at_end.astype(jnp.int32).reshape(1), *hops)
        return blocks, send(blocks, pairs)

    def add_gradients(acts, owner, totals, start):
        where = (owner * (share // tile)).astype(jnp.int32).reshape(1)
        acts = [value[:, None] for value in acts]
        return gradient(where, turned, acts, totals, half, start, tile)

    hidden, totals, merged, products = ([], []), (), [], {}
    act = hops = None
    for k in range(-1, last + 1):
        adding, gathering = k < last, act is not None
        if gathering:
            side_1, centre_1 = send(act, side), send(act, centre)
        if adding:
            if hops is not None:
                merged.append(merge(*hops))
                terms = tie(terms, merged[-1][0])
            if k == 0:
                products[2] = all_features(tokens, 2, act)
                terms = tie(terms, products[2])
            far, near = add(take(terms, 3), in_1).astype(WIRE), take(tie(terms, in_1), 2)
            near = near.astype(WIRE)
            centre_2, in_2 = send(far, centre), send(near, inward)
            before = (in_1,)
        else:
            hidden = jnp.stack([jnp.concatenate(parts, axis=1) for parts in hidden])
            hidden = hidden.reshape(2, 2, slab, share)
            mine = lax.dynamic_index_in_dim(hidden, core, 1, keepdims=False)
            theirs = lax.dynamic_index_in_dim(hidden, 1 - core, 1, keepdims=False)
            theirs = send(theirs, pairs)
            merged.append(merge(*tie(hops, theirs)))
            before = (theirs, merged[-1][0])
        if gathering:
            side_1, centre_1 = tie((side_1, centre_1), before)
            out_2, share_2 = send(centre_1, outward), send(side_1, centre)
        if k < 0:
            products[1] = (own((far, near), LONG), send(theirs, pairs))
            cotangent = tie(grad_hidden[0], far, near)
            cotangent = (
                columns_of(cotangent, part * half, half),
                lax.ppermute(columns_of(cotangent, (1 - part) * half, half), "depth", swap),
            )
            terms = tie(terms, products[1], cotangent[1])
        if not adding:
            own_acts, other_acts = zip(*merged)
            totals = add_gradients(own_acts, core, (), pieces[0][1])
            share_2 = tie(share_2, totals)
            hidden = by(core == 0, *tie((mine, theirs), side_1, centre_1), 2)
            theirs = lax.ppermute(hidden[1], "depth", swap)
            hidden = by(part == 0, hidden[0], theirs, 1)
            other_acts = tie(other_acts, theirs)
        if adding:
            if gathering:
                terms = tie(terms, side_1, centre_1)
            near = add(take(terms, 2), in_2).astype(WIRE)
            swapped = jnp.where(at_end, take(terms, 1), add(take(terms, 0), centre_2))
            swapped = swapped.astype(WIRE)
            centre_3, side_3 = send(near, centre), send(swapped, side)
            if k + 2 <= last:
                payload = take(tie(products[k + 2], near, swapped), 3).astype(WIRE)
                in_1 = send(payload, inward)
            before = (in_2, centre_2)
        if k < 0:
            cotangent = jnp.stack(tie(cotangent, near, swapped))
            cotangent = by(
                core == 0,
                columns_of(cotangent, core * share, share),
                send(columns_of(cotangent, (1 - core) * share, share), pairs),
                1,
            )
            far_weights = exchange_weights(2, (near, swapped))
            tokens = jnp.stack(tie(features, near, swapped), axis=1)
            tokens = (tokens, send(tokens, pairs))
        if k == 0:
            turned = [value.reshape(-1, depth) for value in tie(features, near, swapped)]
            turned = jnp.concatenate(turned).T
            terms = tie(terms, turned)
        if gathering:
            out_2, share_2 = tie((out_2, share_2), before)
            out_3 = send(share_2, outward)
        if adding:
            if gathering:
                terms = tie(terms, out_2, share_2)
            own_sum = jnp.where(at_end, take(terms, 0), take(terms, 1))
            ready = activate(k + 1, add(own_sum, side_3, centre_3))
            if gathering:
                hops = tie((act, side_1, centre_1, out_2, share_2, out_3), ready)
            act, terms = ready, products.get(k + 2)
        else:
            totals = add_gradients(other_acts, 1 - core, totals, pieces[0][1])
            out_3, hidden = lax.optimization_barrier((tie(out_3, totals), hidden))
            own_acts, other_acts = merge(act, side_1, centre_1, out_2, share_2, out_3)
    totals = add_gradients([own_acts], core, totals, pieces[last][1])
    totals = add_gradients([other_acts], 1 - core, totals, pieces[last][1])

    return (hidden[None], *totals)


def contract(picked, piece):
    return lax.dot_general(
        picked, piece, (((0,), (0,)), ((), ())), preferred_element_type=jnp.float32
    )


def local_any(tokens, gate_weight, up_weight, grad_hidden):
    features = lax.all_gather(tokens[0], "row", axis=1, tiled=True)
    columns = gate_weight.shape[1]
    picked = features
    gate_part = jnp.dot(picked, gate_weight, preferred_element_type=jnp.float32)
    up_part = jnp.dot(picked, up_weight, preferred_element_type=jnp.float32)
    summed = lax.psum_scatter(
        jnp.concatenate([gate_part, up_part], axis=1), "col", scatter_dimension=0, tiled=True
    )
    gate_sum = summed[:, :columns]
    up_sum = summed[:, columns:]
    squash = jax.nn.sigmoid(gate_sum)
    hidden = (gate_sum * squash * up_sum).astype(jnp.bfloat16)
    cotangent = grad_hidden[0].astype(jnp.float32)
    gate_act = (cotangent * up_sum * squash * (1.0 + gate_sum * (1.0 - squash))).astype(
        jnp.bfloat16
    )
    up_act = (cotangent * gate_sum * squash).astype(jnp.bfloat16)
    picked = features
    gate_total = contract(picked, lax.all_gather(gate_act, "col", axis=0, tiled=True))
    up_total = contract(picked, lax.all_gather(up_act, "col", axis=0, tiled=True))
    grad_gate, grad_up = (
        lax.psum_scatter(gate_total, "depth", scatter_dimension=1, tiled=True),
        lax.psum_scatter(up_total, "depth", scatter_dimension=1, tiled=True),
    )
    return (hidden[None], grad_gate, grad_up)


def solution(mesh):
    in_specs = (
        P("depth", None, ("col", "row")),
        P("col", "row"),
        P("col", "row"),
        P("depth", "col", "row"),
    )
    out_specs = (P("depth", "col", "row"), P("col", ("row", "depth")), P("col", ("row", "depth")))
    sizes = tuple(mesh.shape[name] for name in ("row", "col", "depth"))
    return jax.shard_map(
        local if sizes == (2, 8, 2) else local_any,
        mesh=mesh,
        in_specs=in_specs,
        out_specs=out_specs,
        check_vma=False,
    )
```

```python
import functools
import math

import jax
import jax.numpy as jnp
from jax import lax
from jax.experimental import pallas as pl
from jax.experimental.pallas import tpu as pltpu
from jax.sharding import PartitionSpec as P

WIRE = jnp.float16
LARGEST_TOKEN, LARGEST_WEIGHT = 6.0, 0.0625
VMEM_LIMIT = 20 * 2**20
NO_COST = pl.CostEstimate(flops=0, bytes_accessed=0, transcendentals=0)
LONG = pl.CostEstimate(flops=6 * 10**9, bytes_accessed=0, transcendentals=0)
SHARES = (5, 2)


def forward_kernel(scale, start, cores, place_ref, *refs):
    tokens, weights = refs[:cores], refs[cores : cores + 2 * cores]
    out_ref, held, arrived = refs[3 * cores :]
    tiles, _, tile = held.shape[1:]
    tile //= 2
    blocks, _, rows, _ = out_ref.shape

    def copy(j, which):
        first = start + j * tile
        if which < 2:
            columns = pl.ds(pl.multiple_of(place_ref[0] * tile + first, tile), tile)
            source = weights[which].at[:, columns]
        else:
            source = weights[which].at[which - 2, :, pl.ds(j * tile, tile)]
        place = pl.ds(which % 2 * tile, tile)
        held_here = held.at[which // 2, j, :, place]
        return pltpu.make_async_copy(source, held_here, arrived.at[which, j])

    for j in range(tiles):
        for which in range(2 * cores):
            copy(j, which).start()
    for j in range(tiles):
        for which in range(2 * cores):
            copy(j, which).wait()
        product = scale * sum(
            jnp.dot(tokens[i][...], held[i, j], preferred_element_type=jnp.float32)
            for i in range(cores)
        )
        for which in range(2):
            half = product[:, which * tile : (which + 1) * tile].reshape(blocks, rows, tile)
            out_ref[:, which, :, j * tile : (j + 1) * tile] = half


def forward(place, tokens, weights, start, width, tile, blocks, scale, cost=NO_COST):
    total, depth = tokens[0].shape
    cores = len(tokens)
    shape = (blocks, 2, total // blocks, width)
    return pl.pallas_call(
        functools.partial(forward_kernel, scale, start, cores),
        out_shape=jax.ShapeDtypeStruct(shape, jnp.float32),
        in_specs=[pl.BlockSpec(memory_space=pltpu.SMEM)]
        + [pl.BlockSpec(memory_space=pltpu.VMEM)] * cores
        + [pl.BlockSpec(memory_space=pl.ANY)] * (2 * cores),
        out_specs=pl.BlockSpec(memory_space=pltpu.VMEM),
        scratch_shapes=[
            pltpu.VMEM((cores, width // tile, depth, 2 * tile), jnp.bfloat16),
            pltpu.SemaphoreType.DMA((2 * cores, width // tile)),
        ],
        compiler_params=pltpu.CompilerParams(vmem_limit_bytes=VMEM_LIMIT),
        cost_estimate=cost,
    )(place, *tokens, *weights)


def gradient_kernel(batches, place_ref, features_ref, *refs):
    acts, outs = refs[:batches], refs[-2:]
    halves = []
    for which in range(2):
        parts = []
        for act_ref in acts:
            blocks, _, _, rows, width = act_ref.shape
            rows = rows * batches // 2
            for i in range(2 // batches):
                part = act_ref[:, 0, which, i * rows : (i + 1) * rows]
                parts.append(part.reshape(blocks * rows, width))
        halves.append(jnp.concatenate(parts))
    both = jnp.dot(
        features_ref[...], jnp.concatenate(halves, axis=1), preferred_element_type=jnp.float32
    )
    for which, out_ref in enumerate(outs):
        out_ref[...] = both[:, which * width : (which + 1) * width]


def gradient(place, features, acts, totals, columns, start, tile):
    depth, total = features.shape
    blocks, cores, _, rows, width = acts[0].shape
    act_spec = pl.BlockSpec((blocks, 1, 2, rows, tile), lambda i, j, place: (0, i, 0, 0, j))
    out_spec = pl.BlockSpec((depth, tile), lambda i, j, place: (0, place[i] + start // tile + j))
    out_shape = jax.ShapeDtypeStruct((depth, columns), jnp.float32)
    in_specs = [pl.BlockSpec((depth, total), lambda i, j, place: (0, 0))]
    in_specs += [act_spec] * len(acts)
    in_specs += [pl.BlockSpec(memory_space=pl.ANY)] * len(totals)
    return pl.pallas_call(
        functools.partial(gradient_kernel, len(acts)),
        out_shape=(out_shape, out_shape),
        grid_spec=pltpu.PrefetchScalarGridSpec(
            num_scalar_prefetch=1,
            grid=(cores, width // tile),
            in_specs=in_specs,
            out_specs=(out_spec, out_spec),
        ),
        input_output_aliases={2 + len(acts) + i: i for i in range(len(totals))},
        compiler_params=pltpu.CompilerParams(vmem_limit_bytes=VMEM_LIMIT),
        cost_estimate=pl.CostEstimate(
            flops=4 * cores * total * depth * width,
            bytes_accessed=cores * (8 * depth + 4 * total) * width + 2 * total * depth,
            transcendentals=0,
        ),
    )(place, features, *acts, *totals)


def gather_kernel(at_end_ref, act, side_1, centre_1, out_2, share_2, out_3, out_ref):
    def fill(*blocks):
        for block, block_ref in enumerate(blocks):
            out_ref[block] = block_ref[...]

    pl.when(at_end_ref[0] == 1)(functools.partial(fill, act, side_1, out_2, out_3))
    pl.when(at_end_ref[0] == 0)(functools.partial(fill, side_1, act, centre_1, share_2))


def gather_blocks(at_end, *hops):
    _, rows, width = hops[0].shape
    spec = pl.BlockSpec((1, rows, width), lambda i, at_end: (i, 0, 0))
    return pl.pallas_call(
        gather_kernel,
        out_shape=jax.ShapeDtypeStruct((4, 2, rows, width), hops[0].dtype),
        grid_spec=pltpu.PrefetchScalarGridSpec(
            num_scalar_prefetch=1,
            grid=(2,),
            in_specs=[spec] * len(hops),
            out_specs=pl.BlockSpec((4, 1, rows, width), lambda i, at_end: (0, i, 0, 0)),
        ),
        compiler_params=pltpu.CompilerParams(vmem_limit_bytes=VMEM_LIMIT),
        cost_estimate=NO_COST,
    )(at_end, *hops)


def tie(value, *after):
    return lax.optimization_barrier((value, after))[0]


def cut(units, shares):
    edges = [round(units * sum(shares[:i]) / sum(shares)) for i in range(len(shares) + 1)]
    return [(a, b - a) for a, b in zip(edges, edges[1:]) if b > a]


def local(tokens, gate_weight, up_weight, grad_hidden):
    line = 4
    row, col, part = (lax.axis_index(name) for name in ("row", "col", "depth"))
    place, core = col // 2, col % 2
    slab = grad_hidden.shape[1]
    rows = 2 * slab
    depth, columns = gate_weight.shape
    half = columns // 2
    share = half // 2
    tile = 256 if share % 256 == 0 else 128
    largest = depth * 2 * line * LARGEST_TOKEN * LARGEST_WEIGHT
    scale = 2.0 ** math.floor(math.log2(65504 / largest))

    swap = [(0, 1), (1, 0)]
    pairs = [(i, i ^ 1) for i in range(2 * line)]

    def between(hops):
        return [(2 * i + c, 2 * j + c) for i, j in hops for c in (0, 1)]

    inward, outward = between([(0, 1), (3, 2)]), between([(1, 0), (2, 3)])
    side, centre = inward + outward, between([(1, 2), (2, 1)])
    at_end = (place == 0) | (place == line - 1)
    at_far = 2 * place >= line

    def send(value, route):
        return lax.ppermute(value, "col", route)

    def wide(value):
        return value.astype(jnp.float32)

    def add(*terms):
        return functools.reduce(jnp.add, map(wide, terms))

    def by(first, mine, theirs, axis):
        return jnp.where(
            first,
            jnp.concatenate([mine, theirs], axis=axis),
            jnp.concatenate([theirs, mine], axis=axis),
        )

    def columns_of(array, start, width):
        return lax.dynamic_slice_in_dim(array, start, width, array.ndim - 1)

    pieces = []
    for begin, count in cut(share // tile, SHARES):
        for batches in ((0, 1),) if pieces else ((0,), (1,)):
            pieces.append((batches, begin * tile, count * tile))
    last = len(pieces) - 1

    def exchange_weights(k, after):
        _, start, width = pieces[k]
        first = part * half + (1 - core) * share + start
        chosen = [
            columns_of(weight, first, width) for weight in tie((gate_weight, up_weight), after)
        ]
        return send(jnp.stack(chosen), pairs)

    mine = tokens[0]
    over_row = lax.ppermute(mine, "row", swap)
    over_depth = lax.ppermute(mine, "depth", swap)
    over_both = lax.ppermute(over_row, "depth", swap)
    own_tile, other_tile = [
        ((part * half + owner * share) // tile).astype(jnp.int32).reshape(1)
        for owner in (core, 1 - core)
    ]

    def arrange(values):
        values = values.reshape(line, rows, depth)
        return jnp.where(at_far, values[::-1], values)

    def own_features(tokens, k, after, wire):
        _, start, width = pieces[k]
        tokens = tie(tokens, after).reshape(-1, depth)
        common = ((gate_weight, up_weight), start, width, tile, line, scale)
        payload = forward(other_tile, [tokens], *common).astype(wire)

        def own(after, cost=NO_COST):
            return forward(own_tile, [tie(tokens, payload, after)], *common, cost)

        return payload, own

    def all_features(tokens, k, after):
        _, start, width = pieces[k]
        tokens = [value.reshape(-1, depth) for value in tie(tokens, after)]
        weights = (gate_weight, up_weight, far_weights, far_weights)
        return forward(own_tile, tokens, weights, start, width, tile, line, scale), None

    def take(terms, block):
        own, theirs = terms
        return own[block] if theirs is None else own[block] + wide(theirs[block])

    over_row = tie(over_row, over_depth)
    features = [arrange(by(row == 0, mine, over_row, 1))]
    theirs, own = own_features(features[0], 0, (), WIRE)
    terms = (own((), LONG), send(theirs, pairs))
    payload = take(terms, 3).astype(WIRE)
    in_1 = send(payload, inward)

    over_depth, over_both = tie((over_depth, over_both), payload)
    features.append(arrange(by(row == 0, over_depth, over_both, 1)))
    theirs, own = own_features(features[1], 1, (), WIRE)
    terms = tie(terms, theirs)

    def activate(k, summed):
        batches, start, width = pieces[k]
        summed = (summed * (1.0 / scale)).reshape(2, len(batches), rows, width)
        gate_sum, up_sum = summed[0], summed[1]
        squash = jax.nn.sigmoid(gate_sum)
        product = (gate_sum * squash * up_sum).astype(jnp.bfloat16)
        for position, batch in enumerate(batches):
            hidden[batch].append(product[position])
        given = jnp.stack([wide(cotangent[b][:, start : start + width]) for b in batches])
        gate_act = given * up_sum * squash * (1.0 + gate_sum * (1.0 - squash))
        up_act = given * gate_sum * squash
        act = jnp.stack([gate_act, up_act]).astype(jnp.bfloat16)
        return act.reshape(2, len(batches) * rows, width)

    def merge(*hops):
        blocks = gather_blocks(at_end.astype(jnp.int32).reshape(1), *hops)
        return blocks, send(blocks, pairs)

    def add_gradients(acts, owner, totals, start):
        where = (owner * (share // tile)).astype(jnp.int32).reshape(1)
        acts = [value[:, None] for value in acts]
        return gradient(where, turned, acts, totals, half, start, tile)

    hidden, totals, merged, products = ([], []), (), [], {}
    act = hops = None
    for k in range(-1, last + 1):
        adding, gathering = k < last, act is not None
        if gathering:
            side_1, centre_1 = send(act, side), send(act, centre)
        if adding:
            if hops is not None:
                merged.append(merge(*hops))
                terms = tie(terms, merged[-1][0])
            if k == 0:
                products[2] = all_features(tokens, 2, act)
                terms = tie(terms, products[2])
            near = take(tie(terms, in_1) if gathering else terms, 2).astype(WIRE)
            far = add(take(tie(terms, near), 3), in_1).astype(WIRE)
            centre_2, in_2 = send(far, centre), send(near, inward)
            before = (in_1,)
        else:
            hidden = jnp.stack([jnp.concatenate(parts, axis=1) for parts in hidden])
            hidden = hidden.reshape(2, 2, slab, share)
            mine = lax.dynamic_index_in_dim(hidden, core, 1, keepdims=False)
            theirs = lax.dynamic_index_in_dim(hidden, 1 - core, 1, keepdims=False)
            theirs = send(theirs, pairs)
            merged.append(merge(*tie(hops, theirs)))
            before = (theirs, merged[-1][0])
        if gathering:
            side_1, centre_1 = tie((side_1, centre_1), before)
            out_2, share_2 = send(centre_1, outward), send(side_1, centre)
        if k < 0:
            products[1] = (own((far, near), LONG), send(theirs, pairs))
            cotangent = tie(grad_hidden[0], far, near)
            cotangent = (
                columns_of(cotangent, part * half, half),
                lax.ppermute(columns_of(cotangent, (1 - part) * half, half), "depth", swap),
            )
            terms = tie(terms, products[1], cotangent[1])
        if not adding:
            own_acts, other_acts = zip(*merged)
            totals = add_gradients(own_acts, core, (), pieces[0][1])
            share_2 = tie(share_2, totals)
            hidden = by(core == 0, *tie((mine, theirs), side_1, centre_1), 2)
            theirs = lax.ppermute(hidden[1], "depth", swap)
            hidden = by(part == 0, hidden[0], theirs, 1)
            other_acts = tie(other_acts, theirs)
        if adding:
            if gathering:
                terms = tie(terms, side_1, centre_1)
            near = add(take(terms, 2), in_2).astype(WIRE)
            swapped = jnp.where(at_end, take(terms, 1), add(take(terms, 0), centre_2))
            swapped = swapped.astype(WIRE)
            centre_3, side_3 = send(near, centre), send(swapped, side)
            if k + 2 <= last:
                payload = take(tie(products[k + 2], near, swapped), 3).astype(WIRE)
                in_1 = send(payload, inward)
            before = (in_2, centre_2)
        if k < 0:
            cotangent = jnp.stack(tie(cotangent, near, swapped))
            cotangent = by(
                core == 0,
                columns_of(cotangent, core * share, share),
                send(columns_of(cotangent, (1 - core) * share, share), pairs),
                1,
            )
            far_weights = exchange_weights(2, (near, swapped))
            tokens = jnp.stack(tie(features, near, swapped), axis=1)
            tokens = (tokens, send(tokens, pairs))
        if k == 0:
            turned = [value.reshape(-1, depth) for value in tie(features, near, swapped)]
            turned = jnp.concatenate(turned).T
            terms = tie(terms, turned)
        if gathering:
            out_2, share_2 = tie((out_2, share_2), before)
            out_3 = send(share_2, outward)
        if adding:
            if gathering:
                terms = tie(terms, out_2, share_2)
            own_sum = jnp.where(at_end, take(terms, 0), take(terms, 1))
            ready = activate(k + 1, add(own_sum, side_3, centre_3))
            if gathering:
                hops = tie((act, side_1, centre_1, out_2, share_2, out_3), ready)
            act, terms = ready, products.get(k + 2)
        else:
            totals = add_gradients(other_acts, 1 - core, totals, pieces[0][1])
            out_3, hidden = lax.optimization_barrier((tie(out_3, totals), hidden))
            own_acts, other_acts = merge(act, side_1, centre_1, out_2, share_2, out_3)
    totals = add_gradients([own_acts], core, totals, pieces[last][1])
    totals = add_gradients([other_acts], 1 - core, totals, pieces[last][1])

    return (hidden[None], *totals)


def contract(picked, piece):
    return lax.dot_general(
        picked, piece, (((0,), (0,)), ((), ())), preferred_element_type=jnp.float32
    )


def local_any(tokens, gate_weight, up_weight, grad_hidden):
    features = lax.all_gather(tokens[0], "row", axis=1, tiled=True)
    columns = gate_weight.shape[1]
    picked = features
    gate_part = jnp.dot(picked, gate_weight, preferred_element_type=jnp.float32)
    up_part = jnp.dot(picked, up_weight, preferred_element_type=jnp.float32)
    summed = lax.psum_scatter(
        jnp.concatenate([gate_part, up_part], axis=1), "col", scatter_dimension=0, tiled=True
    )
    gate_sum = summed[:, :columns]
    up_sum = summed[:, columns:]
    squash = jax.nn.sigmoid(gate_sum)
    hidden = (gate_sum * squash * up_sum).astype(jnp.bfloat16)
    cotangent = grad_hidden[0].astype(jnp.float32)
    gate_act = (cotangent * up_sum * squash * (1.0 + gate_sum * (1.0 - squash))).astype(
        jnp.bfloat16
    )
    up_act = (cotangent * gate_sum * squash).astype(jnp.bfloat16)
    picked = features
    gate_total = contract(picked, lax.all_gather(gate_act, "col", axis=0, tiled=True))
    up_total = contract(picked, lax.all_gather(up_act, "col", axis=0, tiled=True))
    grad_gate, grad_up = (
        lax.psum_scatter(gate_total, "depth", scatter_dimension=1, tiled=True),
        lax.psum_scatter(up_total, "depth", scatter_dimension=1, tiled=True),
    )
    return (hidden[None], grad_gate, grad_up)


def solution(mesh):
    in_specs = (
        P("depth", None, ("col", "row")),
        P("col", "row"),
        P("col", "row"),
        P("depth", "col", "row"),
    )
    out_specs = (P("depth", "col", "row"), P("col", ("row", "depth")), P("col", ("row", "depth")))
    sizes = tuple(mesh.shape[name] for name in ("row", "col", "depth"))
    return jax.shard_map(
        local if sizes == (2, 8, 2) else local_any,
        mesh=mesh,
        in_specs=in_specs,
        out_specs=out_specs,
        check_vma=False,
    )
```

```python
import functools
import math

import jax
import jax.numpy as jnp
from jax import lax
from jax.experimental import pallas as pl
from jax.experimental.pallas import tpu as pltpu
from jax.sharding import PartitionSpec as P

WIRE = jnp.float16
LARGEST_TOKEN, LARGEST_WEIGHT = 6.0, 0.0625
VMEM_LIMIT = 20 * 2**20
FORWARD_VMEM_LIMIT = 48 * 2**20
NO_COST = pl.CostEstimate(flops=0, bytes_accessed=0, transcendentals=0)
LONG = pl.CostEstimate(flops=6 * 10**9, bytes_accessed=0, transcendentals=0)
SHARES = (5, 2)


def forward_kernel(scale, start, cores, place_ref, *refs):
    tokens, weights = refs[:cores], refs[cores : cores + 2 * cores]
    out_ref, held, arrived = refs[3 * cores :]
    tiles, _, tile = held.shape[1:]
    tile //= 2
    blocks, _, rows, _ = out_ref.shape

    def copy(j, which):
        first = start + j * tile
        if which < 2:
            columns = pl.ds(pl.multiple_of(place_ref[0] * tile + first, tile), tile)
            source = weights[which].at[:, columns]
        else:
            source = weights[which].at[which - 2, :, pl.ds(j * tile, tile)]
        place = pl.ds(which % 2 * tile, tile)
        held_here = held.at[which // 2, j, :, place]
        return pltpu.make_async_copy(source, held_here, arrived.at[which, j])

    for j in range(tiles):
        for which in range(2 * cores):
            copy(j, which).start()
    for j in range(tiles):
        for which in range(2 * cores):
            copy(j, which).wait()
        product = scale * sum(
            jnp.dot(tokens[i][...], held[i, j], preferred_element_type=jnp.float32)
            for i in range(cores)
        )
        for which in range(2):
            half = product[:, which * tile : (which + 1) * tile].reshape(blocks, rows, tile)
            out_ref[:, which, :, j * tile : (j + 1) * tile] = half


def forward(place, tokens, weights, start, width, tile, blocks, scale, cost=NO_COST):
    total, depth = tokens[0].shape
    cores = len(tokens)
    shape = (blocks, 2, total // blocks, width)
    return pl.pallas_call(
        functools.partial(forward_kernel, scale, start, cores),
        out_shape=jax.ShapeDtypeStruct(shape, jnp.float32),
        in_specs=[pl.BlockSpec(memory_space=pltpu.SMEM)]
        + [pl.BlockSpec(memory_space=pltpu.VMEM)] * cores
        + [pl.BlockSpec(memory_space=pl.ANY)] * (2 * cores),
        out_specs=pl.BlockSpec(memory_space=pltpu.VMEM),
        scratch_shapes=[
            pltpu.VMEM((cores, width // tile, depth, 2 * tile), jnp.bfloat16),
            pltpu.SemaphoreType.DMA((2 * cores, width // tile)),
        ],
        compiler_params=pltpu.CompilerParams(vmem_limit_bytes=FORWARD_VMEM_LIMIT),
        cost_estimate=cost,
    )(place, *tokens, *weights)


def gradient_kernel(batches, place_ref, features_ref, *refs):
    acts, outs = refs[:batches], refs[-2:]
    halves = []
    for which in range(2):
        parts = []
        for act_ref in acts:
            blocks, _, _, rows, width = act_ref.shape
            rows = rows * batches // 2
            for i in range(2 // batches):
                part = act_ref[:, 0, which, i * rows : (i + 1) * rows]
                parts.append(part.reshape(blocks * rows, width))
        halves.append(jnp.concatenate(parts))
    both = jnp.dot(
        features_ref[...], jnp.concatenate(halves, axis=1), preferred_element_type=jnp.float32
    )
    for which, out_ref in enumerate(outs):
        out_ref[...] = both[:, which * width : (which + 1) * width]


def gradient(place, features, acts, totals, columns, start, tile):
    depth, total = features.shape
    blocks, cores, _, rows, width = acts[0].shape
    act_spec = pl.BlockSpec((blocks, 1, 2, rows, tile), lambda i, j, place: (0, i, 0, 0, j))
    out_spec = pl.BlockSpec((depth, tile), lambda i, j, place: (0, place[i] + start // tile + j))
    out_shape = jax.ShapeDtypeStruct((depth, columns), jnp.float32)
    in_specs = [pl.BlockSpec((depth, total), lambda i, j, place: (0, 0))]
    in_specs += [act_spec] * len(acts)
    in_specs += [pl.BlockSpec(memory_space=pl.ANY)] * len(totals)
    return pl.pallas_call(
        functools.partial(gradient_kernel, len(acts)),
        out_shape=(out_shape, out_shape),
        grid_spec=pltpu.PrefetchScalarGridSpec(
            num_scalar_prefetch=1,
            grid=(cores, width // tile),
            in_specs=in_specs,
            out_specs=(out_spec, out_spec),
        ),
        input_output_aliases={2 + len(acts) + i: i for i in range(len(totals))},
        compiler_params=pltpu.CompilerParams(vmem_limit_bytes=VMEM_LIMIT),
        cost_estimate=pl.CostEstimate(
            flops=4 * cores * total * depth * width,
            bytes_accessed=cores * (8 * depth + 4 * total) * width + 2 * total * depth,
            transcendentals=0,
        ),
    )(place, features, *acts, *totals)


def gather_kernel(at_end_ref, act, side_1, centre_1, out_2, share_2, out_3, out_ref):
    def fill(*blocks):
        for block, block_ref in enumerate(blocks):
            out_ref[block] = block_ref[...]

    pl.when(at_end_ref[0] == 1)(functools.partial(fill, act, side_1, out_2, out_3))
    pl.when(at_end_ref[0] == 0)(functools.partial(fill, side_1, act, centre_1, share_2))


def gather_blocks(at_end, *hops):
    _, rows, width = hops[0].shape
    spec = pl.BlockSpec((1, rows, width), lambda i, at_end: (i, 0, 0))
    return pl.pallas_call(
        gather_kernel,
        out_shape=jax.ShapeDtypeStruct((4, 2, rows, width), hops[0].dtype),
        grid_spec=pltpu.PrefetchScalarGridSpec(
            num_scalar_prefetch=1,
            grid=(2,),
            in_specs=[spec] * len(hops),
            out_specs=pl.BlockSpec((4, 1, rows, width), lambda i, at_end: (0, i, 0, 0)),
        ),
        compiler_params=pltpu.CompilerParams(vmem_limit_bytes=VMEM_LIMIT),
        cost_estimate=NO_COST,
    )(at_end, *hops)


def tie(value, *after):
    return lax.optimization_barrier((value, after))[0]


def cut(units, shares):
    edges = [round(units * sum(shares[:i]) / sum(shares)) for i in range(len(shares) + 1)]
    return [(a, b - a) for a, b in zip(edges, edges[1:]) if b > a]


def local(tokens, gate_weight, up_weight, grad_hidden):
    line = 4
    row, col, part = (lax.axis_index(name) for name in ("row", "col", "depth"))
    place, core = col // 2, col % 2
    slab = grad_hidden.shape[1]
    rows = 2 * slab
    depth, columns = gate_weight.shape
    half = columns // 2
    share = half // 2
    tile = 256 if share % 256 == 0 else 128
    largest = depth * 2 * line * LARGEST_TOKEN * LARGEST_WEIGHT
    scale = 2.0 ** math.floor(math.log2(65504 / largest))

    swap = [(0, 1), (1, 0)]
    pairs = [(i, i ^ 1) for i in range(2 * line)]

    def between(hops):
        return [(2 * i + c, 2 * j + c) for i, j in hops for c in (0, 1)]

    inward, outward = between([(0, 1), (3, 2)]), between([(1, 0), (2, 3)])
    side, centre = inward + outward, between([(1, 2), (2, 1)])
    at_end = (place == 0) | (place == line - 1)
    at_far = 2 * place >= line

    def send(value, route):
        return lax.ppermute(value, "col", route)

    def wide(value):
        return value.astype(jnp.float32)

    def add(*terms):
        return functools.reduce(jnp.add, map(wide, terms))

    def by(first, mine, theirs, axis):
        return jnp.where(
            first,
            jnp.concatenate([mine, theirs], axis=axis),
            jnp.concatenate([theirs, mine], axis=axis),
        )

    def columns_of(array, start, width):
        return lax.dynamic_slice_in_dim(array, start, width, array.ndim - 1)

    pieces = []
    for begin, count in cut(share // tile, SHARES):
        for batches in ((0, 1),) if pieces else ((0,), (1,)):
            pieces.append((batches, begin * tile, count * tile))
    last = len(pieces) - 1

    def exchange_weights(k, after):
        _, start, width = pieces[k]
        first = part * half + (1 - core) * share + start
        chosen = [
            columns_of(weight, first, width) for weight in tie((gate_weight, up_weight), after)
        ]
        return send(jnp.stack(chosen), pairs)

    mine = tokens[0]
    over_row = lax.ppermute(mine, "row", swap)
    over_depth = lax.ppermute(mine, "depth", swap)
    over_both = lax.ppermute(over_row, "depth", swap)
    own_tile, other_tile = [
        ((part * half + owner * share) // tile).astype(jnp.int32).reshape(1)
        for owner in (core, 1 - core)
    ]

    def arrange(values):
        values = values.reshape(line, rows, depth)
        return jnp.where(at_far, values[::-1], values)

    def own_features(tokens, k, after, wire):
        _, start, width = pieces[k]
        tokens = tie(tokens, after).reshape(-1, depth)
        common = ((gate_weight, up_weight), start, width, tile, line, scale)
        payload = forward(other_tile, [tokens], *common).astype(wire)

        def own(after, cost=NO_COST):
            return forward(own_tile, [tie(tokens, payload, after)], *common, cost)

        return payload, own

    def all_features(tokens, k, after):
        _, start, width = pieces[k]
        tokens = [value.reshape(-1, depth) for value in tie(tokens, after)]
        weights = (gate_weight, up_weight, far_weights, far_weights)
        return forward(own_tile, tokens, weights, start, width, tile, line, scale), None

    def take(terms, block):
        own, theirs = terms
        return own[block] if theirs is None else own[block] + wide(theirs[block])

    over_row = tie(over_row, over_depth)
    features = [arrange(by(row == 0, mine, over_row, 1))]
    theirs, own = own_features(features[0], 0, (), WIRE)
    terms = (own((), LONG), send(theirs, pairs))
    payload = take(terms, 3).astype(WIRE)
    in_1 = send(payload, inward)

    over_depth, over_both = tie((over_depth, over_both), payload)
    features.append(arrange(by(row == 0, over_depth, over_both, 1)))
    theirs, own = own_features(features[1], 1, (), WIRE)
    terms = tie(terms, theirs)

    def activate(k, summed):
        batches, start, width = pieces[k]
        summed = (summed * (1.0 / scale)).reshape(2, len(batches), rows, width)
        gate_sum, up_sum = summed[0], summed[1]
        squash = jax.nn.sigmoid(gate_sum)
        product = (gate_sum * squash * up_sum).astype(jnp.bfloat16)
        for position, batch in enumerate(batches):
            hidden[batch].append(product[position])
        given = jnp.stack([wide(cotangent[b][:, start : start + width]) for b in batches])
        gate_act = given * up_sum * squash * (1.0 + gate_sum * (1.0 - squash))
        up_act = given * gate_sum * squash
        act = jnp.stack([gate_act, up_act]).astype(jnp.bfloat16)
        return act.reshape(2, len(batches) * rows, width)

    def merge(*hops):
        blocks = gather_blocks(at_end.astype(jnp.int32).reshape(1), *hops)
        return blocks, send(blocks, pairs)

    def add_gradients(acts, owner, totals, start):
        where = (owner * (share // tile)).astype(jnp.int32).reshape(1)
        acts = [value[:, None] for value in acts]
        return gradient(where, turned, acts, totals, half, start, tile)

    hidden, totals, merged, products = ([], []), (), [], {}
    act = hops = None
    for k in range(-1, last + 1):
        adding, gathering = k < last, act is not None
        if gathering:
            side_1, centre_1 = send(act, side), send(act, centre)
        if adding:
            if hops is not None:
                merged.append(merge(*hops))
                terms = tie(terms, merged[-1][0])
            if k == 0:
                products[2] = all_features(tokens, 2, act)
                terms = tie(terms, products[2])
            near = take(tie(terms, in_1) if gathering else terms, 2).astype(WIRE)
            far = add(take(tie(terms, near), 3), in_1).astype(WIRE)
            centre_2, in_2 = send(far, centre), send(near, inward)
            before = (in_1,)
        else:
            hidden = jnp.stack([jnp.concatenate(parts, axis=1) for parts in hidden])
            hidden = hidden.reshape(2, 2, slab, share)
            mine = lax.dynamic_index_in_dim(hidden, core, 1, keepdims=False)
            theirs = lax.dynamic_index_in_dim(hidden, 1 - core, 1, keepdims=False)
            theirs = send(theirs, pairs)
            merged.append(merge(*tie(hops, theirs)))
            before = (theirs, merged[-1][0])
        if gathering:
            side_1, centre_1 = tie((side_1, centre_1), before)
            out_2, share_2 = send(centre_1, outward), send(side_1, centre)
        if k < 0:
            products[1] = (own((far, near), LONG), send(theirs, pairs))
            cotangent = tie(grad_hidden[0], far, near)
            cotangent = (
                columns_of(cotangent, part * half, half),
                lax.ppermute(columns_of(cotangent, (1 - part) * half, half), "depth", swap),
            )
            terms = tie(terms, products[1], cotangent[1])
        if not adding:
            own_acts, other_acts = zip(*merged)
            totals = add_gradients(own_acts, core, (), pieces[0][1])
            share_2 = tie(share_2, totals)
            hidden = by(core == 0, *tie((mine, theirs), side_1, centre_1), 2)
            theirs = lax.ppermute(hidden[1], "depth", swap)
            hidden = by(part == 0, hidden[0], theirs, 1)
            other_acts = tie(other_acts, theirs)
        if adding:
            if gathering:
                terms = tie(terms, side_1, centre_1)
            near = add(take(terms, 2), in_2).astype(WIRE)
            swapped = jnp.where(at_end, take(terms, 1), add(take(terms, 0), centre_2))
            swapped = swapped.astype(WIRE)
            centre_3, side_3 = send(near, centre), send(swapped, side)
            if k + 2 <= last:
                payload = take(tie(products[k + 2], near, swapped), 3).astype(WIRE)
                in_1 = send(payload, inward)
            before = (in_2, centre_2)
        if k < 0:
            cotangent = jnp.stack(tie(cotangent, near, swapped))
            cotangent = by(
                core == 0,
                columns_of(cotangent, core * share, share),
                send(columns_of(cotangent, (1 - core) * share, share), pairs),
                1,
            )
            far_weights = exchange_weights(2, (near, swapped))
            tokens = jnp.stack(tie(features, near, swapped), axis=1)
            tokens = (tokens, send(tokens, pairs))
        if k == 0:
            turned = [value.reshape(-1, depth) for value in tie(features, near, swapped)]
            turned = jnp.concatenate(turned).T
            terms = tie(terms, turned)
        if gathering:
            out_2, share_2 = tie((out_2, share_2), before)
            out_3 = send(share_2, outward)
        if adding:
            if gathering:
                terms = tie(terms, out_2, share_2)
            own_sum = jnp.where(at_end, take(terms, 0), take(terms, 1))
            ready = activate(k + 1, add(own_sum, side_3, centre_3))
            if gathering:
                hops = tie((act, side_1, centre_1, out_2, share_2, out_3), ready)
            act, terms = ready, products.get(k + 2)
        else:
            totals = add_gradients(other_acts, 1 - core, totals, pieces[0][1])
            out_3, hidden = lax.optimization_barrier((tie(out_3, totals), hidden))
            own_acts, other_acts = merge(act, side_1, centre_1, out_2, share_2, out_3)
    totals = add_gradients([own_acts], core, totals, pieces[last][1])
    totals = add_gradients([other_acts], 1 - core, totals, pieces[last][1])

    return (hidden[None], *totals)


def contract(picked, piece):
    return lax.dot_general(
        picked, piece, (((0,), (0,)), ((), ())), preferred_element_type=jnp.float32
    )


def local_any(tokens, gate_weight, up_weight, grad_hidden):
    features = lax.all_gather(tokens[0], "row", axis=1, tiled=True)
    columns = gate_weight.shape[1]
    picked = features
    gate_part = jnp.dot(picked, gate_weight, preferred_element_type=jnp.float32)
    up_part = jnp.dot(picked, up_weight, preferred_element_type=jnp.float32)
    summed = lax.psum_scatter(
        jnp.concatenate([gate_part, up_part], axis=1), "col", scatter_dimension=0, tiled=True
    )
    gate_sum = summed[:, :columns]
    up_sum = summed[:, columns:]
    squash = jax.nn.sigmoid(gate_sum)
    hidden = (gate_sum * squash * up_sum).astype(jnp.bfloat16)
    cotangent = grad_hidden[0].astype(jnp.float32)
    gate_act = (cotangent * up_sum * squash * (1.0 + gate_sum * (1.0 - squash))).astype(
        jnp.bfloat16
    )
    up_act = (cotangent * gate_sum * squash).astype(jnp.bfloat16)
    picked = features
    gate_total = contract(picked, lax.all_gather(gate_act, "col", axis=0, tiled=True))
    up_total = contract(picked, lax.all_gather(up_act, "col", axis=0, tiled=True))
    grad_gate, grad_up = (
        lax.psum_scatter(gate_total, "depth", scatter_dimension=1, tiled=True),
        lax.psum_scatter(up_total, "depth", scatter_dimension=1, tiled=True),
    )
    return (hidden[None], grad_gate, grad_up)


def solution(mesh):
    in_specs = (
        P("depth", None, ("col", "row")),
        P("col", "row"),
        P("col", "row"),
        P("depth", "col", "row"),
    )
    out_specs = (P("depth", "col", "row"), P("col", ("row", "depth")), P("col", ("row", "depth")))
    sizes = tuple(mesh.shape[name] for name in ("row", "col", "depth"))
    return jax.shard_map(
        local if sizes == (2, 8, 2) else local_any,
        mesh=mesh,
        in_specs=in_specs,
        out_specs=out_specs,
        check_vma=False,
    )
```

```python
import functools
import math

import jax
import jax.numpy as jnp
from jax import lax
from jax.experimental import pallas as pl
from jax.experimental.pallas import tpu as pltpu
from jax.sharding import PartitionSpec as P

WIRE = jnp.float16
LARGEST_TOKEN, LARGEST_WEIGHT = 6.0, 0.0625
VMEM_LIMIT = 20 * 2**20
FORWARD_VMEM_LIMIT = 48 * 2**20
NO_COST = pl.CostEstimate(flops=0, bytes_accessed=0, transcendentals=0)
LONG = pl.CostEstimate(flops=6 * 10**9, bytes_accessed=0, transcendentals=0)
SHARES = (5, 2)


def forward_kernel(scale, start, cores, place_ref, *refs):
    tokens, weights = refs[:cores], refs[cores : cores + 2 * cores]
    out_ref, held, arrived = refs[3 * cores :]
    tiles, _, tile = held.shape[1:]
    tile //= 2
    blocks, _, rows, _ = out_ref.shape

    def copy(j, which):
        first = start + j * tile
        if which < 2:
            columns = pl.ds(pl.multiple_of(place_ref[0] * tile + first, tile), tile)
            source = weights[which].at[:, columns]
        else:
            source = weights[which].at[which - 2, :, pl.ds(j * tile, tile)]
        place = pl.ds(which % 2 * tile, tile)
        held_here = held.at[which // 2, j, :, place]
        return pltpu.make_async_copy(source, held_here, arrived.at[which, j])

    for j in range(tiles):
        for which in range(2 * cores):
            copy(j, which).start()
    for j in range(tiles):
        for which in range(2 * cores):
            copy(j, which).wait()
        product = scale * sum(
            jnp.dot(tokens[i][...], held[i, j], preferred_element_type=jnp.float32)
            for i in range(cores)
        )
        for which in range(2):
            half = product[:, which * tile : (which + 1) * tile].reshape(blocks, rows, tile)
            out_ref[:, which, :, j * tile : (j + 1) * tile] = half


def forward(place, tokens, weights, start, width, tile, blocks, scale, cost=NO_COST):
    total, depth = tokens[0].shape
    cores = len(tokens)
    shape = (blocks, 2, total // blocks, width)
    return pl.pallas_call(
        functools.partial(forward_kernel, scale, start, cores),
        out_shape=jax.ShapeDtypeStruct(shape, jnp.float32),
        in_specs=[pl.BlockSpec(memory_space=pltpu.SMEM)]
        + [pl.BlockSpec(memory_space=pltpu.VMEM)] * cores
        + [pl.BlockSpec(memory_space=pl.ANY)] * (2 * cores),
        out_specs=pl.BlockSpec(memory_space=pltpu.VMEM),
        scratch_shapes=[
            pltpu.VMEM((cores, width // tile, depth, 2 * tile), jnp.bfloat16),
            pltpu.SemaphoreType.DMA((2 * cores, width // tile)),
        ],
        compiler_params=pltpu.CompilerParams(vmem_limit_bytes=FORWARD_VMEM_LIMIT),
        cost_estimate=cost,
    )(place, *tokens, *weights)


def gradient_kernel(batches, place_ref, features_ref, *refs):
    acts, outs = refs[:batches], refs[-2:]
    halves = []
    for which in range(2):
        parts = []
        for act_ref in acts:
            blocks, _, _, rows, width = act_ref.shape
            rows = rows * batches // 2
            for i in range(2 // batches):
                part = act_ref[:, 0, which, i * rows : (i + 1) * rows]
                parts.append(part.reshape(blocks * rows, width))
        halves.append(jnp.concatenate(parts))
    both = jnp.dot(
        features_ref[...], jnp.concatenate(halves, axis=1), preferred_element_type=jnp.float32
    )
    for which, out_ref in enumerate(outs):
        out_ref[...] = both[:, which * width : (which + 1) * width]


def gradient(place, features, acts, totals, columns, start, tile):
    depth, total = features.shape
    blocks, cores, _, rows, width = acts[0].shape
    act_spec = pl.BlockSpec((blocks, 1, 2, rows, tile), lambda i, j, place: (0, i, 0, 0, j))
    out_spec = pl.BlockSpec((depth, tile), lambda i, j, place: (0, place[i] + start // tile + j))
    out_shape = jax.ShapeDtypeStruct((depth, columns), jnp.float32)
    in_specs = [pl.BlockSpec((depth, total), lambda i, j, place: (0, 0))]
    in_specs += [act_spec] * len(acts)
    in_specs += [pl.BlockSpec(memory_space=pl.ANY)] * len(totals)
    return pl.pallas_call(
        functools.partial(gradient_kernel, len(acts)),
        out_shape=(out_shape, out_shape),
        grid_spec=pltpu.PrefetchScalarGridSpec(
            num_scalar_prefetch=1,
            grid=(cores, width // tile),
            in_specs=in_specs,
            out_specs=(out_spec, out_spec),
        ),
        input_output_aliases={2 + len(acts) + i: i for i in range(len(totals))},
        compiler_params=pltpu.CompilerParams(vmem_limit_bytes=VMEM_LIMIT),
        cost_estimate=pl.CostEstimate(
            flops=4 * cores * total * depth * width,
            bytes_accessed=cores * (8 * depth + 4 * total) * width + 2 * total * depth,
            transcendentals=0,
        ),
    )(place, features, *acts, *totals)


def gather_kernel(at_end_ref, act, side_1, centre_1, out_2, share_2, out_3, out_ref):
    def fill(*blocks):
        for block, block_ref in enumerate(blocks):
            out_ref[block] = block_ref[...]

    pl.when(at_end_ref[0] == 1)(functools.partial(fill, act, side_1, out_2, out_3))
    pl.when(at_end_ref[0] == 0)(functools.partial(fill, side_1, act, centre_1, share_2))


def gather_blocks(at_end, *hops):
    _, rows, width = hops[0].shape
    spec = pl.BlockSpec((1, rows, width), lambda i, at_end: (i, 0, 0))
    return pl.pallas_call(
        gather_kernel,
        out_shape=jax.ShapeDtypeStruct((4, 2, rows, width), hops[0].dtype),
        grid_spec=pltpu.PrefetchScalarGridSpec(
            num_scalar_prefetch=1,
            grid=(2,),
            in_specs=[spec] * len(hops),
            out_specs=pl.BlockSpec((4, 1, rows, width), lambda i, at_end: (0, i, 0, 0)),
        ),
        compiler_params=pltpu.CompilerParams(vmem_limit_bytes=VMEM_LIMIT),
        cost_estimate=NO_COST,
    )(at_end, *hops)


def tie(value, *after):
    return lax.optimization_barrier((value, after))[0]


def cut(units, shares):
    edges = [round(units * sum(shares[:i]) / sum(shares)) for i in range(len(shares) + 1)]
    return [(a, b - a) for a, b in zip(edges, edges[1:]) if b > a]


def local(tokens, gate_weight, up_weight, grad_hidden):
    line = 4
    row, col, part = (lax.axis_index(name) for name in ("row", "col", "depth"))
    place, core = col // 2, col % 2
    slab = grad_hidden.shape[1]
    rows = 2 * slab
    depth, columns = gate_weight.shape
    half = columns // 2
    share = half // 2
    tile = 256 if share % 256 == 0 else 128
    largest = depth * 2 * line * LARGEST_TOKEN * LARGEST_WEIGHT
    scale = 2.0 ** math.floor(math.log2(65504 / largest))

    swap = [(0, 1), (1, 0)]
    pairs = [(i, i ^ 1) for i in range(2 * line)]

    def between(hops):
        return [(2 * i + c, 2 * j + c) for i, j in hops for c in (0, 1)]

    inward, outward = between([(0, 1), (3, 2)]), between([(1, 0), (2, 3)])
    side, centre = inward + outward, between([(1, 2), (2, 1)])
    at_end = (place == 0) | (place == line - 1)
    at_far = 2 * place >= line

    def send(value, route):
        return lax.ppermute(value, "col", route)

    def wide(value):
        return value.astype(jnp.float32)

    def add(*terms):
        return functools.reduce(jnp.add, map(wide, terms))

    def by(first, mine, theirs, axis):
        return jnp.where(
            first,
            jnp.concatenate([mine, theirs], axis=axis),
            jnp.concatenate([theirs, mine], axis=axis),
        )

    def columns_of(array, start, width):
        return lax.dynamic_slice_in_dim(array, start, width, array.ndim - 1)

    pieces = []
    for begin, count in cut(share // tile, SHARES):
        for batches in ((0, 1),) if pieces else ((0,), (1,)):
            pieces.append((batches, begin * tile, count * tile))
    last = len(pieces) - 1

    def exchange_weights(k, after):
        _, start, width = pieces[k]
        first = part * half + (1 - core) * share + start
        chosen = [
            columns_of(weight, first, width) for weight in tie((gate_weight, up_weight), after)
        ]
        return send(jnp.stack(chosen), pairs)

    mine = tokens[0]
    over_row = lax.ppermute(mine, "row", swap)
    over_depth = lax.ppermute(mine, "depth", swap)
    over_both = lax.ppermute(over_row, "depth", swap)
    own_tile, other_tile = [
        ((part * half + owner * share) // tile).astype(jnp.int32).reshape(1)
        for owner in (core, 1 - core)
    ]

    def arrange(values):
        values = values.reshape(line, rows, depth)
        return jnp.where(at_far, values[::-1], values)

    def own_features(tokens, k, after, wire):
        _, start, width = pieces[k]
        tokens = tie(tokens, after).reshape(-1, depth)
        common = ((gate_weight, up_weight), start, width, tile, line, scale)
        payload = forward(other_tile, [tokens], *common).astype(wire)

        def own(after, cost=NO_COST):
            return forward(own_tile, [tie(tokens, payload, after)], *common, cost)

        return payload, own

    def all_features(tokens, k, after):
        _, start, width = pieces[k]
        tokens = [value.reshape(-1, depth) for value in tie(tokens, after)]
        weights = (gate_weight, up_weight, far_weights, far_weights)
        return forward(own_tile, tokens, weights, start, width, tile, line, scale), None

    def take(terms, block):
        own, theirs = terms
        return own[block] if theirs is None else own[block] + wide(theirs[block])

    over_row = tie(over_row, over_depth)
    features = [arrange(by(row == 0, mine, over_row, 1))]
    theirs, own = own_features(features[0], 0, (), WIRE)
    terms = (own((), LONG), send(theirs, pairs))
    payload = take(terms, 3).astype(WIRE)
    in_1 = send(payload, inward)

    over_depth, over_both = tie((over_depth, over_both), payload)
    features.append(arrange(by(row == 0, over_depth, over_both, 1)))
    theirs, own = own_features(features[1], 1, (), WIRE)
    terms = tie(terms, theirs)

    def activate(k, summed):
        batches, start, width = pieces[k]
        summed = (summed * (1.0 / scale)).reshape(2, len(batches), rows, width)
        gate_sum, up_sum = summed[0], summed[1]
        squash = jax.nn.sigmoid(gate_sum)
        product = (gate_sum * squash * up_sum).astype(jnp.bfloat16)
        for position, batch in enumerate(batches):
            hidden[batch].append(product[position])
        given = jnp.stack([wide(cotangent[b][:, start : start + width]) for b in batches])
        gate_act = given * up_sum * squash * (1.0 + gate_sum * (1.0 - squash))
        up_act = given * gate_sum * squash
        act = jnp.stack([gate_act, up_act]).astype(jnp.bfloat16)
        return act.reshape(2, len(batches) * rows, width)

    def merge(*hops):
        blocks = gather_blocks(at_end.astype(jnp.int32).reshape(1), *hops)
        return blocks, send(blocks, pairs)

    def add_gradients(acts, owner, totals, start):
        where = (owner * (share // tile)).astype(jnp.int32).reshape(1)
        acts = [value[:, None] for value in acts]
        return gradient(where, turned, acts, totals, half, start, tile)

    hidden, totals, merged, products = ([], []), (), [], {}
    act = hops = None
    for k in range(-1, last + 1):
        adding, gathering = k < last, act is not None
        if gathering:
            side_1, centre_1 = send(act, side), send(act, centre)
        if adding:
            if hops is not None:
                merged.append(merge(*hops))
                terms = tie(terms, merged[-1][0])
            if k == 0:
                terms = tie(terms, far_weights, tokens[1])
            near = take(tie(terms, in_1) if gathering else terms, 2).astype(WIRE)
            far = add(take(tie(terms, near), 3), in_1).astype(WIRE)
            centre_2, in_2 = send(far, centre), send(near, inward)
            before = (in_1,)
        else:
            hidden = jnp.stack([jnp.concatenate(parts, axis=1) for parts in hidden])
            hidden = hidden.reshape(2, 2, slab, share)
            mine = lax.dynamic_index_in_dim(hidden, core, 1, keepdims=False)
            theirs = lax.dynamic_index_in_dim(hidden, 1 - core, 1, keepdims=False)
            theirs = send(theirs, pairs)
            merged.append(merge(*tie(hops, theirs)))
            before = (theirs, merged[-1][0])
        if gathering:
            side_1, centre_1 = tie((side_1, centre_1), before)
            out_2, share_2 = send(centre_1, outward), send(side_1, centre)
        if k == 0:
            products[2] = all_features(tokens, 2, (side_1, centre_1, far, near))
            terms = tie(terms, products[2])
        if k < 0:
            products[1] = (own((far, near), LONG), send(theirs, pairs))
            cotangent = tie(grad_hidden[0], far, near)
            cotangent = (
                columns_of(cotangent, part * half, half),
                lax.ppermute(columns_of(cotangent, (1 - part) * half, half), "depth", swap),
            )
            terms = tie(terms, products[1], cotangent[1])
        if not adding:
            own_acts, other_acts = zip(*merged)
            totals = add_gradients(own_acts, core, (), pieces[0][1])
            share_2 = tie(share_2, totals)
            hidden = by(core == 0, *tie((mine, theirs), side_1, centre_1), 2)
            theirs = lax.ppermute(hidden[1], "depth", swap)
            hidden = by(part == 0, hidden[0], theirs, 1)
            other_acts = tie(other_acts, theirs)
        if adding:
            if gathering:
                terms = tie(terms, side_1, centre_1)
            near = add(take(terms, 2), in_2).astype(WIRE)
            swapped = jnp.where(at_end, take(terms, 1), add(take(terms, 0), centre_2))
            swapped = swapped.astype(WIRE)
            centre_3, side_3 = send(near, centre), send(swapped, side)
            if k + 2 <= last:
                payload = take(tie(products[k + 2], near, swapped), 3).astype(WIRE)
                in_1 = send(payload, inward)
            before = (in_2, centre_2)
        if k < 0:
            cotangent = jnp.stack(tie(cotangent, near, swapped))
            cotangent = by(
                core == 0,
                columns_of(cotangent, core * share, share),
                send(columns_of(cotangent, (1 - core) * share, share), pairs),
                1,
            )
            far_weights = exchange_weights(2, (near, swapped))
            tokens = jnp.stack(tie(features, near, swapped), axis=1)
            tokens = (tokens, send(tokens, pairs))
        if k == 0:
            turned = [value.reshape(-1, depth) for value in tie(features, near, swapped)]
            turned = jnp.concatenate(turned).T
            terms = tie(terms, turned)
        if gathering:
            out_2, share_2 = tie((out_2, share_2), before)
            out_3 = send(share_2, outward)
        if adding:
            if gathering:
                terms = tie(terms, out_2, share_2)
            own_sum = jnp.where(at_end, take(terms, 0), take(terms, 1))
            ready = activate(k + 1, add(own_sum, side_3, centre_3))
            if gathering:
                hops = tie((act, side_1, centre_1, out_2, share_2, out_3), ready)
            act, terms = ready, products.get(k + 2)
        else:
            totals = add_gradients(other_acts, 1 - core, totals, pieces[0][1])
            out_3, hidden = lax.optimization_barrier((tie(out_3, totals), hidden))
            own_acts, other_acts = merge(act, side_1, centre_1, out_2, share_2, out_3)
    totals = add_gradients([own_acts], core, totals, pieces[last][1])
    totals = add_gradients([other_acts], 1 - core, totals, pieces[last][1])

    return (hidden[None], *totals)


def contract(picked, piece):
    return lax.dot_general(
        picked, piece, (((0,), (0,)), ((), ())), preferred_element_type=jnp.float32
    )


def local_any(tokens, gate_weight, up_weight, grad_hidden):
    features = lax.all_gather(tokens[0], "row", axis=1, tiled=True)
    columns = gate_weight.shape[1]
    picked = features
    gate_part = jnp.dot(picked, gate_weight, preferred_element_type=jnp.float32)
    up_part = jnp.dot(picked, up_weight, preferred_element_type=jnp.float32)
    summed = lax.psum_scatter(
        jnp.concatenate([gate_part, up_part], axis=1), "col", scatter_dimension=0, tiled=True
    )
    gate_sum = summed[:, :columns]
    up_sum = summed[:, columns:]
    squash = jax.nn.sigmoid(gate_sum)
    hidden = (gate_sum * squash * up_sum).astype(jnp.bfloat16)
    cotangent = grad_hidden[0].astype(jnp.float32)
    gate_act = (cotangent * up_sum * squash * (1.0 + gate_sum * (1.0 - squash))).astype(
        jnp.bfloat16
    )
    up_act = (cotangent * gate_sum * squash).astype(jnp.bfloat16)
    picked = features
    gate_total = contract(picked, lax.all_gather(gate_act, "col", axis=0, tiled=True))
    up_total = contract(picked, lax.all_gather(up_act, "col", axis=0, tiled=True))
    grad_gate, grad_up = (
        lax.psum_scatter(gate_total, "depth", scatter_dimension=1, tiled=True),
        lax.psum_scatter(up_total, "depth", scatter_dimension=1, tiled=True),
    )
    return (hidden[None], grad_gate, grad_up)


def solution(mesh):
    in_specs = (
        P("depth", None, ("col", "row")),
        P("col", "row"),
        P("col", "row"),
        P("depth", "col", "row"),
    )
    out_specs = (P("depth", "col", "row"), P("col", ("row", "depth")), P("col", ("row", "depth")))
    sizes = tuple(mesh.shape[name] for name in ("row", "col", "depth"))
    return jax.shard_map(
        local if sizes == (2, 8, 2) else local_any,
        mesh=mesh,
        in_specs=in_specs,
        out_specs=out_specs,
        check_vma=False,
    )
```

```python
import functools
import math

import jax
import jax.numpy as jnp
from jax import lax
from jax.experimental import pallas as pl
from jax.experimental.pallas import tpu as pltpu
from jax.sharding import PartitionSpec as P

WIRE = jnp.float16
LARGEST_TOKEN, LARGEST_WEIGHT = 6.0, 0.0625
VMEM_LIMIT = 20 * 2**20
FORWARD_VMEM_LIMIT = 48 * 2**20
NO_COST = pl.CostEstimate(flops=0, bytes_accessed=0, transcendentals=0)
LONG = pl.CostEstimate(flops=6 * 10**9, bytes_accessed=0, transcendentals=0)
SHARES = (5, 2)


def forward_kernel(scale, start, cores, place_ref, *refs):
    tokens, weights = refs[:cores], refs[cores : cores + 2 * cores]
    out_ref, held, arrived = refs[3 * cores :]
    tiles, _, tile = held.shape[1:]
    tile //= 2
    blocks, _, rows, _ = out_ref.shape

    def copy(j, which):
        first = start + j * tile
        if which < 2:
            columns = pl.ds(pl.multiple_of(place_ref[0] * tile + first, tile), tile)
            source = weights[which].at[:, columns]
        else:
            source = weights[which].at[which - 2, :, pl.ds(j * tile, tile)]
        place = pl.ds(which % 2 * tile, tile)
        held_here = held.at[which // 2, j, :, place]
        return pltpu.make_async_copy(source, held_here, arrived.at[which, j])

    for j in range(tiles):
        for which in range(2 * cores):
            copy(j, which).start()
    for j in range(tiles):
        for which in range(2 * cores):
            copy(j, which).wait()
        product = scale * sum(
            jnp.dot(tokens[i][...], held[i, j], preferred_element_type=jnp.float32)
            for i in range(cores)
        )
        for which in range(2):
            half = product[:, which * tile : (which + 1) * tile].reshape(blocks, rows, tile)
            out_ref[:, which, :, j * tile : (j + 1) * tile] = half


def forward(place, tokens, weights, start, width, tile, blocks, scale, cost=NO_COST):
    total, depth = tokens[0].shape
    cores = len(tokens)
    shape = (blocks, 2, total // blocks, width)
    return pl.pallas_call(
        functools.partial(forward_kernel, scale, start, cores),
        out_shape=jax.ShapeDtypeStruct(shape, jnp.float32),
        in_specs=[pl.BlockSpec(memory_space=pltpu.SMEM)]
        + [pl.BlockSpec(memory_space=pltpu.VMEM)] * cores
        + [pl.BlockSpec(memory_space=pl.ANY)] * (2 * cores),
        out_specs=pl.BlockSpec(memory_space=pltpu.VMEM),
        scratch_shapes=[
            pltpu.VMEM((cores, width // tile, depth, 2 * tile), jnp.bfloat16),
            pltpu.SemaphoreType.DMA((2 * cores, width // tile)),
        ],
        compiler_params=pltpu.CompilerParams(vmem_limit_bytes=FORWARD_VMEM_LIMIT),
        cost_estimate=cost,
    )(place, *tokens, *weights)


def gradient_kernel(batches, place_ref, features_ref, *refs):
    acts, outs = refs[:batches], refs[-2:]
    halves = []
    for which in range(2):
        parts = []
        for act_ref in acts:
            blocks, _, _, rows, width = act_ref.shape
            rows = rows * batches // 2
            for i in range(2 // batches):
                part = act_ref[:, 0, which, i * rows : (i + 1) * rows]
                parts.append(part.reshape(blocks * rows, width))
        halves.append(jnp.concatenate(parts))
    both = jnp.dot(
        features_ref[...], jnp.concatenate(halves, axis=1), preferred_element_type=jnp.float32
    )
    for which, out_ref in enumerate(outs):
        out_ref[...] = both[:, which * width : (which + 1) * width]


def gradient(place, features, acts, totals, columns, start, tile):
    depth, total = features.shape
    blocks, cores, _, rows, width = acts[0].shape
    act_spec = pl.BlockSpec((blocks, 1, 2, rows, tile), lambda i, j, place: (0, i, 0, 0, j))
    out_spec = pl.BlockSpec((depth, tile), lambda i, j, place: (0, place[i] + start // tile + j))
    out_shape = jax.ShapeDtypeStruct((depth, columns), jnp.float32)
    in_specs = [pl.BlockSpec((depth, total), lambda i, j, place: (0, 0))]
    in_specs += [act_spec] * len(acts)
    in_specs += [pl.BlockSpec(memory_space=pl.ANY)] * len(totals)
    return pl.pallas_call(
        functools.partial(gradient_kernel, len(acts)),
        out_shape=(out_shape, out_shape),
        grid_spec=pltpu.PrefetchScalarGridSpec(
            num_scalar_prefetch=1,
            grid=(cores, width // tile),
            in_specs=in_specs,
            out_specs=(out_spec, out_spec),
        ),
        input_output_aliases={2 + len(acts) + i: i for i in range(len(totals))},
        compiler_params=pltpu.CompilerParams(vmem_limit_bytes=VMEM_LIMIT),
        cost_estimate=pl.CostEstimate(
            flops=4 * cores * total * depth * width,
            bytes_accessed=cores * (8 * depth + 4 * total) * width + 2 * total * depth,
            transcendentals=0,
        ),
    )(place, features, *acts, *totals)


def gather_kernel(at_end_ref, act, side_1, centre_1, out_2, share_2, out_3, out_ref):
    def fill(*blocks):
        for block, block_ref in enumerate(blocks):
            out_ref[block] = block_ref[...]

    pl.when(at_end_ref[0] == 1)(functools.partial(fill, act, side_1, out_2, out_3))
    pl.when(at_end_ref[0] == 0)(functools.partial(fill, side_1, act, centre_1, share_2))


def gather_blocks(at_end, *hops):
    _, rows, width = hops[0].shape
    spec = pl.BlockSpec((1, rows, width), lambda i, at_end: (i, 0, 0))
    return pl.pallas_call(
        gather_kernel,
        out_shape=jax.ShapeDtypeStruct((4, 2, rows, width), hops[0].dtype),
        grid_spec=pltpu.PrefetchScalarGridSpec(
            num_scalar_prefetch=1,
            grid=(2,),
            in_specs=[spec] * len(hops),
            out_specs=pl.BlockSpec((4, 1, rows, width), lambda i, at_end: (0, i, 0, 0)),
        ),
        compiler_params=pltpu.CompilerParams(vmem_limit_bytes=VMEM_LIMIT),
        cost_estimate=NO_COST,
    )(at_end, *hops)


def tie(value, *after):
    return lax.optimization_barrier((value, after))[0]


def cut(units, shares):
    edges = [round(units * sum(shares[:i]) / sum(shares)) for i in range(len(shares) + 1)]
    return [(a, b - a) for a, b in zip(edges, edges[1:]) if b > a]


def local(tokens, gate_weight, up_weight, grad_hidden):
    line = 4
    row, col, part = (lax.axis_index(name) for name in ("row", "col", "depth"))
    place, core = col // 2, col % 2
    slab = grad_hidden.shape[1]
    rows = 2 * slab
    depth, columns = gate_weight.shape
    half = columns // 2
    share = half // 2
    tile = 256 if share % 256 == 0 else 128
    largest = depth * 2 * line * LARGEST_TOKEN * LARGEST_WEIGHT
    scale = 2.0 ** math.floor(math.log2(65504 / largest))

    swap = [(0, 1), (1, 0)]
    pairs = [(i, i ^ 1) for i in range(2 * line)]

    def between(hops):
        return [(2 * i + c, 2 * j + c) for i, j in hops for c in (0, 1)]

    inward, outward = between([(0, 1), (3, 2)]), between([(1, 0), (2, 3)])
    side, centre = inward + outward, between([(1, 2), (2, 1)])
    at_end = (place == 0) | (place == line - 1)
    at_far = 2 * place >= line

    def send(value, route):
        return lax.ppermute(value, "col", route)

    def wide(value):
        return value.astype(jnp.float32)

    def add(*terms):
        return functools.reduce(jnp.add, map(wide, terms))

    def by(first, mine, theirs, axis):
        return jnp.where(
            first,
            jnp.concatenate([mine, theirs], axis=axis),
            jnp.concatenate([theirs, mine], axis=axis),
        )

    def columns_of(array, start, width):
        return lax.dynamic_slice_in_dim(array, start, width, array.ndim - 1)

    pieces = []
    for begin, count in cut(share // tile, SHARES):
        for batches in ((0, 1),) if pieces else ((0,), (1,)):
            pieces.append((batches, begin * tile, count * tile))
    last = len(pieces) - 1

    def exchange_weights(k, after):
        _, start, width = pieces[k]
        first = part * half + (1 - core) * share + start
        chosen = [
            columns_of(weight, first, width) for weight in tie((gate_weight, up_weight), after)
        ]
        return send(jnp.stack(chosen), pairs)

    mine = tokens[0]
    over_row = lax.ppermute(mine, "row", swap)
    over_depth = lax.ppermute(mine, "depth", swap)
    over_both = lax.ppermute(over_row, "depth", swap)
    own_tile, other_tile = [
        ((part * half + owner * share) // tile).astype(jnp.int32).reshape(1)
        for owner in (core, 1 - core)
    ]

    def arrange(values):
        values = values.reshape(line, rows, depth)
        return jnp.where(at_far, values[::-1], values)

    def own_features(tokens, k, after, wire):
        _, start, width = pieces[k]
        tokens = tie(tokens, after).reshape(-1, depth)
        common = ((gate_weight, up_weight), start, width, tile, line, scale)
        payload = forward(other_tile, [tokens], *common).astype(wire)

        def own(after, cost=NO_COST):
            return forward(own_tile, [tie(tokens, payload, after)], *common, cost)

        return payload, own

    def all_features(tokens, k, after):
        _, start, width = pieces[k]
        tokens = [value.reshape(-1, depth) for value in tie(tokens, after)]
        weights = (gate_weight, up_weight, far_weights, far_weights)
        return forward(own_tile, tokens, weights, start, width, tile, line, scale), None

    def take(terms, block):
        own, theirs = terms
        return own[block] if theirs is None else own[block] + wide(theirs[block])

    over_row = tie(over_row, over_depth)
    features = [arrange(by(row == 0, mine, over_row, 1))]
    theirs, own = own_features(features[0], 0, (), WIRE)
    terms = (own((), LONG), send(theirs, pairs))
    payload = take(terms, 3).astype(WIRE)
    in_1 = send(payload, inward)

    over_depth, over_both = tie((over_depth, over_both), payload)
    features.append(arrange(by(row == 0, over_depth, over_both, 1)))
    theirs, own = own_features(features[1], 1, (), WIRE)
    terms = tie(terms, theirs)

    def activate(k, summed):
        batches, start, width = pieces[k]
        summed = (summed * (1.0 / scale)).reshape(2, len(batches), rows, width)
        gate_sum, up_sum = summed[0], summed[1]
        squash = jax.nn.sigmoid(gate_sum)
        product = (gate_sum * squash * up_sum).astype(jnp.bfloat16)
        for position, batch in enumerate(batches):
            hidden[batch].append(product[position])
        given = jnp.stack([wide(cotangent[b][:, start : start + width]) for b in batches])
        gate_act = given * up_sum * squash * (1.0 + gate_sum * (1.0 - squash))
        up_act = given * gate_sum * squash
        act = jnp.stack([gate_act, up_act]).astype(jnp.bfloat16)
        return act.reshape(2, len(batches) * rows, width)

    def merge(*hops):
        blocks = gather_blocks(at_end.astype(jnp.int32).reshape(1), *hops)
        return blocks, send(blocks, pairs)

    def add_gradients(acts, owner, totals, start):
        where = (owner * (share // tile)).astype(jnp.int32).reshape(1)
        acts = [value[:, None] for value in acts]
        return gradient(where, turned, acts, totals, half, start, tile)

    hidden, totals, merged, products = ([], []), (), [], {}
    act = hops = None
    for k in range(-1, last + 1):
        adding, gathering = k < last, act is not None
        if gathering:
            side_1, centre_1 = send(act, side), send(act, centre)
        if adding:
            if hops is not None:
                merged.append(merge(*hops))
                terms = tie(terms, merged[-1][0])
            if k == 0:
                terms = tie(terms, far_weights, tokens[1])
            near = take(tie(terms, in_1) if gathering else terms, 2).astype(WIRE)
            far = add(take(tie(terms, near), 3), in_1).astype(WIRE)
            centre_2, in_2 = send(far, centre), send(near, inward)
            before = (in_1,)
        else:
            hidden = jnp.stack([jnp.concatenate(parts, axis=1) for parts in hidden])
            hidden = hidden.reshape(2, 2, slab, share)
            mine = lax.dynamic_index_in_dim(hidden, core, 1, keepdims=False)
            theirs = lax.dynamic_index_in_dim(hidden, 1 - core, 1, keepdims=False)
            theirs = send(theirs, pairs)
            merged.append(merge(*tie(hops, theirs)))
            before = (theirs, merged[-1][0])
        if gathering:
            side_1, centre_1 = tie((side_1, centre_1), before)
            out_2, share_2 = send(centre_1, outward), send(side_1, centre)
        if k == 0:
            products[2] = all_features(tokens, 2, (side_1, centre_1, far, near))
            terms = tie(terms, products[2])
        if k < 0:
            products[1] = (own((far, near), LONG), send(theirs, pairs))
            cotangent = tie(grad_hidden[0], far, near)
            cotangent = (
                columns_of(cotangent, part * half, half),
                lax.ppermute(columns_of(cotangent, (1 - part) * half, half), "depth", swap),
            )
            terms = tie(terms, products[1], cotangent[1])
        if not adding:
            own_acts, other_acts = zip(*merged)
            totals = add_gradients(own_acts, core, (), pieces[0][1])
            share_2 = tie(share_2, totals)
            hidden = by(core == 0, *tie((mine, theirs), side_1, centre_1), 2)
            theirs = lax.ppermute(hidden[1], "depth", swap)
            hidden = by(part == 0, hidden[0], theirs, 1)
            other_acts = tie(other_acts, theirs)
        if adding:
            if gathering:
                terms = tie(terms, side_1, centre_1)
            near = add(take(terms, 2), in_2).astype(WIRE)
            swapped = jnp.where(at_end, take(terms, 1), add(take(terms, 0), centre_2))
            swapped = swapped.astype(WIRE)
            centre_3, side_3 = send(near, centre), send(swapped, side)
            if k + 2 <= last:
                payload = take(tie(products[k + 2], near, swapped), 3).astype(WIRE)
                in_1 = send(payload, inward)
            before = (in_2, centre_2)
        if k < 0:
            cotangent = jnp.stack(tie(cotangent, near, swapped))
            cotangent = by(
                core == 0,
                columns_of(cotangent, core * share, share),
                send(columns_of(cotangent, (1 - core) * share, share), pairs),
                1,
            )
            far_weights = exchange_weights(2, (near, swapped))
            tokens = jnp.stack(tie(features, near, swapped), axis=1)
            tokens = (tokens, send(tokens, pairs))
        if k == last - 1:
            turned = [value.reshape(-1, depth) for value in tie(features, near, swapped)]
            turned = jnp.concatenate(turned).T
            terms = tie(terms, turned)
        if gathering:
            out_2, share_2 = tie((out_2, share_2), before)
            out_3 = send(share_2, outward)
        if adding:
            if gathering:
                terms = tie(terms, out_2, share_2)
            own_sum = jnp.where(at_end, take(terms, 0), take(terms, 1))
            ready = activate(k + 1, add(own_sum, side_3, centre_3))
            if gathering:
                hops = tie((act, side_1, centre_1, out_2, share_2, out_3), ready)
            act, terms = ready, products.get(k + 2)
        else:
            totals = add_gradients(other_acts, 1 - core, totals, pieces[0][1])
            out_3, hidden = lax.optimization_barrier((tie(out_3, totals), hidden))
            own_acts, other_acts = merge(act, side_1, centre_1, out_2, share_2, out_3)
    totals = add_gradients([own_acts], core, totals, pieces[last][1])
    totals = add_gradients([other_acts], 1 - core, totals, pieces[last][1])

    return (hidden[None], *totals)


def contract(picked, piece):
    return lax.dot_general(
        picked, piece, (((0,), (0,)), ((), ())), preferred_element_type=jnp.float32
    )


def local_any(tokens, gate_weight, up_weight, grad_hidden):
    features = lax.all_gather(tokens[0], "row", axis=1, tiled=True)
    columns = gate_weight.shape[1]
    picked = features
    gate_part = jnp.dot(picked, gate_weight, preferred_element_type=jnp.float32)
    up_part = jnp.dot(picked, up_weight, preferred_element_type=jnp.float32)
    summed = lax.psum_scatter(
        jnp.concatenate([gate_part, up_part], axis=1), "col", scatter_dimension=0, tiled=True
    )
    gate_sum = summed[:, :columns]
    up_sum = summed[:, columns:]
    squash = jax.nn.sigmoid(gate_sum)
    hidden = (gate_sum * squash * up_sum).astype(jnp.bfloat16)
    cotangent = grad_hidden[0].astype(jnp.float32)
    gate_act = (cotangent * up_sum * squash * (1.0 + gate_sum * (1.0 - squash))).astype(
        jnp.bfloat16
    )
    up_act = (cotangent * gate_sum * squash).astype(jnp.bfloat16)
    picked = features
    gate_total = contract(picked, lax.all_gather(gate_act, "col", axis=0, tiled=True))
    up_total = contract(picked, lax.all_gather(up_act, "col", axis=0, tiled=True))
    grad_gate, grad_up = (
        lax.psum_scatter(gate_total, "depth", scatter_dimension=1, tiled=True),
        lax.psum_scatter(up_total, "depth", scatter_dimension=1, tiled=True),
    )
    return (hidden[None], grad_gate, grad_up)


def solution(mesh):
    in_specs = (
        P("depth", None, ("col", "row")),
        P("col", "row"),
        P("col", "row"),
        P("depth", "col", "row"),
    )
    out_specs = (P("depth", "col", "row"), P("col", ("row", "depth")), P("col", ("row", "depth")))
    sizes = tuple(mesh.shape[name] for name in ("row", "col", "depth"))
    return jax.shard_map(
        local if sizes == (2, 8, 2) else local_any,
        mesh=mesh,
        in_specs=in_specs,
        out_specs=out_specs,
        check_vma=False,
    )
```

```python
import functools
import math

import jax
import jax.numpy as jnp
from jax import lax
from jax.experimental import pallas as pl
from jax.experimental.pallas import tpu as pltpu
from jax.sharding import PartitionSpec as P

WIRE = jnp.float16
LARGEST_TOKEN, LARGEST_WEIGHT = 6.0, 0.0625
VMEM_LIMIT = 20 * 2**20
FORWARD_VMEM_LIMIT = 48 * 2**20
NO_COST = pl.CostEstimate(flops=0, bytes_accessed=0, transcendentals=0)
LONG = pl.CostEstimate(flops=6 * 10**9, bytes_accessed=0, transcendentals=0)
SHARES = (5, 2)


def forward_kernel(scale, start, cores, place_ref, *refs):
    tokens, weights = refs[:cores], refs[cores : cores + 2 * cores]
    out_ref, held, arrived = refs[3 * cores :]
    tiles, _, tile = held.shape[1:]
    tile //= 2
    blocks, _, rows, _ = out_ref.shape

    def copy(j, which):
        first = start + j * tile
        if which < 2:
            columns = pl.ds(pl.multiple_of(place_ref[0] * tile + first, tile), tile)
            source = weights[which].at[:, columns]
        else:
            source = weights[which].at[which - 2, :, pl.ds(j * tile, tile)]
        place = pl.ds(which % 2 * tile, tile)
        held_here = held.at[which // 2, j, :, place]
        return pltpu.make_async_copy(source, held_here, arrived.at[which, j])

    for j in range(tiles):
        for which in range(2 * cores):
            copy(j, which).start()
    for j in range(tiles):
        for which in range(2 * cores):
            copy(j, which).wait()
        product = scale * sum(
            jnp.dot(tokens[i][...], held[i, j], preferred_element_type=jnp.float32)
            for i in range(cores)
        )
        for which in range(2):
            half = product[:, which * tile : (which + 1) * tile].reshape(blocks, rows, tile)
            out_ref[:, which, :, j * tile : (j + 1) * tile] = half


def forward(place, tokens, weights, start, width, tile, blocks, scale, cost=NO_COST):
    total, depth = tokens[0].shape
    cores = len(tokens)
    shape = (blocks, 2, total // blocks, width)
    return pl.pallas_call(
        functools.partial(forward_kernel, scale, start, cores),
        out_shape=jax.ShapeDtypeStruct(shape, jnp.float32),
        in_specs=[pl.BlockSpec(memory_space=pltpu.SMEM)]
        + [pl.BlockSpec(memory_space=pltpu.VMEM)] * cores
        + [pl.BlockSpec(memory_space=pl.ANY)] * (2 * cores),
        out_specs=pl.BlockSpec(memory_space=pltpu.VMEM),
        scratch_shapes=[
            pltpu.VMEM((cores, width // tile, depth, 2 * tile), jnp.bfloat16),
            pltpu.SemaphoreType.DMA((2 * cores, width // tile)),
        ],
        compiler_params=pltpu.CompilerParams(vmem_limit_bytes=FORWARD_VMEM_LIMIT),
        cost_estimate=cost,
    )(place, *tokens, *weights)


def gradient_kernel(batches, place_ref, features_ref, *refs):
    acts, outs = refs[:batches], refs[-2:]
    halves = []
    for which in range(2):
        parts = []
        for act_ref in acts:
            blocks, _, _, rows, width = act_ref.shape
            rows = rows * batches // 2
            for i in range(2 // batches):
                part = act_ref[:, 0, which, i * rows : (i + 1) * rows]
                parts.append(part.reshape(blocks * rows, width))
        halves.append(jnp.concatenate(parts))
    both = jnp.dot(
        features_ref[...], jnp.concatenate(halves, axis=1), preferred_element_type=jnp.float32
    )
    for which, out_ref in enumerate(outs):
        out_ref[...] = both[:, which * width : (which + 1) * width]


def gradient(place, features, acts, totals, columns, start, tile):
    depth, total = features.shape
    blocks, cores, _, rows, width = acts[0].shape
    act_spec = pl.BlockSpec((blocks, 1, 2, rows, tile), lambda i, j, place: (0, i, 0, 0, j))
    out_spec = pl.BlockSpec((depth, tile), lambda i, j, place: (0, place[i] + start // tile + j))
    out_shape = jax.ShapeDtypeStruct((depth, columns), jnp.float32)
    in_specs = [pl.BlockSpec((depth, total), lambda i, j, place: (0, 0))]
    in_specs += [act_spec] * len(acts)
    in_specs += [pl.BlockSpec(memory_space=pl.ANY)] * len(totals)
    return pl.pallas_call(
        functools.partial(gradient_kernel, len(acts)),
        out_shape=(out_shape, out_shape),
        grid_spec=pltpu.PrefetchScalarGridSpec(
            num_scalar_prefetch=1,
            grid=(cores, width // tile),
            in_specs=in_specs,
            out_specs=(out_spec, out_spec),
        ),
        input_output_aliases={2 + len(acts) + i: i for i in range(len(totals))},
        compiler_params=pltpu.CompilerParams(vmem_limit_bytes=VMEM_LIMIT),
        cost_estimate=pl.CostEstimate(
            flops=4 * cores * total * depth * width,
            bytes_accessed=cores * (8 * depth + 4 * total) * width + 2 * total * depth,
            transcendentals=0,
        ),
    )(place, features, *acts, *totals)


def gather_kernel(at_end_ref, act, side_1, centre_1, out_2, share_2, out_3, out_ref):
    def fill(*blocks):
        for block, block_ref in enumerate(blocks):
            out_ref[block] = block_ref[...]

    pl.when(at_end_ref[0] == 1)(functools.partial(fill, act, side_1, out_2, out_3))
    pl.when(at_end_ref[0] == 0)(functools.partial(fill, side_1, act, centre_1, share_2))


def gather_blocks(at_end, *hops):
    _, rows, width = hops[0].shape
    spec = pl.BlockSpec((1, rows, width), lambda i, at_end: (i, 0, 0))
    return pl.pallas_call(
        gather_kernel,
        out_shape=jax.ShapeDtypeStruct((4, 2, rows, width), hops[0].dtype),
        grid_spec=pltpu.PrefetchScalarGridSpec(
            num_scalar_prefetch=1,
            grid=(2,),
            in_specs=[spec] * len(hops),
            out_specs=pl.BlockSpec((4, 1, rows, width), lambda i, at_end: (0, i, 0, 0)),
        ),
        compiler_params=pltpu.CompilerParams(vmem_limit_bytes=VMEM_LIMIT),
        cost_estimate=NO_COST,
    )(at_end, *hops)


def tie(value, *after):
    return lax.optimization_barrier((value, after))[0]


def cut(units, shares):
    edges = [round(units * sum(shares[:i]) / sum(shares)) for i in range(len(shares) + 1)]
    return [(a, b - a) for a, b in zip(edges, edges[1:]) if b > a]


def local(tokens, gate_weight, up_weight, grad_hidden):
    line = 4
    row, col, part = (lax.axis_index(name) for name in ("row", "col", "depth"))
    place, core = col // 2, col % 2
    slab = grad_hidden.shape[1]
    rows = 2 * slab
    depth, columns = gate_weight.shape
    half = columns // 2
    share = half // 2
    tile = 256 if share % 256 == 0 else 128
    largest = depth * 2 * line * LARGEST_TOKEN * LARGEST_WEIGHT
    scale = 2.0 ** math.floor(math.log2(65504 / largest))

    swap = [(0, 1), (1, 0)]
    pairs = [(i, i ^ 1) for i in range(2 * line)]

    def between(hops):
        return [(2 * i + c, 2 * j + c) for i, j in hops for c in (0, 1)]

    inward, outward = between([(0, 1), (3, 2)]), between([(1, 0), (2, 3)])
    side, centre = inward + outward, between([(1, 2), (2, 1)])
    at_end = (place == 0) | (place == line - 1)
    at_far = 2 * place >= line

    def send(value, route):
        return lax.ppermute(value, "col", route)

    def wide(value):
        return value.astype(jnp.float32)

    def add(*terms):
        return functools.reduce(jnp.add, map(wide, terms))

    def by(first, mine, theirs, axis):
        return jnp.where(
            first,
            jnp.concatenate([mine, theirs], axis=axis),
            jnp.concatenate([theirs, mine], axis=axis),
        )

    def columns_of(array, start, width):
        return lax.dynamic_slice_in_dim(array, start, width, array.ndim - 1)

    pieces = []
    for begin, count in cut(share // tile, SHARES):
        for batches in ((0, 1),) if pieces else ((0,), (1,)):
            pieces.append((batches, begin * tile, count * tile))
    last = len(pieces) - 1

    def exchange_weights(k, after):
        _, start, width = pieces[k]
        first = part * half + (1 - core) * share + start
        chosen = [
            columns_of(weight, first, width) for weight in tie((gate_weight, up_weight), after)
        ]
        return send(jnp.stack(chosen), pairs)

    mine = tokens[0]
    over_row = lax.ppermute(mine, "row", swap)
    over_depth = lax.ppermute(mine, "depth", swap)
    over_both = lax.ppermute(over_row, "depth", swap)
    own_tile, other_tile = [
        ((part * half + owner * share) // tile).astype(jnp.int32).reshape(1)
        for owner in (core, 1 - core)
    ]

    def arrange(values):
        values = values.reshape(line, rows, depth)
        return jnp.where(at_far, values[::-1], values)

    def own_features(tokens, k, after, wire):
        _, start, width = pieces[k]
        tokens = tie(tokens, after).reshape(-1, depth)
        common = ((gate_weight, up_weight), start, width, tile, line, scale)
        payload = forward(other_tile, [tokens], *common).astype(wire)

        def own(after, cost=NO_COST):
            return forward(own_tile, [tie(tokens, payload, after)], *common, cost)

        return payload, own

    def all_features(tokens, k, after):
        _, start, width = pieces[k]
        tokens = [value.reshape(-1, depth) for value in tie(tokens, after)]
        weights = (gate_weight, up_weight, far_weights, far_weights)
        return forward(own_tile, tokens, weights, start, width, tile, line, scale), None

    def take(terms, block):
        own, theirs = terms
        return own[block] if theirs is None else own[block] + wide(theirs[block])

    over_row = tie(over_row, over_depth)
    features = [arrange(by(row == 0, mine, over_row, 1))]
    theirs, own = own_features(features[0], 0, (), WIRE)
    terms = (own((), LONG), send(theirs, pairs))
    payload = take(terms, 3).astype(WIRE)
    in_1 = send(payload, inward)

    over_depth, over_both = tie((over_depth, over_both), payload)
    features.append(arrange(by(row == 0, over_depth, over_both, 1)))
    theirs, own = own_features(features[1], 1, (), WIRE)
    terms = tie(terms, theirs)

    def activate(k, summed):
        batches, start, width = pieces[k]
        summed = (summed * (1.0 / scale)).reshape(2, len(batches), rows, width)
        gate_sum, up_sum = summed[0], summed[1]
        squash = jax.nn.sigmoid(gate_sum)
        product = (gate_sum * squash * up_sum).astype(jnp.bfloat16)
        for position, batch in enumerate(batches):
            hidden[batch].append(product[position])
        given = jnp.stack([wide(cotangent[b][:, start : start + width]) for b in batches])
        gate_act = given * up_sum * squash * (1.0 + gate_sum * (1.0 - squash))
        up_act = given * gate_sum * squash
        act = jnp.stack([gate_act, up_act]).astype(jnp.bfloat16)
        return act.reshape(2, len(batches) * rows, width)

    def merge(*hops):
        blocks = gather_blocks(at_end.astype(jnp.int32).reshape(1), *hops)
        return blocks, send(blocks, pairs)

    def add_gradients(acts, owner, totals, start):
        where = (owner * (share // tile)).astype(jnp.int32).reshape(1)
        acts = [value[:, None] for value in acts]
        return gradient(where, turned, acts, totals, half, start, tile)

    hidden, totals, merged, products = ([], []), (), [], {}
    act = hops = None
    for k in range(-1, last + 1):
        adding, gathering = k < last, act is not None
        if gathering:
            side_1, centre_1 = send(act, side), send(act, centre)
        if adding:
            if hops is not None:
                merged.append(merge(*hops))
                terms = tie(terms, merged[-1][0])
            if k == 0:
                terms = tie(terms, far_weights, tokens[1])
            near = take(tie(terms, in_1) if gathering else terms, 2).astype(WIRE)
            far = add(take(tie(terms, near), 3), in_1).astype(WIRE)
            centre_2, in_2 = send(far, centre), send(near, inward)
            before = (in_1,)
        else:
            hidden = jnp.stack([jnp.concatenate(parts, axis=1) for parts in hidden])
            hidden = hidden.reshape(2, 2, slab, share)
            mine = lax.dynamic_index_in_dim(hidden, core, 1, keepdims=False)
            theirs = lax.dynamic_index_in_dim(hidden, 1 - core, 1, keepdims=False)
            theirs = send(theirs, pairs)
            merged.append(merge(*tie(hops, theirs)))
            before = (theirs, merged[-1][0])
        if gathering:
            side_1, centre_1 = tie((side_1, centre_1), before)
            out_2, share_2 = send(centre_1, outward), send(side_1, centre)
        if k < 0:
            products[1] = (own((far, near), LONG), send(theirs, pairs))
            cotangent = tie(grad_hidden[0], far, near)
            cotangent = (
                columns_of(cotangent, part * half, half),
                lax.ppermute(columns_of(cotangent, (1 - part) * half, half), "depth", swap),
            )
            terms = tie(terms, products[1], cotangent[1])
        if not adding:
            own_acts, other_acts = zip(*merged)
            totals = add_gradients(own_acts, core, (), pieces[0][1])
            share_2 = tie(share_2, totals)
            hidden = by(core == 0, *tie((mine, theirs), side_1, centre_1), 2)
            theirs = lax.ppermute(hidden[1], "depth", swap)
            hidden = by(part == 0, hidden[0], theirs, 1)
            other_acts = tie(other_acts, theirs)
        if adding:
            if gathering:
                terms = tie(terms, side_1, centre_1)
            near = add(take(terms, 2), in_2).astype(WIRE)
            swapped = jnp.where(at_end, take(terms, 1), add(take(terms, 0), centre_2))
            swapped = swapped.astype(WIRE)
            centre_3, side_3 = send(near, centre), send(swapped, side)
            if k == 0:
                products[2] = all_features(tokens, 2, (near, swapped))
            if k + 2 <= last:
                payload = take(tie(products[k + 2], near, swapped), 3).astype(WIRE)
                in_1 = send(payload, inward)
            before = (in_2, centre_2)
        if k < 0:
            cotangent = jnp.stack(tie(cotangent, near, swapped))
            cotangent = by(
                core == 0,
                columns_of(cotangent, core * share, share),
                send(columns_of(cotangent, (1 - core) * share, share), pairs),
                1,
            )
            far_weights = exchange_weights(2, (near, swapped))
            tokens = jnp.stack(tie(features, near, swapped), axis=1)
            tokens = (tokens, send(tokens, pairs))
        if k == last - 1:
            turned = [value.reshape(-1, depth) for value in tie(features, near, swapped)]
            turned = jnp.concatenate(turned).T
            terms = tie(terms, turned)
        if gathering:
            out_2, share_2 = tie((out_2, share_2), before)
            out_3 = send(share_2, outward)
        if adding:
            if gathering:
                terms = tie(terms, out_2, share_2)
            own_sum = jnp.where(at_end, take(terms, 0), take(terms, 1))
            ready = activate(k + 1, add(own_sum, side_3, centre_3))
            if gathering:
                hops = tie((act, side_1, centre_1, out_2, share_2, out_3), ready)
            act, terms = ready, products.get(k + 2)
        else:
            totals = add_gradients(other_acts, 1 - core, totals, pieces[0][1])
            out_3, hidden = lax.optimization_barrier((tie(out_3, totals), hidden))
            own_acts, other_acts = merge(act, side_1, centre_1, out_2, share_2, out_3)
    totals = add_gradients([own_acts], core, totals, pieces[last][1])
    totals = add_gradients([other_acts], 1 - core, totals, pieces[last][1])

    return (hidden[None], *totals)


def contract(picked, piece):
    return lax.dot_general(
        picked, piece, (((0,), (0,)), ((), ())), preferred_element_type=jnp.float32
    )


def local_any(tokens, gate_weight, up_weight, grad_hidden):
    features = lax.all_gather(tokens[0], "row", axis=1, tiled=True)
    columns = gate_weight.shape[1]
    picked = features
    gate_part = jnp.dot(picked, gate_weight, preferred_element_type=jnp.float32)
    up_part = jnp.dot(picked, up_weight, preferred_element_type=jnp.float32)
    summed = lax.psum_scatter(
        jnp.concatenate([gate_part, up_part], axis=1), "col", scatter_dimension=0, tiled=True
    )
    gate_sum = summed[:, :columns]
    up_sum = summed[:, columns:]
    squash = jax.nn.sigmoid(gate_sum)
    hidden = (gate_sum * squash * up_sum).astype(jnp.bfloat16)
    cotangent = grad_hidden[0].astype(jnp.float32)
    gate_act = (cotangent * up_sum * squash * (1.0 + gate_sum * (1.0 - squash))).astype(
        jnp.bfloat16
    )
    up_act = (cotangent * gate_sum * squash).astype(jnp.bfloat16)
    picked = features
    gate_total = contract(picked, lax.all_gather(gate_act, "col", axis=0, tiled=True))
    up_total = contract(picked, lax.all_gather(up_act, "col", axis=0, tiled=True))
    grad_gate, grad_up = (
        lax.psum_scatter(gate_total, "depth", scatter_dimension=1, tiled=True),
        lax.psum_scatter(up_total, "depth", scatter_dimension=1, tiled=True),
    )
    return (hidden[None], grad_gate, grad_up)


def solution(mesh):
    in_specs = (
        P("depth", None, ("col", "row")),
        P("col", "row"),
        P("col", "row"),
        P("depth", "col", "row"),
    )
    out_specs = (P("depth", "col", "row"), P("col", ("row", "depth")), P("col", ("row", "depth")))
    sizes = tuple(mesh.shape[name] for name in ("row", "col", "depth"))
    return jax.shard_map(
        local if sizes == (2, 8, 2) else local_any,
        mesh=mesh,
        in_specs=in_specs,
        out_specs=out_specs,
        check_vma=False,
    )
```
